32 devices in a mesh: clip: 8 (over z, x), frame: 4 (over y, core).
Axes of the slice: x: 2, y: 2, z: 4, core: 2. Of those that a mesh axis runs over, the one named last changes fastest.
Arguments:
- frames_in: bfloat16 [8, 8, 96, 1280], P('clip', 'frame'), may hold values from -6 to 6
- ref_feats: bfloat16 [8, 96, 1280], P('clip', 'frame'), may hold values from -6 to 6
- out_grad: bfloat16 [8, 8, 96, 1280], P('clip', 'frame'), may hold values from -6 to 6
- space_query: bfloat16 [1280, 640], P('frame'), may hold values from -0.15625 to 0.15625
- space_key: bfloat16 [1280, 640], P('frame'), may hold values from -0.15625 to 0.15625
- space_value: bfloat16 [1280, 640], P('frame'), may hold values from -0.15625 to 0.15625
- space_output: bfloat16 [640, 1280], P('frame'), may hold values from -0.25 to 0.25
- time_query: bfloat16 [1280, 640], P('frame'), may hold values from -0.15625 to 0.15625
- time_key: bfloat16 [1280, 640], P('frame'), may hold values from -0.15625 to 0.15625
- time_value: bfloat16 [1280, 640], P('frame'), may hold values from -0.15625 to 0.15625
- time_output: bfloat16 [640, 1280], P('frame'), may hold values from -0.25 to 0.25
Outputs:
- out: bfloat16 [8, 8, 96, 1280], P('clip', 'frame')
- frames_grad: bfloat16 [8, 8, 96, 1280], P('clip', 'frame')
- ref_grad: bfloat16 [8, 96, 1280], P('clip', 'frame')
- space_query_grad: float32 [1280, 640], P('frame')
- space_key_grad: float32 [1280, 640], P('frame')
- space_value_grad: float32 [1280, 640], P('frame')
- space_output_grad: float32 [640, 1280], P('frame')
- time_query_grad: float32 [1280, 640], P('frame')
- time_key_grad: float32 [1280, 640], P('frame')
- time_value_grad: float32 [1280, 640], P('frame')
- time_output_grad: float32 [640, 1280], P('frame')
The draws below stay inside these ranges and needn't reach their ends.
All inputs are finite; a program needn't handle non-finite values.
Results may differ from the reference program's by a relative error of at most 0.035.
Values may be sent and summed in bfloat16 or wider, within the bound.
No kernel may reach another device: no remote copies, remote signals or barrier semaphores. Data moves between devices by JAX's collectives and lax.ppermute only.
A program may use at most 128 MiB of HBM per device.

```python
import math
import jax
import jax.numpy as jnp
from jax import lax

D = 1280
HEADS = 4
S = 96
FR_DEV = 2
INNER = 640
FRAMES = 8
CLIPS = 8
BLOCKS = 4
REF_DEV = 24


def level_of(rng, dims, shards, least, largest):
    level = 1.0
    for position, blocks in shards:
        steps = jax.random.uniform(jax.random.fold_in(jax.random.fold_in(rng, 6), position), (blocks,), jnp.float32, least / len(shards), largest / len(shards))
        level = level * jnp.repeat(jnp.exp(steps), dims[position] // blocks).reshape((-1,) + (1,) * (len(dims) - 1 - position))
    return level


def normal_values(key, shape, deviation, reach, shards=(), held_as=jnp.bfloat16):
    loudness = level_of(key, shape, shards, -0.22, 0.18) if shards else 1.0
    values = jax.random.normal(key, shape, jnp.float32) * deviation * loudness
    return jnp.minimum(jnp.maximum(values, -reach), reach).astype(held_as)


def setup_inputs(seed: int = 0) -> dict:
    arg_keys = jax.random.split(jax.random.key(seed), 12)
    return {
        "frames_in": normal_values(arg_keys[0], (CLIPS, FRAMES, S, D), 1.0, 6.0, ((0, 8), (1, 4))),
        "ref_feats": normal_values(arg_keys[1], (CLIPS, S, D), 1.0, 6.0, ((0, 8), (1, 4))),
        "out_grad": normal_values(arg_keys[2], (CLIPS, FRAMES, S, D), 1.0, 6.0, ((0, 8), (1, 4))),
        "space_query": normal_values(arg_keys[3], (D, INNER), D ** -0.5, 0.15625, ((0, 4),)),
        "space_key": normal_values(arg_keys[4], (D, INNER), D ** -0.5, 0.15625, ((0, 4),)),
        "space_value": normal_values(arg_keys[5], (D, INNER), D ** -0.5, 0.15625, ((0, 4),)),
        "space_output": normal_values(arg_keys[6], (INNER, D), INNER ** -0.5, 0.25, ((0, 4),)),
        "time_query": normal_values(arg_keys[7], (D, INNER), D ** -0.5, 0.15625, ((0, 4),)),
        "time_key": normal_values(arg_keys[8], (D, INNER), D ** -0.5, 0.15625, ((0, 4),)),
        "time_value": normal_values(arg_keys[9], (D, INNER), D ** -0.5, 0.15625, ((0, 4),)),
        "time_output": normal_values(arg_keys[10], (INNER, D), INNER ** -0.5, 0.25, ((0, 4),)),
    }


EPSILON = 1e-05

def layer_stats(rows):
    wide = rows.astype(jnp.float32)
    centre = lax.optimization_barrier(jnp.mean(wide, -1, keepdims=True))
    offset = wide - centre
    inverse = lax.rsqrt(lax.optimization_barrier(jnp.mean(offset * offset, -1, keepdims=True)) + EPSILON)
    return (offset * inverse, inverse)

def layer_back(centred, inverse, cotangent):
    first = lax.optimization_barrier(jnp.mean(cotangent, -1, keepdims=True))
    second = lax.optimization_barrier(jnp.mean(cotangent * centred, -1, keepdims=True))
    return inverse * (cotangent - first - centred * second)

def position_table(first, count, width):
    frame_ids = (first + jnp.arange(count, dtype=jnp.int32)).astype(jnp.float32)
    halves = jnp.arange(width // 2, dtype=jnp.int32).astype(jnp.float32)
    rates = jnp.exp(halves * (-2.0 * math.log(10000.0) / width))
    angles = frame_ids[:, None] * rates[None, :]
    return jnp.stack([jnp.sin(angles), jnp.cos(angles)], -1).reshape(count, width)

def einsum_forms(temporal):
    if temporal:
        return ('qbhe,kbhe->bhqk', 'bhqk,kbhe->qbhe', 'bhqk,qbhe->kbhe')
    return ('bqhe,bkhe->bhqk', 'bhqk,bkhe->bqhe', 'bhqk,bqhe->bkhe')

def product(form, left, right):
    return jnp.einsum(form, left.astype(jnp.float32), right.astype(jnp.float32))

def attention(query, keys, values, temporal):
    score_form, mix_form, back_form = einsum_forms(temporal)
    scores = product(score_form, query, keys) * query.shape[-1] ** (-0.5)
    powers = jnp.exp(scores)
    probs = powers / lax.optimization_barrier(jnp.sum(powers, -1, keepdims=True))
    rounded = probs.astype(jnp.bfloat16)
    mixed = product(mix_form, rounded, values).astype(jnp.bfloat16)
    return (mixed, probs, rounded)

def attention_back(query, keys, values, probs, rounded, cotangent, temporal):
    score_form, mix_form, back_form = einsum_forms(temporal)
    prob_grad = product(score_form, cotangent, values)
    score_grad = probs * (prob_grad - lax.optimization_barrier(jnp.sum(probs * prob_grad, -1, keepdims=True)))
    score_rounded = (score_grad * query.shape[-1] ** (-0.5)).astype(jnp.bfloat16)
    query_grad = product(mix_form, score_rounded, keys).astype(jnp.bfloat16)
    key_grad = product(back_form, score_rounded, query)
    value_grad = product(back_form, rounded, cotangent)
    return (query_grad, key_grad, value_grad)

def split_heads(rows):
    return rows.reshape(rows.shape[:-1] + (HEADS, rows.shape[-1] // HEADS))

def merge_heads(rows):
    return rows.reshape(rows.shape[:-2] + (rows.shape[-2] * rows.shape[-1],))

def project(rows, weight):
    flat_rows = rows.reshape(-1, rows.shape[-1])
    result = jnp.dot(flat_rows, weight, preferred_element_type=jnp.float32)
    return result.reshape(rows.shape[:-1] + (weight.shape[1],))

def project_back(rows, weight):
    flat_rows = rows.reshape(-1, rows.shape[-1])
    result = lax.dot_general(flat_rows, weight, (((1,), (1,)), ((), ())), preferred_element_type=jnp.float32)
    return result.reshape(rows.shape[:-1] + (weight.shape[0],))

def outer_sum(left, right):
    left_rows = left.reshape(-1, left.shape[-1])
    right_rows = right.reshape(-1, right.shape[-1])
    return lax.dot_general(left_rows, right_rows, (((0,), (0,)), ((), ())), preferred_element_type=jnp.float32)

def reference(frames_in, ref_feats, out_grad, space_query, space_key, space_value, space_output, time_query, time_key, time_value, time_output):
    table = position_table(0, FRAMES, D)

    def one_clip(carry, data):
        frames, refer, cotangent = data
        centred_one, inverse_one = layer_stats(frames)
        normed_one = centred_one.astype(jnp.bfloat16)
        spatial_query = project(normed_one, space_query).astype(jnp.bfloat16)
        spatial_key = project(normed_one, space_key).astype(jnp.bfloat16)
        spatial_value = project(normed_one, space_value).astype(jnp.bfloat16)
        refer_key = project(refer, space_key).astype(jnp.bfloat16)
        refer_value = project(refer, space_value).astype(jnp.bfloat16)
        keys_joined = jnp.concatenate([spatial_key, jnp.broadcast_to(refer_key[None], spatial_key.shape)], 1)
        values_joined = jnp.concatenate([spatial_value, jnp.broadcast_to(refer_value[None], spatial_value.shape)], 1)
        spatial_mixed, spatial_probs, spatial_rounded = attention(split_heads(spatial_query), split_heads(keys_joined), split_heads(values_joined), False)
        spatial_mixed = merge_heads(spatial_mixed)
        hidden_one = (frames.astype(jnp.float32) + project(spatial_mixed, space_output)).astype(jnp.bfloat16)
        centred_two, inverse_two = layer_stats(hidden_one)
        normed_two = (centred_two + table[:, None, :]).astype(jnp.bfloat16)
        temporal_query = project(normed_two, time_query).astype(jnp.bfloat16)
        temporal_key = project(normed_two, time_key).astype(jnp.bfloat16)
        temporal_value = project(normed_two, time_value).astype(jnp.bfloat16)
        temporal_mixed, temporal_probs, temporal_rounded = attention(split_heads(temporal_query), split_heads(temporal_key), split_heads(temporal_value), True)
        temporal_mixed = merge_heads(temporal_mixed)
        output = (hidden_one.astype(jnp.float32) + project(temporal_mixed, time_output)).astype(jnp.bfloat16)
        mixed_grad_two = project_back(cotangent, time_output).astype(jnp.bfloat16)
        query_grad_two, key_grad_two, value_grad_two = attention_back(split_heads(temporal_query), split_heads(temporal_key), split_heads(temporal_value), temporal_probs, temporal_rounded, split_heads(mixed_grad_two), True)
        query_grad_two = merge_heads(query_grad_two)
        key_grad_two = merge_heads(key_grad_two).astype(jnp.bfloat16)
        value_grad_two = merge_heads(value_grad_two).astype(jnp.bfloat16)
        normed_grad_two = project_back(query_grad_two, time_query) + project_back(key_grad_two, time_key) + project_back(value_grad_two, time_value)
        hidden_grad = (cotangent.astype(jnp.float32) + layer_back(centred_two, inverse_two, normed_grad_two)).astype(jnp.bfloat16)
        mixed_grad_one = project_back(hidden_grad, space_output).astype(jnp.bfloat16)
        query_grad_one, key_joined_grad, value_joined_grad = attention_back(split_heads(spatial_query), split_heads(keys_joined), split_heads(values_joined), spatial_probs, spatial_rounded, split_heads(mixed_grad_one), False)
        query_grad_one = merge_heads(query_grad_one)
        key_grad_one = merge_heads(key_joined_grad[:, :S]).astype(jnp.bfloat16)
        value_grad_one = merge_heads(value_joined_grad[:, :S]).astype(jnp.bfloat16)
        refer_key_grad = merge_heads(lax.optimization_barrier(jnp.sum(key_joined_grad[:, S:], 0))).astype(jnp.bfloat16)
        refer_value_grad = merge_heads(lax.optimization_barrier(jnp.sum(value_joined_grad[:, S:], 0))).astype(jnp.bfloat16)
        normed_grad_one = project_back(query_grad_one, space_query) + project_back(key_grad_one, space_key) + project_back(value_grad_one, space_value)
        frames_grad = (hidden_grad.astype(jnp.float32) + layer_back(centred_one, inverse_one, normed_grad_one)).astype(jnp.bfloat16)
        refer_grad = (project_back(refer_key_grad, space_key) + project_back(refer_value_grad, space_value)).astype(jnp.bfloat16)

        def add_block(block, sums):
            start = (block * FR_DEV).astype(jnp.int32)
            ref_start = (block * REF_DEV).astype(jnp.int32)

            def rows(array):
                return lax.dynamic_slice_in_dim(array, start, FR_DEV, 0)

            def ref_rows(array):
                return lax.dynamic_slice_in_dim(array, ref_start, REF_DEV, 0)
            normed_block = rows(normed_one)
            second_block = rows(normed_two)
            terms = (outer_sum(normed_block, rows(query_grad_one)), outer_sum(normed_block, rows(key_grad_one)) + outer_sum(ref_rows(refer), ref_rows(refer_key_grad)), outer_sum(normed_block, rows(value_grad_one)) + outer_sum(ref_rows(refer), ref_rows(refer_value_grad)), outer_sum(rows(spatial_mixed), rows(hidden_grad)), outer_sum(second_block, rows(query_grad_two)), outer_sum(second_block, rows(key_grad_two)), outer_sum(second_block, rows(value_grad_two)), outer_sum(rows(temporal_mixed), rows(cotangent)))
            return tuple((total + lax.optimization_barrier(term.astype(jnp.bfloat16)).astype(jnp.float32) for total, term in zip(sums, terms)))
        carry = lax.fori_loop(0, BLOCKS, add_block, carry)
        return (carry, (output, frames_grad, refer_grad))
    wide = jnp.zeros((D, INNER), jnp.float32)
    tall = jnp.zeros((INNER, D), jnp.float32)
    start_sums = (wide, wide, wide, tall, wide, wide, wide, tall)
    grads, (output, frames_grad, refer_grad) = lax.scan(one_clip, start_sums, (frames_in, ref_feats, out_grad))
    return (output, frames_grad, refer_grad, grads[0], grads[1], grads[2], grads[3], grads[4], grads[5], grads[6], grads[7])
```

```python
import math

import functools

import jax
import jax.numpy as jnp
from jax import lax
from jax.experimental import pallas as pl
from jax.experimental.pallas import tpu as pltpu
from jax.sharding import PartitionSpec as P

HEADS = 4


EPSILON = 1e-05


def layer_stats(rows):
    wide = rows.astype(jnp.float32)
    centre = jnp.mean(wide, -1, keepdims=True)
    offset = wide - centre
    inverse = lax.rsqrt(jnp.mean(offset * offset, -1, keepdims=True) + EPSILON)
    return (offset * inverse, inverse)


def layer_back(centred, inverse, cotangent):
    first = jnp.mean(cotangent, -1, keepdims=True)
    second = jnp.mean(cotangent * centred, -1, keepdims=True)
    return inverse * (cotangent - first - centred * second)


def position_table(first, count, width):
    frame_ids = (first + jnp.arange(count, dtype=jnp.int32)).astype(jnp.float32)
    halves = jnp.arange(width // 2, dtype=jnp.int32).astype(jnp.float32)
    rates = jnp.exp(halves * (-2.0 * math.log(10000.0) / width))
    angles = frame_ids[:, None] * rates[None, :]
    return jnp.stack([jnp.sin(angles), jnp.cos(angles)], -1).reshape(count, width)


def einsum_forms(temporal):
    if temporal:
        return ("qbhe,kbhe->bhqk", "bhqk,kbhe->qbhe", "bhqk,qbhe->kbhe")
    return ("bqhe,bkhe->bhqk", "bhqk,bkhe->bqhe", "bhqk,bqhe->bkhe")


def product(form, left, right):
    return jnp.einsum(form, left, right, preferred_element_type=jnp.float32)


def attention(query, keys, values, temporal):
    score_form, mix_form, back_form = einsum_forms(temporal)
    scores = product(score_form, query, keys) * query.shape[-1] ** (-0.5)
    powers = jnp.exp(scores)
    probs = powers / jnp.sum(powers, -1, keepdims=True)
    rounded = probs.astype(jnp.bfloat16)
    mixed = product(mix_form, rounded, values).astype(jnp.bfloat16)
    return (mixed, probs, rounded)


def attention_back(query, keys, values, probs, rounded, cotangent, temporal):
    score_form, mix_form, back_form = einsum_forms(temporal)
    prob_grad = product(score_form, cotangent, values)
    score_grad = probs * (prob_grad - jnp.sum(probs * prob_grad, -1, keepdims=True))
    score_rounded = (score_grad * query.shape[-1] ** (-0.5)).astype(jnp.bfloat16)
    query_grad = product(mix_form, score_rounded, keys).astype(jnp.bfloat16)
    key_grad = product(back_form, score_rounded, query)
    value_grad = product(back_form, rounded, cotangent)
    return (query_grad, key_grad, value_grad)


def split_heads(rows):
    return rows.reshape(rows.shape[:-1] + (HEADS, rows.shape[-1] // HEADS))


def merge_heads(rows):
    return rows.reshape(rows.shape[:-2] + (rows.shape[-2] * rows.shape[-1],))


def project(rows, weight):
    flat_rows = rows.reshape(-1, rows.shape[-1])
    result = jnp.dot(flat_rows, weight, preferred_element_type=jnp.float32)
    return result.reshape(rows.shape[:-1] + (weight.shape[1],))


def project_back(rows, weight):
    flat_rows = rows.reshape(-1, rows.shape[-1])
    result = lax.dot_general(
        flat_rows, weight, (((1,), (1,)), ((), ())), preferred_element_type=jnp.float32
    )
    return result.reshape(rows.shape[:-1] + (weight.shape[0],))


def outer_sum(left, right):
    left_rows = left.reshape(-1, left.shape[-1])
    right_rows = right.reshape(-1, right.shape[-1])
    return lax.dot_general(
        left_rows, right_rows, (((0,), (0,)), ((), ())), preferred_element_type=jnp.float32
    )


def per_device_general(
    frames_in,
    ref_feats,
    out_grad,
    space_query,
    space_key,
    space_value,
    space_output,
    time_query,
    time_key,
    time_value,
    time_output,
):
    block = lax.axis_index("frame")
    (
        full_space_query,
        full_space_key,
        full_space_value,
        full_space_output,
        full_time_query,
        full_time_key,
        full_time_value,
        full_time_output,
    ) = (
        lax.all_gather(space_query, "frame", axis=0, tiled=True),
        lax.all_gather(space_key, "frame", axis=0, tiled=True),
        lax.all_gather(space_value, "frame", axis=0, tiled=True),
        lax.all_gather(space_output, "frame", axis=0, tiled=True),
        lax.all_gather(time_query, "frame", axis=0, tiled=True),
        lax.all_gather(time_key, "frame", axis=0, tiled=True),
        lax.all_gather(time_value, "frame", axis=0, tiled=True),
        lax.all_gather(time_output, "frame", axis=0, tiled=True),
    )
    frames = frames_in[0]
    refer = ref_feats[0]
    cotangent = out_grad[0]
    frame_count = frames.shape[0]
    token_count = frames.shape[1]
    centred_one, inverse_one = layer_stats(frames)
    normed_one = centred_one.astype(jnp.bfloat16)
    spatial_query = project(normed_one, full_space_query).astype(jnp.bfloat16)
    spatial_key = project(normed_one, full_space_key).astype(jnp.bfloat16)
    spatial_value = project(normed_one, full_space_value).astype(jnp.bfloat16)
    own_key = project(refer, full_space_key).astype(jnp.bfloat16)
    own_value = project(refer, full_space_value).astype(jnp.bfloat16)
    refer_key, refer_value = (
        lax.all_gather(own_key, "frame", axis=0, tiled=True),
        lax.all_gather(own_value, "frame", axis=0, tiled=True),
    )
    keys_joined = jnp.concatenate(
        [spatial_key, jnp.broadcast_to(refer_key[None], spatial_key.shape)], 1
    )
    values_joined = jnp.concatenate(
        [spatial_value, jnp.broadcast_to(refer_value[None], spatial_value.shape)], 1
    )
    spatial_mixed, spatial_probs, spatial_rounded = attention(
        split_heads(spatial_query), split_heads(keys_joined), split_heads(values_joined), False
    )
    spatial_mixed = merge_heads(spatial_mixed)
    hidden_one = (frames.astype(jnp.float32) + project(spatial_mixed, full_space_output)).astype(
        jnp.bfloat16
    )
    centred_two, inverse_two = layer_stats(hidden_one)
    table = position_table(block * frame_count, frame_count, frames.shape[2])
    normed_two = (centred_two + table[:, None, :]).astype(jnp.bfloat16)
    normed_rows = lax.all_to_all(normed_two, "frame", split_axis=1, concat_axis=0, tiled=True)
    temporal_query = project(normed_rows, full_time_query).astype(jnp.bfloat16)
    temporal_key = project(normed_rows, full_time_key).astype(jnp.bfloat16)
    temporal_value = project(normed_rows, full_time_value).astype(jnp.bfloat16)
    temporal_mixed, temporal_probs, temporal_rounded = attention(
        split_heads(temporal_query), split_heads(temporal_key), split_heads(temporal_value), True
    )
    mixed_two = lax.all_to_all(
        merge_heads(temporal_mixed), "frame", split_axis=0, concat_axis=1, tiled=True
    )
    output = (hidden_one.astype(jnp.float32) + project(mixed_two, full_time_output)).astype(
        jnp.bfloat16
    )
    mixed_grad_two = project_back(cotangent, full_time_output).astype(jnp.bfloat16)
    token_grad = lax.all_to_all(mixed_grad_two, "frame", split_axis=1, concat_axis=0, tiled=True)
    token_query_grad, token_key_grad, token_value_grad = attention_back(
        split_heads(temporal_query),
        split_heads(temporal_key),
        split_heads(temporal_value),
        temporal_probs,
        temporal_rounded,
        split_heads(token_grad),
        True,
    )
    query_grad_two, key_grad_two, value_grad_two = (
        lax.all_to_all(
            merge_heads(token_query_grad), "frame", split_axis=0, concat_axis=1, tiled=True
        ),
        lax.all_to_all(
            merge_heads(token_key_grad).astype(jnp.bfloat16),
            "frame",
            split_axis=0,
            concat_axis=1,
            tiled=True,
        ),
        lax.all_to_all(
            merge_heads(token_value_grad).astype(jnp.bfloat16),
            "frame",
            split_axis=0,
            concat_axis=1,
            tiled=True,
        ),
    )
    normed_grad_two = (
        project_back(query_grad_two, full_time_query)
        + project_back(key_grad_two, full_time_key)
        + project_back(value_grad_two, full_time_value)
    )
    hidden_grad = (
        cotangent.astype(jnp.float32) + layer_back(centred_two, inverse_two, normed_grad_two)
    ).astype(jnp.bfloat16)
    mixed_grad_one = project_back(hidden_grad, full_space_output).astype(jnp.bfloat16)
    query_grad_one, key_joined_grad, value_joined_grad = attention_back(
        split_heads(spatial_query),
        split_heads(keys_joined),
        split_heads(values_joined),
        spatial_probs,
        spatial_rounded,
        split_heads(mixed_grad_one),
        False,
    )
    query_grad_one = merge_heads(query_grad_one)
    key_grad_one = merge_heads(key_joined_grad[:, :token_count]).astype(jnp.bfloat16)
    value_grad_one = merge_heads(value_joined_grad[:, :token_count]).astype(jnp.bfloat16)
    partial_key = merge_heads(jnp.sum(key_joined_grad[:, token_count:], 0))
    partial_value = merge_heads(jnp.sum(value_joined_grad[:, token_count:], 0))
    summed_key, summed_value = (
        lax.psum_scatter(
            partial_key.astype(jnp.bfloat16), "frame", scatter_dimension=0, tiled=True
        ).astype(jnp.float32),
        lax.psum_scatter(
            partial_value.astype(jnp.bfloat16), "frame", scatter_dimension=0, tiled=True
        ).astype(jnp.float32),
    )
    refer_key_grad = summed_key.astype(jnp.bfloat16)
    refer_value_grad = summed_value.astype(jnp.bfloat16)
    normed_grad_one = (
        project_back(query_grad_one, full_space_query)
        + project_back(key_grad_one, full_space_key)
        + project_back(value_grad_one, full_space_value)
    )
    frames_grad = (
        hidden_grad.astype(jnp.float32) + layer_back(centred_one, inverse_one, normed_grad_one)
    ).astype(jnp.bfloat16)
    refer_grad = (
        project_back(refer_key_grad, full_space_key)
        + project_back(refer_value_grad, full_space_value)
    ).astype(jnp.bfloat16)
    term_sq = outer_sum(normed_one, query_grad_one)
    term_sk = outer_sum(normed_one, key_grad_one) + outer_sum(refer, refer_key_grad)
    term_sv = outer_sum(normed_one, value_grad_one) + outer_sum(refer, refer_value_grad)
    term_so = outer_sum(spatial_mixed, hidden_grad)
    term_tq = outer_sum(normed_two, query_grad_two)
    term_tk = outer_sum(normed_two, key_grad_two)
    term_tv = outer_sum(normed_two, value_grad_two)
    term_to = outer_sum(mixed_two, cotangent)
    share_sq, share_sk, share_sv, share_so, share_tq, share_tk, share_tv, share_to = (
        lax.psum_scatter(
            term_sq.astype(jnp.bfloat16), "frame", scatter_dimension=0, tiled=True
        ).astype(jnp.float32),
        lax.psum_scatter(
            term_sk.astype(jnp.bfloat16), "frame", scatter_dimension=0, tiled=True
        ).astype(jnp.float32),
        lax.psum_scatter(
            term_sv.astype(jnp.bfloat16), "frame", scatter_dimension=0, tiled=True
        ).astype(jnp.float32),
        lax.psum_scatter(
            term_so.astype(jnp.bfloat16), "frame", scatter_dimension=0, tiled=True
        ).astype(jnp.float32),
        lax.psum_scatter(
            term_tq.astype(jnp.bfloat16), "frame", scatter_dimension=0, tiled=True
        ).astype(jnp.float32),
        lax.psum_scatter(
            term_tk.astype(jnp.bfloat16), "frame", scatter_dimension=0, tiled=True
        ).astype(jnp.float32),
        lax.psum_scatter(
            term_tv.astype(jnp.bfloat16), "frame", scatter_dimension=0, tiled=True
        ).astype(jnp.float32),
        lax.psum_scatter(
            term_to.astype(jnp.bfloat16), "frame", scatter_dimension=0, tiled=True
        ).astype(jnp.float32),
    )
    total_sq, total_sk, total_sv, total_so, total_tq, total_tk, total_tv, total_to = (
        lax.psum(share_sq.astype(jnp.bfloat16), "clip").astype(jnp.float32),
        lax.psum(share_sk.astype(jnp.bfloat16), "clip").astype(jnp.float32),
        lax.psum(share_sv.astype(jnp.bfloat16), "clip").astype(jnp.float32),
        lax.psum(share_so.astype(jnp.bfloat16), "clip").astype(jnp.float32),
        lax.psum(share_tq.astype(jnp.bfloat16), "clip").astype(jnp.float32),
        lax.psum(share_tk.astype(jnp.bfloat16), "clip").astype(jnp.float32),
        lax.psum(share_tv.astype(jnp.bfloat16), "clip").astype(jnp.float32),
        lax.psum(share_to.astype(jnp.bfloat16), "clip").astype(jnp.float32),
    )
    return (
        output[None],
        frames_grad[None],
        refer_grad[None],
        total_sq,
        total_sk,
        total_sv,
        total_so,
        total_tq,
        total_tk,
        total_tv,
        total_to,
    )


F32 = jnp.float32
BF16 = jnp.bfloat16
CHUNK = 32


def mm(left, right):
    return jnp.dot(left, right, preferred_element_type=F32)


def mm_bt(left, right):
    return lax.dot_general(left, right, (((1,), (1,)), ((), ())), preferred_element_type=F32)


def mm_at(left, right):
    return lax.dot_general(left, right, (((0,), (0,)), ((), ())), preferred_element_type=F32)


def wide_call(body, name, out_shape, scratch, limit_mb, flops, num_in):
    return pl.pallas_call(
        body,
        name=name,
        out_shape=out_shape,
        in_specs=[pl.BlockSpec(memory_space=pltpu.SMEM)]
        + [pl.BlockSpec(memory_space=pltpu.VMEM)] * (num_in - 1),
        out_specs=tuple(pl.BlockSpec(memory_space=pltpu.VMEM) for _ in out_shape),
        scratch_shapes=scratch,
        compiler_params=pltpu.CompilerParams(vmem_limit_bytes=limit_mb * 1024 * 1024),
        cost_estimate=pl.CostEstimate(flops=flops, bytes_accessed=8_000_000, transcendentals=0),
    )


def struct(*shape, dtype=BF16):
    return jax.ShapeDtypeStruct(shape, dtype)


def flip(value, axis, bit):
    size = lax.axis_size(axis)
    return lax.ppermute(value, axis, [(i, i ^ bit) for i in range(size)])


def after(value, *others):
    return lax.optimization_barrier((value,) + others)[0]


def pack_body(heads, idx, wq, wk, wv, *outs):
    width = wq.shape[1] // heads
    room = outs[0].shape[1]
    for h in range(heads):
        parts = [w[:, h * width : (h + 1) * width] for w in (wq, wk, wv)]
        parts.append(jnp.zeros((wq.shape[0], room - 3 * width), BF16))
        outs[h][...] = jnp.concatenate(parts, 1)


def spatial_forward_body(n, tokens, width, idx, *refs):
    frames, weights, refer = refs[:n], refs[n : 2 * n], refs[2 * n]
    x_out, w_out, q_out, k_out, v_out, p_out, o_out = refs[2 * n + 1 : 2 * n + 8]
    mixed, turn = refs[2 * n + 8 :]
    me = idx[0]
    rows = frames[0].shape[0]
    depth = weights[0].shape[0]
    lanes = q_out.shape[1]
    room = w_out.shape[1]
    total = n * rows
    for r in range(n):
        w_out[pl.ds(pl.multiple_of((me ^ r) * depth, depth), depth), :] = weights[r][...]
    for r in range(n):

        def norm(i, _, r=r):
            at = pl.multiple_of(i * CHUNK, CHUNK)
            centred, _ = layer_stats(frames[r][pl.ds(at, CHUNK), :])
            x_out[pl.ds(r * rows + at, CHUNK), :] = centred.astype(BF16)
            return 0

        lax.fori_loop(0, rows // CHUNK, norm, 0)
    x_out[total:, :] = refer[...]
    for start, count in [(r * rows, rows) for r in range(n)] + [(total, refer.shape[0])]:
        three = mm(x_out[start : start + count, :], w_out[...])
        keep = lax.broadcasted_iota(jnp.int32, (count, lanes), 1) < width
        q_out[start : start + count, :] = jnp.where(keep, three[:, :lanes], 0.0).astype(BF16)
        k_out[start : start + count, :] = jnp.where(
            keep, pltpu.roll(three, room - width, 1)[:, :lanes], 0.0
        ).astype(BF16)
        v_out[start : start + count, :] = jnp.where(
            keep, pltpu.roll(three, room - 2 * width, 1)[:, :lanes], 0.0
        ).astype(BF16)
    scale = width**-0.5
    for b in range(total // tokens):
        at = slice(b * tokens, (b + 1) * tokens)
        keys = jnp.concatenate([k_out[at, :], k_out[total:, :]], 0)
        values = jnp.concatenate([v_out[at, :], v_out[total:, :]], 0)
        powers = jnp.exp(mm_bt(q_out[at, :], keys) * scale)
        probs = powers / jnp.sum(powers, -1, keepdims=True)
        p_out[at, :] = probs
        mixed[at, :] = mm(probs.astype(BF16), values)
    share = tokens // n
    per = rows // tokens
    for r in range(n):
        first = pl.multiple_of((me ^ r) * share, share)
        for b in range(total // tokens):
            to = ((b // per) ^ r) * per + b % per
            turn[to * share : (to + 1) * share, :] = mixed[pl.ds(b * tokens + first, share), :]
        o_out[r] = turn[...].astype(BF16)


def spatial_backward_body(n, tokens, width, idx, *refs):
    grads = refs[:n]
    x_ref, w_ref, q_ref, k_ref, v_ref, p_ref = refs[n : n + 6]
    keep_out, send_out, keep_ref, send_ref, term_out = refs[n + 6 : n + 11]
    spread, turn, packed = refs[n + 11 :]
    me = idx[0]
    share = tokens // n
    total = p_ref.shape[0]
    rows = total // n
    lanes = q_ref.shape[1]
    room = w_ref.shape[1]
    per = rows // tokens
    for r in range(n):
        first = pl.multiple_of((me ^ r) * share, share)
        turn[...] = grads[r][...].astype(F32)
        for b in range(total // tokens):
            to = ((b // per) ^ r) * per + b % per
            spread[pl.ds(b * tokens + first, share), :] = turn[to * share : (to + 1) * share, :]
    scale = width**-0.5

    def pack(first, second, third):
        def wide(part):
            blank = jnp.zeros((part.shape[0], room - lanes), F32)
            return jnp.concatenate([part, blank], 1)

        result = pltpu.roll(wide(second), width, 1) + pltpu.roll(wide(third), 2 * width, 1)
        return result if first is None else result + wide(first)

    key_sum = jnp.zeros((k_ref.shape[0] - total, lanes), F32)
    value_sum = key_sum
    for b in range(total // tokens):
        at = slice(b * tokens, (b + 1) * tokens)
        query = q_ref[at, :]
        keys = jnp.concatenate([k_ref[at, :], k_ref[total:, :]], 0)
        values = jnp.concatenate([v_ref[at, :], v_ref[total:, :]], 0)
        cotangent = spread[at, :].astype(BF16)
        probs = p_ref[at, :]
        back = mm_bt(cotangent, values)
        score = (probs * (back - jnp.sum(probs * back, -1, keepdims=True)) * scale).astype(BF16)
        query_grad = mm(score, keys)
        key_grad = mm_at(score, query)
        value_grad = mm_at(probs.astype(BF16), cotangent)
        key_sum = key_sum + key_grad[tokens:]
        value_sum = value_sum + value_grad[tokens:]
        packed[at, :] = pack(query_grad, key_grad[:tokens], value_grad[:tokens]).astype(BF16)
    packed[total:, :] = pack(None, key_sum, value_sum).astype(BF16)
    for r in range(n):
        part = mm_bt(packed[r * rows : (r + 1) * rows, :], w_ref[...]).astype(BF16)
        (send_out if r & 1 else keep_out)[r >> 1] = part
    part = mm_bt(packed[total:, :], w_ref[...])
    for r in range(n):
        (send_ref if r & 1 else keep_ref)[r >> 1] = part[r * share : (r + 1) * share].astype(BF16)
    depth = x_ref.shape[1] // 5
    for j in range(5):
        at = slice(j * depth, (j + 1) * depth)
        term_out[at, :] = mm_at(x_ref[:, at], packed[...]).astype(BF16)


def temporal_body(n, heads, idx, *refs):
    mixed, so_parts, tq_parts, tk_parts, tv_parts, to_parts = (
        refs[i * n : (i + 1) * n] for i in range(6)
    )
    frames, cotangent, table, same = refs[6 * n : 6 * n + 4]
    grad_outs = refs[6 * n + 4 : 7 * n + 4]
    gh_out, n2_out, gq_out, gk_out, gv_out, o2_out, out_out = refs[7 * n + 4 : 7 * n + 11]
    so, tq, tk, tv, to, hidden, centred, inverse, wide, qs, gos = refs[7 * n + 11 :]
    me = idx[0]
    rows, dim = frames.shape
    inner = tq.shape[1]
    width = inner // heads
    for r in range(n):
        for parts, whole in ((tq_parts, tq), (tk_parts, tk), (tv_parts, tv), (to_parts, to)):
            depth = parts[r].shape[0]
            whole[pl.ds(pl.multiple_of((me ^ r) * depth, depth), depth), :] = parts[r][...]
        depth = so_parts[r].shape[0]
        so[r, :depth, :] = so_parts[r][...]
        so[r, depth:, :] = jnp.zeros((so.shape[1] - depth, dim), BF16)
    step = dim // 5
    for j in range(5):
        at = slice(j * step, (j + 1) * step)
        acc = frames[:, at].astype(F32)
        for r in range(n):
            acc = acc + mm(mixed[r][...], so[r, :, at])
        hidden[:, at] = acc.astype(BF16).astype(F32)

    def norm(i, _):
        at = pl.ds(pl.multiple_of(i * CHUNK, CHUNK), CHUNK)
        offset, scale = layer_stats(hidden[at, :])
        centred[at, :] = offset
        inverse[at, :] = jnp.broadcast_to(scale, (CHUNK, inverse.shape[1]))
        n2_out[at, :] = (offset + table[at, :]).astype(BF16)
        return 0

    lax.fori_loop(0, rows // CHUNK, norm, 0)
    lane_head = lax.broadcasted_iota(jnp.int32, (rows, inner), 1)

    def own(h, value):
        inside = (lane_head >= h * width) & (lane_head < (h + 1) * width)
        return jnp.where(inside, value, 0.0)

    scale = width**-0.5
    query = mm(n2_out[...], tq[...])
    for h in range(heads):
        qs[h * rows : (h + 1) * rows, :] = own(h, query).astype(BF16)
    keys = mm(n2_out[...], tk[...]).astype(BF16)
    values = mm(n2_out[...], tv[...]).astype(BF16)
    mixed_grad = mm_bt(cotangent[...], to[...])
    for h in range(heads):
        gos[h * rows : (h + 1) * rows, :] = own(h, mixed_grad).astype(BF16)
    key_grad = jnp.zeros((rows, inner), F32)
    value_grad = jnp.zeros((rows, inner), F32)
    query_grad = jnp.zeros((rows, inner), F32)
    o2 = jnp.zeros((rows, inner), F32)
    for h in range(heads):
        at = slice(h * rows, (h + 1) * rows)
        scores = mm_bt(qs[at, :], keys) * scale
        powers = jnp.where(same[...] > 0.5, jnp.exp(scores), 0.0)
        probs = powers / jnp.sum(powers, -1, keepdims=True)
        rounded = probs.astype(BF16)
        o2 = o2 + own(h, mm(rounded, values))
        back = mm_bt(gos[at, :], values)
        score = (probs * (back - jnp.sum(probs * back, -1, keepdims=True)) * scale).astype(BF16)
        query_grad = query_grad + own(h, mm(score, keys))
        key_grad = key_grad + mm_at(score, qs[at, :])
        value_grad = value_grad + mm_at(rounded, gos[at, :])
    o2_out[...] = o2.astype(BF16)
    gq_out[...] = query_grad.astype(BF16)
    gk_out[...] = key_grad.astype(BF16)
    gv_out[...] = value_grad.astype(BF16)
    for j in range(5):
        at = slice(j * step, (j + 1) * step)
        wide[:, at] = (
            mm_bt(gq_out[...], tq[at, :]) + mm_bt(gk_out[...], tk[at, :]) + mm_bt(gv_out[...], tv[at, :])
        )

    def back_norm(i, _):
        at = pl.ds(pl.multiple_of(i * CHUNK, CHUNK), CHUNK)
        back = layer_back(centred[at, :], inverse[at, :1], wide[at, :])
        gh_out[at, :] = (cotangent[at, :].astype(F32) + back).astype(BF16)
        return 0

    lax.fori_loop(0, rows // CHUNK, back_norm, 0)
    for r in range(n):
        grad_outs[r][...] = mm_bt(gh_out[...], so[r]).astype(BF16)
    for j in range(5):
        at = slice(j * step, (j + 1) * step)
        out_out[:, at] = (hidden[:, at] + mm(o2_out[...], to[:, at])).astype(BF16)


def terms_body(n, idx, *refs):
    mixed = refs[:n]
    gh, n2, gq, gk, gv, o2, cotangent = refs[n : n + 7]
    keep_a, send_a, keep_b, send_b = refs[n + 7 : n + 11]
    tall, flat = refs[n + 11 :]
    me = idx[0]
    dim, inner = tall.shape
    depth, low = dim // n, inner // n

    for i, grad in enumerate((gq, gk, gv)):
        for j in range(5):
            at = slice(j * (dim // 5), (j + 1) * (dim // 5))
            tall[at, :] = mm_at(n2[:, at], grad[...]).astype(BF16)
        for r in range(n):
            to = send_a if r & 1 else keep_a
            to[r >> 1, i * depth : (i + 1) * depth, :] = tall[
                pl.ds(pl.multiple_of((me ^ r) * depth, depth), depth), :
            ]
    for j in range(5):
        at = slice(j * (inner // 5), (j + 1) * (inner // 5))
        flat[at, :] = mm_at(o2[:, at], cotangent[...]).astype(BF16)
    for r in range(n):
        to = send_b if r & 1 else keep_b
        to[r >> 1, :low, :] = flat[pl.ds(pl.multiple_of((me ^ r) * low, low), low), :]
        to[r >> 1, low:, :] = mm_at(mixed[r][...], gh[...])[:low].astype(BF16)


def finish_body(idx, frames, hidden_grad, first, second, out):
    def step(i, _):
        at = pl.ds(pl.multiple_of(i * CHUNK, CHUNK), CHUNK)
        centred, inverse = layer_stats(frames[at, :])
        grad = first[at, :].astype(F32) + second[at, :].astype(F32)
        back = layer_back(centred, inverse, grad)
        out[at, :] = (hidden_grad[at, :].astype(F32) + back).astype(BF16)
        return 0

    lax.fori_loop(0, frames.shape[0] // CHUNK, step, 0)


def add(left, right):
    return (left.astype(F32) + right.astype(F32)).astype(BF16)


def pick(value, index, axis=0):
    return lax.dynamic_index_in_dim(value, index, axis, keepdims=False)


def clip_scatter(value, clip, bits):
    for place in reversed(range(bits)):
        axis = bits - 1 - place
        bit = (clip >> place) & 1
        moved = flip(pick(value, 1 - bit, axis), "clip", 1 << place)
        value = add(pick(value, bit, axis), moved)
        value = jnp.expand_dims(value, axis)
    return value.reshape(value.shape[bits:])


def clip_gather(value, clip, bits):
    pieces = [value]
    for place in range(bits):
        pieces = pieces + [flip(p, "clip", 1 << place) for p in pieces]
    stack = jnp.stack(pieces)
    order = jnp.arange(1 << bits) ^ clip
    return stack, order


def per_device(
    frames_in,
    ref_feats,
    out_grad,
    space_query,
    space_key,
    space_value,
    space_output,
    time_query,
    time_key,
    time_value,
    time_output,
):
    n = lax.axis_size("frame")
    clips = lax.axis_size("clip")
    bits = clips.bit_length() - 1
    me = lax.axis_index("frame")
    clip = lax.axis_index("clip")
    idx = jnp.stack([me, clip]).astype(jnp.int32)
    _, per, tokens, dim = frames_in.shape
    inner = space_query.shape[1]
    width = inner // HEADS
    lanes = -(-width // 128) * 128
    room = -(-3 * width // 128) * 128
    depth = dim // n
    rows = per * tokens
    total = n * rows
    share = tokens // n
    frames = frames_in.reshape(rows, dim)
    refer = ref_feats[0]
    cotangent = out_grad[0]

    def gather(value):
        one, two = flip(value, "frame", 1), flip(value, "frame", 2)
        return [value, one, two, flip(two, "frame", 1)]

    def relative(parts):
        return [pick(parts, me ^ r) for r in range(n)]

    def exchange(parts):
        return [parts[0]] + [flip(parts[r], "frame", r) for r in range(1, n)]

    packs = wide_call(
        functools.partial(pack_body, HEADS), "pack_heads", [struct(depth, room)] * HEADS, [], 24, 0, 4
    )(idx, space_query, space_key, space_value)
    packs = exchange(relative(jnp.stack(packs)))
    all_frames = gather(frames)
    all_refer = jnp.concatenate(gather(refer), 0)
    token_parts = cotangent.reshape(per, n, share, dim)
    token_grad = jnp.concatenate(
        [p.reshape(per * share, dim) for p in exchange([pick(token_parts, me ^ r, 1) for r in range(n)])], 0
    )
    held = after((space_output, time_query, time_key, time_value, time_output), all_frames[2], packs[2])
    so_parts, tq_parts, tk_parts, tv_parts, to_parts = [gather(w) for w in held]
    token_frames = jnp.concatenate(
        [
            lax.dynamic_slice_in_dim(f.reshape(per, tokens, dim), me * share, share, 1).reshape(
                per * share, dim
            )
            for f in all_frames
        ],
        0,
    )
    table = position_table(0, n * per, dim).reshape(n, per, dim)
    table = jnp.concatenate([pick(table, me ^ r) for r in range(n)], 0)
    table = jnp.repeat(table, share, 0)
    token_rows = n * per * share
    token_of = jnp.arange(token_rows) % share
    same = (token_of[:, None] == token_of[None, :]).astype(F32)

    x_all, w_all, q_all, k_all, v_all, probs, mixed = wide_call(
        functools.partial(spatial_forward_body, n, tokens, width),
        "spatial_forward",
        [
            struct(total + tokens, dim),
            struct(dim, room),
            struct(total + tokens, lanes),
            struct(total + tokens, lanes),
            struct(total + tokens, lanes),
            struct(total, 2 * tokens, dtype=F32),
            struct(n, token_rows, lanes),
        ],
        [pltpu.VMEM((total, lanes), F32), pltpu.VMEM((token_rows, lanes), F32)],
        40,
        2_000_000_000,
        2 * n + 2,
    )(idx, *all_frames, *packs, all_refer)
    mixed = exchange([mixed[r] for r in range(n)])

    outs = wide_call(
        functools.partial(temporal_body, n, HEADS),
        "temporal",
        [struct(token_rows, lanes)] * n
        + [struct(token_rows, dim)] * 2
        + [struct(token_rows, inner)] * 4
        + [struct(token_rows, dim)],
        [
            pltpu.VMEM((n, lanes, dim), BF16),
            pltpu.VMEM((dim, inner), BF16),
            pltpu.VMEM((dim, inner), BF16),
            pltpu.VMEM((dim, inner), BF16),
            pltpu.VMEM((inner, dim), BF16),
            pltpu.VMEM((token_rows, dim), F32),
            pltpu.VMEM((token_rows, dim), F32),
            pltpu.VMEM((token_rows, 128), F32),
            pltpu.VMEM((token_rows, dim), F32),
            pltpu.VMEM((HEADS * token_rows, inner), BF16),
            pltpu.VMEM((HEADS * token_rows, inner), BF16),
        ],
        48,
        5_000_000_000,
        6 * n + 5,
    )(idx, *mixed, *so_parts, *tq_parts, *tk_parts, *tv_parts, *to_parts, token_frames, token_grad, table, same)
    mixed_grads = exchange(list(outs[:n]))
    hidden_grad, n2, gq, gk, gv, o2, out_tokens = outs[n:]

    keep_a, send_a, keep_b, send_b = wide_call(
        functools.partial(terms_body, n),
        "temporal_terms",
        [struct(n // 2, 3 * depth, inner)] * 2 + [struct(n // 2, 2 * (inner // n), dim)] * 2,
        [pltpu.VMEM((dim, inner), BF16), pltpu.VMEM((inner, dim), BF16)],
        40,
        3_000_000_000,
        n + 8,
    )(idx, *mixed, hidden_grad, n2, gq, gk, gv, o2, token_grad)

    keep_out, send_out, keep_ref, send_ref, term = wide_call(
        functools.partial(spatial_backward_body, n, tokens, width),
        "spatial_backward",
        [struct(n // 2, rows, dim)] * 2 + [struct(n // 2, share, dim)] * 2 + [struct(dim, room)],
        [
            pltpu.VMEM((total, lanes), F32),
            pltpu.VMEM((token_rows, lanes), F32),
            pltpu.VMEM((total + tokens, room), BF16),
        ],
        40,
        4_000_000_000,
        n + 7,
    )(idx, *mixed_grads, x_all, w_all, q_all, k_all, v_all, probs)

    def to_frames(value):
        parts = exchange(list(value.reshape(n, per * share, dim)))
        stack = jnp.stack([p.reshape(per, share, dim) for p in parts], 1)
        order = jnp.arange(n) ^ me
        return jnp.take(stack, order, 1).reshape(per, tokens, dim)

    output = to_frames(out_tokens)
    hidden_frames = to_frames(hidden_grad).reshape(rows, dim)

    near = add(keep_out, flip(send_out, "frame", 1))
    far = flip(near[1], "frame", 2)
    near_ref = add(keep_ref, flip(send_ref, "frame", 1))
    refer_grad = add(near_ref[0], flip(near_ref[1], "frame", 2))
    frames_grad = wide_call(finish_body, "finish", [struct(rows, dim)], [], 24, 0, 5)(
        idx, frames, hidden_frames, near[0], far
    )[0].reshape(per, tokens, dim)

    split = (2,) * bits

    def over_frame(keep, send):
        near = add(keep, flip(send, "frame", 1))
        return add(near[0], flip(near[1], "frame", 2))

    sum_a = over_frame(keep_a, send_a)
    sum_b = over_frame(keep_b, send_b)
    sum_a = clip_scatter(sum_a.reshape(split + (-1, inner)), clip, bits)
    sum_b = clip_scatter(sum_b.reshape(split + (-1, dim)), clip, bits)
    term = term.reshape(n, clips, depth // clips, room).swapaxes(0, 1)
    sum_c = clip_scatter(term.reshape(split + (n, depth // clips, room)), clip, bits)
    heads = exchange(relative(sum_c))
    heads = jnp.take(jnp.stack(heads), jnp.arange(n) ^ me, 0)
    sum_c = jnp.stack(
        [
            heads[:, :, i * width : (i + 1) * width].swapaxes(0, 1).reshape(-1, inner)
            for i in range(3)
        ]
    )

    def whole(value):
        stack, order = clip_gather(value, clip, bits)
        return jnp.take(stack, order, 0)

    all_a = whole(sum_a).reshape(3, depth, inner).astype(F32)
    all_b = whole(sum_b).reshape(2, inner // n, dim).astype(F32)
    all_c = whole(sum_c).swapaxes(0, 1).reshape(3, depth, inner).astype(F32)
    return (
        output[None],
        frames_grad[None],
        refer_grad[None],
        all_c[0],
        all_c[1],
        all_c[2],
        all_b[1],
        all_a[0],
        all_a[1],
        all_a[2],
        all_b[0],
    )


def solution(mesh):
    in_specs = (
        P("clip", "frame", None, None),
        P("clip", "frame", None),
        P("clip", "frame", None, None),
        P("frame", None),
        P("frame", None),
        P("frame", None),
        P("frame", None),
        P("frame", None),
        P("frame", None),
        P("frame", None),
        P("frame", None),
    )
    out_specs = (
        P("clip", "frame", None, None),
        P("clip", "frame", None, None),
        P("clip", "frame", None),
        P("frame", None),
        P("frame", None),
        P("frame", None),
        P("frame", None),
        P("frame", None),
        P("frame", None),
        P("frame", None),
        P("frame", None),
    )
    clips = mesh.shape["clip"]
    by_heads = mesh.shape["frame"] == HEADS == 4 and clips & (clips - 1) == 0
    return jax.shard_map(
        per_device if by_heads else per_device_general, mesh=mesh, in_specs=in_specs, out_specs=out_specs, check_vma=False
    )
```

```python
import math

import functools

import jax
import jax.numpy as jnp
from jax import lax
from jax.experimental import pallas as pl
from jax.experimental.pallas import tpu as pltpu
from jax.sharding import PartitionSpec as P

HEADS = 4
F32 = jnp.float32
BF16 = jnp.bfloat16


EPSILON = 1e-05


def layer_stats(rows):
    wide = rows.astype(jnp.float32)
    centre = jnp.mean(wide, -1, keepdims=True)
    offset = wide - centre
    inverse = lax.rsqrt(jnp.mean(offset * offset, -1, keepdims=True) + EPSILON)
    return (offset * inverse, inverse)


def layer_back(centred, inverse, cotangent):
    first = jnp.mean(cotangent, -1, keepdims=True)
    second = jnp.mean(cotangent * centred, -1, keepdims=True)
    return inverse * (cotangent - first - centred * second)


def position_table(first, count, width):
    frame_ids = (first + jnp.arange(count, dtype=jnp.int32)).astype(jnp.float32)
    halves = jnp.arange(width // 2, dtype=jnp.int32).astype(jnp.float32)
    rates = jnp.exp(halves * (-2.0 * math.log(10000.0) / width))
    angles = frame_ids[:, None] * rates[None, :]
    return jnp.stack([jnp.sin(angles), jnp.cos(angles)], -1).reshape(count, width)


def position_rows(frame_ids, width):
    lane = jnp.arange(width, dtype=jnp.int32)
    rates = jnp.exp((lane // 2).astype(F32) * (-2.0 * math.log(10000.0) / width))
    angles = frame_ids.astype(F32)[:, None] * rates[None, :]
    return jnp.where(lane % 2 == 0, jnp.sin(angles), jnp.cos(angles))


def einsum_forms(temporal):
    if temporal:
        return ("qbhe,kbhe->bhqk", "bhqk,kbhe->qbhe", "bhqk,qbhe->kbhe")
    return ("bqhe,bkhe->bhqk", "bhqk,bkhe->bqhe", "bhqk,bqhe->bkhe")


def product(form, left, right):
    return jnp.einsum(form, left, right, preferred_element_type=jnp.float32)


def attention(query, keys, values, temporal):
    score_form, mix_form, back_form = einsum_forms(temporal)
    scores = product(score_form, query, keys) * query.shape[-1] ** (-0.5)
    powers = jnp.exp(scores)
    probs = powers / jnp.sum(powers, -1, keepdims=True)
    rounded = probs.astype(jnp.bfloat16)
    mixed = product(mix_form, rounded, values).astype(jnp.bfloat16)
    return (mixed, probs, rounded)


def attention_back(query, keys, values, probs, rounded, cotangent, temporal):
    score_form, mix_form, back_form = einsum_forms(temporal)
    prob_grad = product(score_form, cotangent, values)
    score_grad = probs * (prob_grad - jnp.sum(probs * prob_grad, -1, keepdims=True))
    score_rounded = (score_grad * query.shape[-1] ** (-0.5)).astype(jnp.bfloat16)
    query_grad = product(mix_form, score_rounded, keys).astype(jnp.bfloat16)
    key_grad = product(back_form, score_rounded, query)
    value_grad = product(back_form, rounded, cotangent)
    return (query_grad, key_grad, value_grad)


def split_heads(rows):
    return rows.reshape(rows.shape[:-1] + (HEADS, rows.shape[-1] // HEADS))


def merge_heads(rows):
    return rows.reshape(rows.shape[:-2] + (rows.shape[-2] * rows.shape[-1],))


def project(rows, weight):
    flat_rows = rows.reshape(-1, rows.shape[-1])
    result = jnp.dot(flat_rows, weight, preferred_element_type=jnp.float32)
    return result.reshape(rows.shape[:-1] + (weight.shape[1],))


def project_back(rows, weight):
    flat_rows = rows.reshape(-1, rows.shape[-1])
    result = lax.dot_general(
        flat_rows, weight, (((1,), (1,)), ((), ())), preferred_element_type=jnp.float32
    )
    return result.reshape(rows.shape[:-1] + (weight.shape[0],))


def outer_sum(left, right):
    left_rows = left.reshape(-1, left.shape[-1])
    right_rows = right.reshape(-1, right.shape[-1])
    return lax.dot_general(
        left_rows, right_rows, (((0,), (0,)), ((), ())), preferred_element_type=jnp.float32
    )


def per_device_general(
    frames_in,
    ref_feats,
    out_grad,
    space_query,
    space_key,
    space_value,
    space_output,
    time_query,
    time_key,
    time_value,
    time_output,
):
    block = lax.axis_index("frame")
    (
        full_space_query,
        full_space_key,
        full_space_value,
        full_space_output,
        full_time_query,
        full_time_key,
        full_time_value,
        full_time_output,
    ) = (
        lax.all_gather(space_query, "frame", axis=0, tiled=True),
        lax.all_gather(space_key, "frame", axis=0, tiled=True),
        lax.all_gather(space_value, "frame", axis=0, tiled=True),
        lax.all_gather(space_output, "frame", axis=0, tiled=True),
        lax.all_gather(time_query, "frame", axis=0, tiled=True),
        lax.all_gather(time_key, "frame", axis=0, tiled=True),
        lax.all_gather(time_value, "frame", axis=0, tiled=True),
        lax.all_gather(time_output, "frame", axis=0, tiled=True),
    )
    frames = frames_in[0]
    refer = ref_feats[0]
    cotangent = out_grad[0]
    frame_count = frames.shape[0]
    token_count = frames.shape[1]
    centred_one, inverse_one = layer_stats(frames)
    normed_one = centred_one.astype(jnp.bfloat16)
    spatial_query = project(normed_one, full_space_query).astype(jnp.bfloat16)
    spatial_key = project(normed_one, full_space_key).astype(jnp.bfloat16)
    spatial_value = project(normed_one, full_space_value).astype(jnp.bfloat16)
    own_key = project(refer, full_space_key).astype(jnp.bfloat16)
    own_value = project(refer, full_space_value).astype(jnp.bfloat16)
    refer_key, refer_value = (
        lax.all_gather(own_key, "frame", axis=0, tiled=True),
        lax.all_gather(own_value, "frame", axis=0, tiled=True),
    )
    keys_joined = jnp.concatenate(
        [spatial_key, jnp.broadcast_to(refer_key[None], spatial_key.shape)], 1
    )
    values_joined = jnp.concatenate(
        [spatial_value, jnp.broadcast_to(refer_value[None], spatial_value.shape)], 1
    )
    spatial_mixed, spatial_probs, spatial_rounded = attention(
        split_heads(spatial_query), split_heads(keys_joined), split_heads(values_joined), False
    )
    spatial_mixed = merge_heads(spatial_mixed)
    hidden_one = (frames.astype(jnp.float32) + project(spatial_mixed, full_space_output)).astype(
        jnp.bfloat16
    )
    centred_two, inverse_two = layer_stats(hidden_one)
    table = position_table(block * frame_count, frame_count, frames.shape[2])
    normed_two = (centred_two + table[:, None, :]).astype(jnp.bfloat16)
    normed_rows = lax.all_to_all(normed_two, "frame", split_axis=1, concat_axis=0, tiled=True)
    temporal_query = project(normed_rows, full_time_query).astype(jnp.bfloat16)
    temporal_key = project(normed_rows, full_time_key).astype(jnp.bfloat16)
    temporal_value = project(normed_rows, full_time_value).astype(jnp.bfloat16)
    temporal_mixed, temporal_probs, temporal_rounded = attention(
        split_heads(temporal_query), split_heads(temporal_key), split_heads(temporal_value), True
    )
    mixed_two = lax.all_to_all(
        merge_heads(temporal_mixed), "frame", split_axis=0, concat_axis=1, tiled=True
    )
    output = (hidden_one.astype(jnp.float32) + project(mixed_two, full_time_output)).astype(
        jnp.bfloat16
    )
    mixed_grad_two = project_back(cotangent, full_time_output).astype(jnp.bfloat16)
    token_grad = lax.all_to_all(mixed_grad_two, "frame", split_axis=1, concat_axis=0, tiled=True)
    token_query_grad, token_key_grad, token_value_grad = attention_back(
        split_heads(temporal_query),
        split_heads(temporal_key),
        split_heads(temporal_value),
        temporal_probs,
        temporal_rounded,
        split_heads(token_grad),
        True,
    )
    query_grad_two, key_grad_two, value_grad_two = (
        lax.all_to_all(
            merge_heads(token_query_grad), "frame", split_axis=0, concat_axis=1, tiled=True
        ),
        lax.all_to_all(
            merge_heads(token_key_grad).astype(jnp.bfloat16),
            "frame",
            split_axis=0,
            concat_axis=1,
            tiled=True,
        ),
        lax.all_to_all(
            merge_heads(token_value_grad).astype(jnp.bfloat16),
            "frame",
            split_axis=0,
            concat_axis=1,
            tiled=True,
        ),
    )
    normed_grad_two = (
        project_back(query_grad_two, full_time_query)
        + project_back(key_grad_two, full_time_key)
        + project_back(value_grad_two, full_time_value)
    )
    hidden_grad = (
        cotangent.astype(jnp.float32) + layer_back(centred_two, inverse_two, normed_grad_two)
    ).astype(jnp.bfloat16)
    mixed_grad_one = project_back(hidden_grad, full_space_output).astype(jnp.bfloat16)
    query_grad_one, key_joined_grad, value_joined_grad = attention_back(
        split_heads(spatial_query),
        split_heads(keys_joined),
        split_heads(values_joined),
        spatial_probs,
        spatial_rounded,
        split_heads(mixed_grad_one),
        False,
    )
    query_grad_one = merge_heads(query_grad_one)
    key_grad_one = merge_heads(key_joined_grad[:, :token_count]).astype(jnp.bfloat16)
    value_grad_one = merge_heads(value_joined_grad[:, :token_count]).astype(jnp.bfloat16)
    partial_key = merge_heads(jnp.sum(key_joined_grad[:, token_count:], 0))
    partial_value = merge_heads(jnp.sum(value_joined_grad[:, token_count:], 0))
    summed_key, summed_value = (
        lax.psum_scatter(
            partial_key.astype(jnp.bfloat16), "frame", scatter_dimension=0, tiled=True
        ).astype(jnp.float32),
        lax.psum_scatter(
            partial_value.astype(jnp.bfloat16), "frame", scatter_dimension=0, tiled=True
        ).astype(jnp.float32),
    )
    refer_key_grad = summed_key.astype(jnp.bfloat16)
    refer_value_grad = summed_value.astype(jnp.bfloat16)
    normed_grad_one = (
        project_back(query_grad_one, full_space_query)
        + project_back(key_grad_one, full_space_key)
        + project_back(value_grad_one, full_space_value)
    )
    frames_grad = (
        hidden_grad.astype(jnp.float32) + layer_back(centred_one, inverse_one, normed_grad_one)
    ).astype(jnp.bfloat16)
    refer_grad = (
        project_back(refer_key_grad, full_space_key)
        + project_back(refer_value_grad, full_space_value)
    ).astype(jnp.bfloat16)
    term_sq = outer_sum(normed_one, query_grad_one)
    term_sk = outer_sum(normed_one, key_grad_one) + outer_sum(refer, refer_key_grad)
    term_sv = outer_sum(normed_one, value_grad_one) + outer_sum(refer, refer_value_grad)
    term_so = outer_sum(spatial_mixed, hidden_grad)
    term_tq = outer_sum(normed_two, query_grad_two)
    term_tk = outer_sum(normed_two, key_grad_two)
    term_tv = outer_sum(normed_two, value_grad_two)
    term_to = outer_sum(mixed_two, cotangent)
    share_sq, share_sk, share_sv, share_so, share_tq, share_tk, share_tv, share_to = (
        lax.psum_scatter(
            term_sq.astype(jnp.bfloat16), "frame", scatter_dimension=0, tiled=True
        ).astype(jnp.float32),
        lax.psum_scatter(
            term_sk.astype(jnp.bfloat16), "frame", scatter_dimension=0, tiled=True
        ).astype(jnp.float32),
        lax.psum_scatter(
            term_sv.astype(jnp.bfloat16), "frame", scatter_dimension=0, tiled=True
        ).astype(jnp.float32),
        lax.psum_scatter(
            term_so.astype(jnp.bfloat16), "frame", scatter_dimension=0, tiled=True
        ).astype(jnp.float32),
        lax.psum_scatter(
            term_tq.astype(jnp.bfloat16), "frame", scatter_dimension=0, tiled=True
        ).astype(jnp.float32),
        lax.psum_scatter(
            term_tk.astype(jnp.bfloat16), "frame", scatter_dimension=0, tiled=True
        ).astype(jnp.float32),
        lax.psum_scatter(
            term_tv.astype(jnp.bfloat16), "frame", scatter_dimension=0, tiled=True
        ).astype(jnp.float32),
        lax.psum_scatter(
            term_to.astype(jnp.bfloat16), "frame", scatter_dimension=0, tiled=True
        ).astype(jnp.float32),
    )
    total_sq, total_sk, total_sv, total_so, total_tq, total_tk, total_tv, total_to = (
        lax.psum(share_sq.astype(jnp.bfloat16), "clip").astype(jnp.float32),
        lax.psum(share_sk.astype(jnp.bfloat16), "clip").astype(jnp.float32),
        lax.psum(share_sv.astype(jnp.bfloat16), "clip").astype(jnp.float32),
        lax.psum(share_so.astype(jnp.bfloat16), "clip").astype(jnp.float32),
        lax.psum(share_tq.astype(jnp.bfloat16), "clip").astype(jnp.float32),
        lax.psum(share_tk.astype(jnp.bfloat16), "clip").astype(jnp.float32),
        lax.psum(share_tv.astype(jnp.bfloat16), "clip").astype(jnp.float32),
        lax.psum(share_to.astype(jnp.bfloat16), "clip").astype(jnp.float32),
    )
    return (
        output[None],
        frames_grad[None],
        refer_grad[None],
        total_sq,
        total_sk,
        total_sv,
        total_so,
        total_tq,
        total_tk,
        total_tv,
        total_to,
    )


CHUNK = 32


def mm(left, right):
    return jnp.dot(left, right, preferred_element_type=F32)


def mm_bt(left, right):
    return lax.dot_general(left, right, (((1,), (1,)), ((), ())), preferred_element_type=F32)


def mm_at(left, right):
    return lax.dot_general(left, right, (((0,), (0,)), ((), ())), preferred_element_type=F32)


def wide_call(body, name, out_shape, scratch, limit_mb, flops, num_in, kept=0, out_kept=()):
    return pl.pallas_call(
        body,
        name=name,
        out_shape=out_shape,
        in_specs=[pl.BlockSpec(memory_space=pltpu.SMEM)]
        + [pl.BlockSpec(memory_space=pltpu.HBM)] * kept
        + [pl.BlockSpec(memory_space=pltpu.VMEM)] * (num_in - 1 - kept),
        out_specs=tuple(
            pl.BlockSpec(memory_space=pltpu.HBM if i in out_kept else pltpu.VMEM)
            for i in range(len(out_shape))
        ),
        scratch_shapes=scratch,
        compiler_params=pltpu.CompilerParams(vmem_limit_bytes=limit_mb * 1024 * 1024),
        cost_estimate=pl.CostEstimate(flops=flops, bytes_accessed=8_000_000, transcendentals=0),
    )


def struct(*shape, dtype=BF16):
    return jax.ShapeDtypeStruct(shape, dtype)


def flip(value, axis, bit):
    size = lax.axis_size(axis)
    return lax.ppermute(value, axis, [(i, i ^ bit) for i in range(size)])


def after(value, *others):
    return lax.optimization_barrier((value,) + others)[0]


def load(sources, held, sems):
    copies = [pltpu.make_async_copy(w, h, sems.at[i]) for i, (w, h) in enumerate(zip(sources, held))]
    for copy in copies:
        copy.start()
    return copies


def pack_body(heads, idx, *refs):
    sources, near, (far, quarter), packs = refs[:8], refs[8:10], refs[10:12], refs[12]
    held, sems = refs[13:21], refs[21]
    me, side, mine = idx[0], idx[1] & 1, idx[1] & 3
    half = far.shape[1]
    depth, inner = held[0].shape
    low = held[6].shape[0]
    width = inner // heads
    part = depth // 4
    copies = load(sources, held, sems)
    for copy in copies[:3]:
        copy.wait()
    for h in range(heads):
        parts = [held[i][:, h * width : (h + 1) * width] for i in range(3)]
        parts.append(jnp.zeros((depth, packs.shape[2] - 3 * width), BF16))
        packs[h] = jnp.concatenate(parts, 1)
    for r in range(2):
        near[r][...] = packs[me ^ r]
        far[r] = packs[me ^ (r + 2), pl.ds(pl.multiple_of(side * half, half), half), :]
    for copy in copies[3:]:
        copy.wait()
    at = pl.ds(pl.multiple_of(mine * part, part), part)
    for i in range(3):
        quarter[i * part : (i + 1) * part, :] = held[3 + i][at, :]
    for v in range(4):

        @pl.when(mine == v)
        def _(v=v):
            quarter[3 * part :, :] = held[6 + (v >> 1)][:, (v & 1) * inner : (v & 1) * inner + inner]


def block_body(n, per, idx, *refs):
    sources, block, near, across = refs[:6], refs[6], refs[7:9], refs[9]
    held, (wide, few, sems) = refs[10:16], refs[16:]
    me = idx[0]
    depth, inner = held[1].shape
    low = held[4].shape[0]
    copies = load(sources, held, sems)
    copies[0].wait()
    wide[...] = held[0][...].astype(F32)
    share = few.shape[0] // per
    tokens = wide.shape[0] // per
    for r in range(n):
        first = pl.multiple_of((me ^ r) * share, share)
        for j in range(per):
            few[j * share : (j + 1) * share, :] = wide[pl.ds(j * tokens + first, share), :]
        if r < 2:
            near[r][...] = few[...].astype(BF16)
        else:
            across[r - 2] = few[...].astype(BF16)
    for copy in copies[1:]:
        copy.wait()
    for i in range(3):
        block[i * depth : (i + 1) * depth, :] = held[1 + i][...]
    for v in range(4):
        at = 3 * depth + v * low
        block[at : at + low, :] = held[4 + (v >> 1)][:, (v & 1) * inner : (v & 1) * inner + inner]


def spatial_forward_body(n, tokens, width, idx, *refs):
    frames, refer, refs = refs[:n], refs[n : 2 * n], refs[2 * n :]
    near, far = refs[:2], ((refs[2], refs[3]), (refs[4], refs[5]))
    x_out, w_out, q_out, k_out, v_out, p_out, o_out = refs[6:13]
    mixed, turn, few = refs[13:]
    me, side = idx[0], idx[1] & 1
    share = tokens // n
    rows = frames[0].shape[0]
    depth = near[0].shape[0]
    half = depth // 2
    lanes = q_out.shape[1]
    room = w_out.shape[1]
    total = n * rows
    for r in range(2):
        w_out[pl.ds(pl.multiple_of((me ^ r) * depth, depth), depth), :] = near[r][...]
        for k in range(2):
            at = pl.multiple_of((me ^ (r + 2)) * depth + (side ^ k) * half, half)
            w_out[pl.ds(at, half), :] = far[r][k][r]
    for r in range(n):

        def norm(i, _, r=r):
            at = pl.multiple_of(i * CHUNK, CHUNK)
            centred, _ = layer_stats(frames[r][pl.ds(at, CHUNK), :])
            x_out[pl.ds(r * rows + at, CHUNK), :] = centred.astype(BF16)
            return 0

        lax.fori_loop(0, rows // CHUNK, norm, 0)
        few[r * share : (r + 1) * share, :] = refer[r][...].astype(F32)
    x_out[total:, :] = few[...].astype(BF16)
    for start, count in [(r * rows, rows) for r in range(n)] + [(total, tokens)]:
        three = mm(x_out[start : start + count, :], w_out[...])
        keep = lax.broadcasted_iota(jnp.int32, (count, lanes), 1) < width
        q_out[start : start + count, :] = jnp.where(keep, three[:, :lanes], 0.0).astype(BF16)
        k_out[start : start + count, :] = jnp.where(
            keep, pltpu.roll(three, room - width, 1)[:, :lanes], 0.0
        ).astype(BF16)
        v_out[start : start + count, :] = jnp.where(
            keep, pltpu.roll(three, room - 2 * width, 1)[:, :lanes], 0.0
        ).astype(BF16)
    scale = width**-0.5
    for b in range(total // tokens):
        at = slice(b * tokens, (b + 1) * tokens)
        keys = jnp.concatenate([k_out[at, :], k_out[total:, :]], 0)
        values = jnp.concatenate([v_out[at, :], v_out[total:, :]], 0)
        powers = jnp.exp(mm_bt(q_out[at, :], keys) * scale)
        probs = powers / jnp.sum(powers, -1, keepdims=True)
        p_out[at, :] = probs
        mixed[at, :] = mm(probs.astype(BF16), values)
    per = rows // tokens
    for r in range(n):
        first = pl.multiple_of((me ^ r) * share, share)
        for b in range(total // tokens):
            to = ((b // per) ^ r) * per + b % per
            turn[to * share : (to + 1) * share, :] = mixed[pl.ds(b * tokens + first, share), :]
        o_out[r] = turn[...].astype(BF16)


def spatial_backward_body(n, tokens, width, idx, *refs):
    grads = refs[:n]
    x_ref, w_ref, q_ref, k_ref, v_ref, p_ref = refs[n : n + 6]
    keep_out, send_out, keep_term, send_term = refs[n + 6 : n + 10]
    spread, turn, packed, term = refs[n + 10 :]
    me = idx[0]
    share = tokens // n
    total = p_ref.shape[0]
    rows = total // n
    lanes = q_ref.shape[1]
    room = w_ref.shape[1]
    per = rows // tokens
    for r in range(n):
        first = pl.multiple_of((me ^ r) * share, share)
        turn[...] = grads[r][...].astype(F32)
        for b in range(total // tokens):
            to = ((b // per) ^ r) * per + b % per
            spread[pl.ds(b * tokens + first, share), :] = turn[to * share : (to + 1) * share, :]
    scale = width**-0.5

    def pack(first, second, third):
        def wide(part):
            blank = jnp.zeros((part.shape[0], room - lanes), F32)
            return jnp.concatenate([part, blank], 1)

        result = pltpu.roll(wide(second), width, 1) + pltpu.roll(wide(third), 2 * width, 1)
        return result if first is None else result + wide(first)

    key_sum = jnp.zeros((k_ref.shape[0] - total, lanes), F32)
    value_sum = key_sum
    for b in range(total // tokens):
        at = slice(b * tokens, (b + 1) * tokens)
        query = q_ref[at, :]
        keys = jnp.concatenate([k_ref[at, :], k_ref[total:, :]], 0)
        values = jnp.concatenate([v_ref[at, :], v_ref[total:, :]], 0)
        cotangent = spread[at, :].astype(BF16)
        probs = p_ref[at, :]
        back = mm_bt(cotangent, values)
        score = (probs * (back - jnp.sum(probs * back, -1, keepdims=True)) * scale).astype(BF16)
        query_grad = mm(score, keys)
        key_grad = mm_at(score, query)
        value_grad = mm_at(probs.astype(BF16), cotangent)
        key_sum = key_sum + key_grad[tokens:]
        value_sum = value_sum + value_grad[tokens:]
        packed[at, :] = pack(query_grad, key_grad[:tokens], value_grad[:tokens]).astype(BF16)
    packed[total:, :] = pack(None, key_sum, value_sum).astype(BF16)
    for r in range(n):
        part = mm_bt(packed[r * rows : (r + 1) * rows, :], w_ref[...]).astype(BF16)
        (send_out if r & 1 else keep_out)[r >> 1, :rows, :] = part
    part = mm_bt(packed[total:, :], w_ref[...])
    for r in range(n):
        few = part[r * share : (r + 1) * share].astype(BF16)
        (send_out if r & 1 else keep_out)[r >> 1, rows:, :] = few
    depth = x_ref.shape[1] // 5
    for j in range(5):
        at = slice(j * depth, (j + 1) * depth)
        term[at, :] = mm_at(x_ref[:, at], packed[...])
    side = idx[1] & 1
    count, piece = keep_term.shape[0], keep_term.shape[2]
    for j in range(n):
        for k in range(count):
            for out, half in ((keep_term, side), (send_term, 1 - side)):
                at = pl.multiple_of((j * 2 * count + half * count + k) * piece, piece)
                out[k, j] = term[pl.ds(at, piece), :].astype(BF16)


def temporal_body(n, heads, per, idx, *refs):
    mixed, refs = refs[:n], refs[n:]
    near, far, refs = refs[:2], (refs[2:6], refs[6:10]), refs[10:]
    frames, table = refs[0], refs[n + 1]
    cotangents = refs[1 : n + 1]
    refs = refs[n + 2 :]
    grad_outs, back_outs, refs = refs[:n], refs[n : 2 * n], refs[2 * n :]
    gh_out, n2_out, gq_out, gk_out, gv_out, o2_out, cotangent = refs[:7]
    so, tq, tk, tv, to, hidden, centred, inverse, wide, qs, gos = refs[7:]
    me, quarter = idx[0], idx[1] & 3
    rows, dim = frames.shape
    inner = tq.shape[1]
    width = inner // heads
    depth, low = dim // n, inner // n
    part = depth // 4
    few = rows // n
    share = few // per
    for r in range(n):
        cotangent[r * few : (r + 1) * few, :] = cotangents[r][...] if r < 2 else cotangents[r][r - 2]
        base = (me ^ r) * depth
        low_at = pl.ds(pl.multiple_of((me ^ r) * low, low), low)

        def put(v, source, r=r, low_at=low_at):
            lanes = slice((v & 1) * inner, (v & 1) * inner + inner)
            if v < 2:
                so[r, :low, lanes] = source
            else:
                to[low_at, lanes] = source

        if r < 2:
            for i, whole in enumerate((tq, tk, tv)):
                whole[pl.ds(pl.multiple_of(base, depth), depth), :] = near[r][i * depth : (i + 1) * depth, :]
            for v in range(4):
                at = 3 * depth + v * low
                put(v, near[r][at : at + low, :])
        else:
            for s in range(4):
                source = far[r - 2][s]
                at = pl.ds(pl.multiple_of(base + (quarter ^ s) * part, part), part)
                for i, whole in enumerate((tq, tk, tv)):
                    whole[at, :] = source[i * part : (i + 1) * part, :]
                for v in range(4):

                    @pl.when((quarter ^ s) == v)
                    def _(v=v, source=source, put=put):
                        put(v, source[3 * part :, :])

        so[r, low:, :] = jnp.zeros((so.shape[1] - low, dim), BF16)
    step = dim // 5
    for j in range(5):
        at = slice(j * step, (j + 1) * step)
        acc = frames[:, at].astype(F32)
        for r in range(n):
            acc = acc + mm(mixed[r][...], so[r, :, at])
        hidden[:, at] = acc.astype(BF16).astype(F32)

    def norm(i, _):
        at = pl.ds(pl.multiple_of(i * share, share), share)
        offset, scale = layer_stats(hidden[at, :])
        centred[at, :] = offset
        inverse[at, :] = jnp.broadcast_to(scale, (share, inverse.shape[1]))
        wide[at, :] = offset + table[pl.ds(i, 1), :]
        return 0

    lax.fori_loop(0, rows // share, norm, 0)
    n2_out[...] = wide[...].astype(BF16)

    def token(axis):
        place = lax.broadcasted_iota(jnp.int32, (rows, rows), axis).astype(F32)
        return place - share * jnp.floor((place + 0.5) * (1.0 / share))

    same = token(0) == token(1)
    lane_head = lax.broadcasted_iota(jnp.int32, (rows, inner), 1)

    def own(h, value):
        inside = (lane_head >= h * width) & (lane_head < (h + 1) * width)
        return jnp.where(inside, value, 0.0)

    scale = width**-0.5
    query = mm(n2_out[...], tq[...])
    for h in range(heads):
        qs[h * rows : (h + 1) * rows, :] = own(h, query).astype(BF16)
    keys = mm(n2_out[...], tk[...]).astype(BF16)
    values = mm(n2_out[...], tv[...]).astype(BF16)
    mixed_grad = mm_bt(cotangent[...], to[...])
    for h in range(heads):
        gos[h * rows : (h + 1) * rows, :] = own(h, mixed_grad).astype(BF16)
    key_grad = jnp.zeros((rows, inner), F32)
    value_grad = jnp.zeros((rows, inner), F32)
    query_grad = jnp.zeros((rows, inner), F32)
    o2 = jnp.zeros((rows, inner), F32)
    for h in range(heads):
        at = slice(h * rows, (h + 1) * rows)
        scores = mm_bt(qs[at, :], keys) * scale
        powers = jnp.where(same, jnp.exp(scores), 0.0)
        probs = powers / jnp.sum(powers, -1, keepdims=True)
        rounded = probs.astype(BF16)
        o2 = o2 + own(h, mm(rounded, values))
        back = mm_bt(gos[at, :], values)
        score = (probs * (back - jnp.sum(probs * back, -1, keepdims=True)) * scale).astype(BF16)
        query_grad = query_grad + own(h, mm(score, keys))
        key_grad = key_grad + mm_at(score, qs[at, :])
        value_grad = value_grad + mm_at(rounded, gos[at, :])
    o2_out[...] = o2.astype(BF16)
    gq_out[...] = query_grad.astype(BF16)
    gk_out[...] = key_grad.astype(BF16)
    gv_out[...] = value_grad.astype(BF16)
    for j in range(5):
        at = slice(j * step, (j + 1) * step)
        wide[:, at] = (
            mm_bt(gq_out[...], tq[at, :]) + mm_bt(gk_out[...], tk[at, :]) + mm_bt(gv_out[...], tv[at, :])
        )

    def back_norm(i, _):
        at = pl.ds(pl.multiple_of(i * CHUNK, CHUNK), CHUNK)
        back = layer_back(centred[at, :], inverse[at, :1], wide[at, :])
        gh_out[at, :] = (cotangent[at, :].astype(F32) + back).astype(BF16)
        return 0

    lax.fori_loop(0, rows // CHUNK, back_norm, 0)
    for r in range(n):
        grad_outs[r][...] = mm_bt(gh_out[...], so[r]).astype(BF16)
    for j in range(5):
        at = slice(j * step, (j + 1) * step)
        part = (hidden[:, at] + mm(o2_out[...], to[:, at])).astype(BF16)
        for r in range(n):
            back_outs[r][:few, at] = part[r * few : (r + 1) * few]
    for r in range(n):
        back_outs[r][few:, :] = gh_out[r * few : (r + 1) * few, :]


def terms_body(n, idx, *refs):
    mixed = refs[:n]
    gh, n2, gq, gk, gv, o2, cotangent = refs[n : n + 7]
    talls, flats = refs[n + 7 : n + 9], refs[n + 9 : n + 11]
    tall, flat = refs[n + 11 :]
    me = idx[0]
    dim, inner = tall.shape
    depth, low = dim // n, inner // n
    pieces, piece = talls[0].shape[1], talls[0].shape[3]
    for i, grad in enumerate((gq, gk, gv)):
        for j in range(5):
            at = slice(j * (dim // 5), (j + 1) * (dim // 5))
            tall[at, :] = mm_at(n2[:, at], grad[...])
        for r in range(n):
            for p in range(pieces):
                at = pl.multiple_of((me ^ r) * depth + p * piece, piece)
                talls[r & 1][r >> 1, p, i] = tall[pl.ds(at, piece), :].astype(BF16)
    for j in range(5):
        at = slice(j * (inner // 5), (j + 1) * (inner // 5))
        flat[at, :] = mm_at(o2[:, at], cotangent[...]).astype(BF16)
    half = low // 2
    for r in range(n):
        out = flats[r & 1]
        mine = mm_at(mixed[r][...], gh[...])[:low].astype(BF16)
        for j in range(2):
            lanes = slice(j * inner, (j + 1) * inner)
            for k in range(2):
                at = pl.multiple_of((me ^ r) * low + k * half, half)
                out[r >> 1, 2 * j + k] = mine[k * half : (k + 1) * half, lanes]
                out[r >> 1, 4 + 2 * j + k] = flat[pl.ds(at, half), lanes]


def finish_body(n, per, idx, frames, *refs):
    parts, near, far = refs[:n], refs[n], refs[n + 1]
    out, frames_grad, refer_grad, turn, wide = refs[n + 2 :]
    me = idx[0]
    rows, few = frames.shape[0], parts[0].shape[0] // 2
    share, tokens = few // per, rows // per
    for r in range(n):
        first = pl.multiple_of((me ^ r) * share, share)
        turn[...] = parts[r][...].astype(F32)
        for which in range(2):
            for j in range(per):
                at = which * few + j * share
                wide[which, pl.ds(j * tokens + first, share), :] = turn[at : at + share, :]
    out[...] = wide[0].astype(BF16)

    def step(i, _):
        at = pl.ds(pl.multiple_of(i * CHUNK, CHUNK), CHUNK)
        centred, inverse = layer_stats(frames[at, :])
        grad = near[at, :].astype(F32) + far[at, :].astype(F32)
        back = layer_back(centred, inverse, grad)
        frames_grad[at, :] = (wide[1, at, :] + back).astype(BF16)
        return 0

    lax.fori_loop(0, rows // CHUNK, step, 0)
    refer_grad[...] = (near[rows:, :].astype(F32) + far[rows:, :].astype(F32)).astype(BF16)


def place_body(idx, near, far, *outs):
    side, level = idx[1] & 1, idx[1] >> 1
    count, _, piece = near.shape[:3]
    for source, half in ((near, side), (far, 1 - side)):
        for k in range(count):
            at = pl.multiple_of((half * count + (level ^ k)) * piece, piece)
            for i, out in enumerate(outs):
                out[pl.ds(at, piece), :] = source[k, i].astype(F32)


def place_flat_body(idx, near, far, *outs):
    side, level = idx[1] & 1, idx[1] >> 1
    count, piece, inner = near.shape
    for source, half in ((near, side), (far, 1 - side)):
        for k in range(count):
            place = level ^ k
            at = pl.multiple_of((place & 1) * piece, piece)
            for i, out in enumerate(outs):
                for j in range(2):

                    @pl.when((half == i) & ((place >> 1) == j))
                    def _(source=source, k=k, at=at, out=out, j=j):
                        out[pl.ds(at, piece), j * inner : (j + 1) * inner] = source[k].astype(F32)


def place_heads_body(width, idx, near, far, *outs):
    me, side, level = idx[0], idx[1] & 1, idx[1] >> 1
    count, n, piece = near.shape[:3]
    for source, half in ((near, side), (far, 1 - side)):
        for k in range(count):
            at = pl.multiple_of((half * count + (level ^ k)) * piece, piece)
            heads = [source[k, me ^ h].astype(F32) for h in range(n)]
            for i, out in enumerate(outs):
                parts = [h[:, i * width : (i + 1) * width] for h in heads]
                out[pl.ds(at, piece), :] = jnp.concatenate(parts, 1)


def add(*parts):
    total = parts[0].astype(F32)
    for part in parts[1:]:
        total = total + part.astype(F32)
    return total.astype(BF16)


def pick(value, index, axis=0):
    return lax.dynamic_index_in_dim(value, index, axis, keepdims=False)


class Links:
    def __init__(self, window):
        self.window = window
        self.past = {}

    def send(self, link, value, axis, bit):
        past = self.past.setdefault(link, [])
        if len(past) >= self.window:
            value = after(value, past[-self.window])
        got = flip(value, axis, bit)
        past.append(got)
        return got


def per_device(
    frames_in,
    ref_feats,
    out_grad,
    space_query,
    space_key,
    space_value,
    space_output,
    time_query,
    time_key,
    time_value,
    time_output,
):
    n = lax.axis_size("frame")
    clips = lax.axis_size("clip")
    me = lax.axis_index("frame")
    clip = lax.axis_index("clip")
    side, level = clip & 1, clip >> 1
    idx = jnp.stack([me, clip]).astype(jnp.int32)
    _, per, tokens, dim = frames_in.shape
    inner = space_query.shape[1]
    width = inner // HEADS
    lanes = -(-width // 128) * 128
    room = -(-3 * width // 128) * 128
    depth, low = dim // n, inner // n
    rows = per * tokens
    total = n * rows
    share = tokens // n
    few = per * share
    token_rows = n * few
    count, piece = clips // 2, depth // clips
    frames = frames_in.reshape(rows, dim)
    links = Links(2)

    def exchange(parts):
        return [parts[0]] + [flip(parts[r], "frame", r) for r in range(1, n)]

    def gather(value):
        far = flip(value, "frame", 2)
        return [value, flip(value, "frame", 1), far, flip(far, "frame", 1)]

    own, near, far_pack, quarter = wide_call(
        functools.partial(pack_body, HEADS),
        "pack_heads",
        [
            struct(depth, room),
            struct(depth, room),
            struct(2, depth // 2, room),
            struct(3 * depth // 4 + low, inner),
        ],
        [pltpu.VMEM((HEADS, depth, room), BF16)]
        + [pltpu.VMEM((depth, inner), BF16)] * 6
        + [pltpu.VMEM((low, dim), BF16)] * 2
        + [pltpu.SemaphoreType.DMA((8,))],
        60,
        0,
        9,
        8,
    )(idx, space_query, space_key, space_value, time_query, time_key, time_value, space_output, time_output)
    far_pack = flip(far_pack, "frame", 2)
    first = flip(quarter, "frame", 2)
    far_frames = flip(after(frames, far_pack), "frame", 2)
    all_refer = gather(ref_feats[0])
    side_pack = flip(far_pack, "clip", 1)
    packs = [own, flip(near, "frame", 1), far_pack, side_pack]
    packs = packs + [flip(p, "frame", 1) for p in packs[2:]]
    second, third = flip(first, "clip", 1), flip(first, "clip", 2)
    far = [first, second, third, flip(second, "clip", 2)]
    far_frames = after(far_frames, second, third)
    all_frames = [frames, flip(frames, "frame", 1), far_frames, flip(far_frames, "frame", 1)]
    far = far + [flip(p, "frame", 1) for p in far]
    block, grad_own, grad_near, across = wide_call(
        functools.partial(block_body, n, per),
        "weight_block",
        [struct(3 * depth + 4 * low, inner)] + [struct(few, dim)] * 2 + [struct(2, few, dim)],
        [pltpu.VMEM((rows, dim), BF16)]
        + [pltpu.VMEM((depth, inner), BF16)] * 3
        + [pltpu.VMEM((low, dim), BF16)] * 2
        + [pltpu.VMEM((rows, dim), F32), pltpu.VMEM((few, dim), F32), pltpu.SemaphoreType.DMA((6,))],
        60,
        0,
        7,
        6,
    )(idx, after(out_grad.reshape(rows, dim), own), time_query, time_key, time_value, space_output, time_output)
    blocks = [block, flip(block, "frame", 1)] + far
    across = flip(after(across, first), "frame", 2)
    token_grad = [grad_own, flip(grad_near, "frame", 1), across, flip(across, "frame", 1)]
    token_frames = jnp.concatenate(
        [
            lax.dynamic_slice_in_dim(f.reshape(per, tokens, dim), me * share, share, 1).reshape(few, dim)
            for f in all_frames
        ],
        0,
    )
    frame_ids = jnp.concatenate([(me ^ r) * per + jnp.arange(per) for r in range(n)])
    table = position_rows(frame_ids, dim)

    x_all, w_all, q_all, k_all, v_all, probs, mixed = wide_call(
        functools.partial(spatial_forward_body, n, tokens, width),
        "spatial_forward",
        [
            struct(total + tokens, dim),
            struct(dim, room),
            struct(total + tokens, lanes),
            struct(total + tokens, lanes),
            struct(total + tokens, lanes),
            struct(total, 2 * tokens, dtype=F32),
            struct(n, token_rows, lanes),
        ],
        [
            pltpu.VMEM((total, lanes), F32),
            pltpu.VMEM((token_rows, lanes), F32),
            pltpu.VMEM((tokens, dim), F32),
        ],
        26,
        2_000_000_000,
        2 * n + 7,
    )(idx, *all_frames, *all_refer, *packs)
    mixed = exchange(list(after([mixed[r] for r in range(n)], across)))

    outs = wide_call(
        functools.partial(temporal_body, n, HEADS, per),
        "temporal",
        [struct(token_rows, lanes)] * n
        + [struct(2 * few, dim)] * n
        + [struct(token_rows, dim)] * 2
        + [struct(token_rows, inner)] * 4
        + [struct(token_rows, dim)],
        [
            pltpu.VMEM((n, lanes, dim), BF16),
            pltpu.VMEM((dim, inner), BF16),
            pltpu.VMEM((dim, inner), BF16),
            pltpu.VMEM((dim, inner), BF16),
            pltpu.VMEM((inner, dim), BF16),
            pltpu.VMEM((token_rows, dim), F32),
            pltpu.VMEM((token_rows, dim), F32),
            pltpu.VMEM((token_rows, 128), F32),
            pltpu.VMEM((token_rows, dim), F32),
            pltpu.VMEM((HEADS * token_rows, inner), BF16),
            pltpu.VMEM((HEADS * token_rows, inner), BF16),
        ],
        36,
        5_000_000_000,
        2 * n + 13,
    )(idx, *mixed, *blocks, token_frames, *token_grad, table)
    mixed_grads = exchange(list(outs[:n]))
    backs = outs[n : 2 * n]
    hidden_grad, n2, gq, gk, gv, o2, token_grad = outs[2 * n :]

    keep_tall, send_tall, keep_flat, send_flat = wide_call(
        functools.partial(terms_body, n),
        "temporal_terms",
        [struct(n // 2, clips, 3, piece, inner)] * 2 + [struct(n // 2, clips, low // 2, inner)] * 2,
        [pltpu.VMEM((dim, inner), F32), pltpu.VMEM((inner, dim), BF16)],
        26,
        3_000_000_000,
        n + 8,
    )(idx, *mixed, hidden_grad, n2, gq, gk, gv, o2, token_grad)

    tall = add(keep_tall, flip(send_tall, "frame", 1))
    flat = add(keep_flat, flip(send_flat, "frame", 1))
    backs = exchange([backs[0]] + [after(t, mixed_grads[2]) for t in backs[1:]])
    mixed_grads[1] = after(mixed_grads[1], tall, flat)
    keep_out, send_out, keep_term, send_term = wide_call(
        functools.partial(spatial_backward_body, n, tokens, width),
        "spatial_backward",
        [struct(n // 2, rows + share, dim)] * 2 + [struct(count, n, piece, room)] * 2,
        [
            pltpu.VMEM((total, lanes), F32),
            pltpu.VMEM((token_rows, lanes), F32),
            pltpu.VMEM((total + tokens, room), BF16),
            pltpu.VMEM((dim, room), F32),
        ],
        26,
        4_000_000_000,
        n + 7,
    )(idx, *mixed_grads, x_all, w_all, q_all, k_all, v_all, probs)

    def over_x(value):
        moved = links.send("x", pick(value, 1 - side), "clip", 1)
        return add(pick(value, side), moved)

    def over_y(value):
        return add(value[0], links.send("y", value[1], "frame", 2))

    def over_z(value):
        moved = [links.send(f"z{k}", pick(value, level ^ k), "clip", 2 * k) for k in range(1, count)]
        return add(pick(value, level), *moved)

    def spread_z(value):
        return jnp.stack([value] + [links.send(f"z{k}", value, "clip", 2 * k) for k in range(1, count)])

    def spread_x(value):
        return value, links.send("x", value, "clip", 1)

    bit = level & 1
    flat = flat.reshape(n // 2, 2, 2, 2, low // 2, inner)
    flat = add(pick(flat, bit, 3), links.send("z1", pick(flat, 1 - bit, 3), "clip", 2))
    tall = over_y(tall).reshape(2, count, 3, piece, inner)
    head = add(keep_term, links.send("x", send_term, "clip", 1))
    flat = over_y(flat)
    head = over_z(head)
    tall = over_x(tall)
    flat = over_x(flat)
    head = jnp.stack(exchange([pick(head, me ^ r) for r in range(n)]))
    high = level >> 1
    flat = add(pick(flat, high), links.send("z2", pick(flat, 1 - high), "clip", 4))
    tall = over_z(tall)
    near = add(keep_out, flip(send_out, "frame", 1))
    head = after(head, near, *backs)
    partial_far = flip(near[1], "frame", 2)
    head = spread_z(head)
    flat = spread_z(flat)
    tall = spread_z(after(tall, partial_far))
    head = spread_x(head)
    flat = spread_x(flat)
    tall = spread_x(tall)

    output, frames_grad, refer_grad = wide_call(
        functools.partial(finish_body, n, per),
        "finish",
        [struct(rows, dim)] * 2 + [struct(share, dim)],
        [pltpu.VMEM((2 * few, dim), F32), pltpu.VMEM((2, rows, dim), F32)],
        16,
        0,
        n + 4,
    )(idx, frames, *backs, near[0], partial_far)

    head_grads = wide_call(
        functools.partial(place_heads_body, width),
        "place_heads",
        [struct(depth, inner, dtype=F32)] * 3,
        [],
        24,
        0,
        3,
    )(idx, *head)
    tall_grads = wide_call(place_body, "place_tall", [struct(depth, inner, dtype=F32)] * 3, [], 24, 0, 3)(idx, *tall)
    flat_grads = wide_call(place_flat_body, "place_flat", [struct(low, dim, dtype=F32)] * 2, [], 24, 0, 3)(idx, *flat)
    return (
        output.reshape(frames_in.shape),
        frames_grad.reshape(frames_in.shape),
        refer_grad[None],
        *head_grads,
        flat_grads[0],
        *tall_grads,
        flat_grads[1],
    )


def solution(mesh):
    in_specs = (
        P("clip", "frame", None, None),
        P("clip", "frame", None),
        P("clip", "frame", None, None),
        P("frame", None),
        P("frame", None),
        P("frame", None),
        P("frame", None),
        P("frame", None),
        P("frame", None),
        P("frame", None),
        P("frame", None),
    )
    out_specs = (
        P("clip", "frame", None, None),
        P("clip", "frame", None, None),
        P("clip", "frame", None),
        P("frame", None),
        P("frame", None),
        P("frame", None),
        P("frame", None),
        P("frame", None),
        P("frame", None),
        P("frame", None),
        P("frame", None),
    )
    clips = mesh.shape["clip"]
    by_heads = mesh.shape["frame"] == HEADS == 4 and clips == 8
    return jax.shard_map(
        per_device if by_heads else per_device_general, mesh=mesh, in_specs=in_specs, out_specs=out_specs, check_vma=False
    )
```

```python
import math

import functools
import itertools

import jax
import jax.numpy as jnp
from jax import lax
from jax.experimental import pallas as pl
from jax.experimental.pallas import tpu as pltpu
from jax.sharding import PartitionSpec as P

HEADS = 4
F32 = jnp.float32
BF16 = jnp.bfloat16


EPSILON = 1e-05


def layer_stats(rows):
    wide = rows.astype(jnp.float32)
    centre = jnp.mean(wide, -1, keepdims=True)
    offset = wide - centre
    inverse = lax.rsqrt(jnp.mean(offset * offset, -1, keepdims=True) + EPSILON)
    return (offset * inverse, inverse)


def layer_back(centred, inverse, cotangent):
    first = jnp.mean(cotangent, -1, keepdims=True)
    second = jnp.mean(cotangent * centred, -1, keepdims=True)
    return inverse * (cotangent - first - centred * second)


def position_table(first, count, width):
    frame_ids = (first + jnp.arange(count, dtype=jnp.int32)).astype(jnp.float32)
    halves = jnp.arange(width // 2, dtype=jnp.int32).astype(jnp.float32)
    rates = jnp.exp(halves * (-2.0 * math.log(10000.0) / width))
    angles = frame_ids[:, None] * rates[None, :]
    return jnp.stack([jnp.sin(angles), jnp.cos(angles)], -1).reshape(count, width)


def position_rows(frame_ids, width):
    lane = jnp.arange(width, dtype=jnp.int32)
    rates = jnp.exp((lane // 2).astype(F32) * (-2.0 * math.log(10000.0) / width))
    angles = frame_ids.astype(F32)[:, None] * rates[None, :]
    return jnp.where(lane % 2 == 0, jnp.sin(angles), jnp.cos(angles))


def einsum_forms(temporal):
    if temporal:
        return ("qbhe,kbhe->bhqk", "bhqk,kbhe->qbhe", "bhqk,qbhe->kbhe")
    return ("bqhe,bkhe->bhqk", "bhqk,bkhe->bqhe", "bhqk,bqhe->bkhe")


def product(form, left, right):
    return jnp.einsum(form, left, right, preferred_element_type=jnp.float32)


def attention(query, keys, values, temporal):
    score_form, mix_form, back_form = einsum_forms(temporal)
    scores = product(score_form, query, keys) * query.shape[-1] ** (-0.5)
    powers = jnp.exp(scores)
    probs = powers / jnp.sum(powers, -1, keepdims=True)
    rounded = probs.astype(jnp.bfloat16)
    mixed = product(mix_form, rounded, values).astype(jnp.bfloat16)
    return (mixed, probs, rounded)


def attention_back(query, keys, values, probs, rounded, cotangent, temporal):
    score_form, mix_form, back_form = einsum_forms(temporal)
    prob_grad = product(score_form, cotangent, values)
    score_grad = probs * (prob_grad - jnp.sum(probs * prob_grad, -1, keepdims=True))
    score_rounded = (score_grad * query.shape[-1] ** (-0.5)).astype(jnp.bfloat16)
    query_grad = product(mix_form, score_rounded, keys).astype(jnp.bfloat16)
    key_grad = product(back_form, score_rounded, query)
    value_grad = product(back_form, rounded, cotangent)
    return (query_grad, key_grad, value_grad)


def split_heads(rows):
    return rows.reshape(rows.shape[:-1] + (HEADS, rows.shape[-1] // HEADS))


def merge_heads(rows):
    return rows.reshape(rows.shape[:-2] + (rows.shape[-2] * rows.shape[-1],))


def project(rows, weight):
    flat_rows = rows.reshape(-1, rows.shape[-1])
    result = jnp.dot(flat_rows, weight, preferred_element_type=jnp.float32)
    return result.reshape(rows.shape[:-1] + (weight.shape[1],))


def project_back(rows, weight):
    flat_rows = rows.reshape(-1, rows.shape[-1])
    result = lax.dot_general(
        flat_rows, weight, (((1,), (1,)), ((), ())), preferred_element_type=jnp.float32
    )
    return result.reshape(rows.shape[:-1] + (weight.shape[0],))


def outer_sum(left, right):
    left_rows = left.reshape(-1, left.shape[-1])
    right_rows = right.reshape(-1, right.shape[-1])
    return lax.dot_general(
        left_rows, right_rows, (((0,), (0,)), ((), ())), preferred_element_type=jnp.float32
    )


def per_device_general(
    frames_in,
    ref_feats,
    out_grad,
    space_query,
    space_key,
    space_value,
    space_output,
    time_query,
    time_key,
    time_value,
    time_output,
):
    block = lax.axis_index("frame")
    (
        full_space_query,
        full_space_key,
        full_space_value,
        full_space_output,
        full_time_query,
        full_time_key,
        full_time_value,
        full_time_output,
    ) = (
        lax.all_gather(space_query, "frame", axis=0, tiled=True),
        lax.all_gather(space_key, "frame", axis=0, tiled=True),
        lax.all_gather(space_value, "frame", axis=0, tiled=True),
        lax.all_gather(space_output, "frame", axis=0, tiled=True),
        lax.all_gather(time_query, "frame", axis=0, tiled=True),
        lax.all_gather(time_key, "frame", axis=0, tiled=True),
        lax.all_gather(time_value, "frame", axis=0, tiled=True),
        lax.all_gather(time_output, "frame", axis=0, tiled=True),
    )
    frames = frames_in[0]
    refer = ref_feats[0]
    cotangent = out_grad[0]
    frame_count = frames.shape[0]
    token_count = frames.shape[1]
    centred_one, inverse_one = layer_stats(frames)
    normed_one = centred_one.astype(jnp.bfloat16)
    spatial_query = project(normed_one, full_space_query).astype(jnp.bfloat16)
    spatial_key = project(normed_one, full_space_key).astype(jnp.bfloat16)
    spatial_value = project(normed_one, full_space_value).astype(jnp.bfloat16)
    own_key = project(refer, full_space_key).astype(jnp.bfloat16)
    own_value = project(refer, full_space_value).astype(jnp.bfloat16)
    refer_key, refer_value = (
        lax.all_gather(own_key, "frame", axis=0, tiled=True),
        lax.all_gather(own_value, "frame", axis=0, tiled=True),
    )
    keys_joined = jnp.concatenate(
        [spatial_key, jnp.broadcast_to(refer_key[None], spatial_key.shape)], 1
    )
    values_joined = jnp.concatenate(
        [spatial_value, jnp.broadcast_to(refer_value[None], spatial_value.shape)], 1
    )
    spatial_mixed, spatial_probs, spatial_rounded = attention(
        split_heads(spatial_query), split_heads(keys_joined), split_heads(values_joined), False
    )
    spatial_mixed = merge_heads(spatial_mixed)
    hidden_one = (frames.astype(jnp.float32) + project(spatial_mixed, full_space_output)).astype(
        jnp.bfloat16
    )
    centred_two, inverse_two = layer_stats(hidden_one)
    table = position_table(block * frame_count, frame_count, frames.shape[2])
    normed_two = (centred_two + table[:, None, :]).astype(jnp.bfloat16)
    normed_rows = lax.all_to_all(normed_two, "frame", split_axis=1, concat_axis=0, tiled=True)
    temporal_query = project(normed_rows, full_time_query).astype(jnp.bfloat16)
    temporal_key = project(normed_rows, full_time_key).astype(jnp.bfloat16)
    temporal_value = project(normed_rows, full_time_value).astype(jnp.bfloat16)
    temporal_mixed, temporal_probs, temporal_rounded = attention(
        split_heads(temporal_query), split_heads(temporal_key), split_heads(temporal_value), True
    )
    mixed_two = lax.all_to_all(
        merge_heads(temporal_mixed), "frame", split_axis=0, concat_axis=1, tiled=True
    )
    output = (hidden_one.astype(jnp.float32) + project(mixed_two, full_time_output)).astype(
        jnp.bfloat16
    )
    mixed_grad_two = project_back(cotangent, full_time_output).astype(jnp.bfloat16)
    token_grad = lax.all_to_all(mixed_grad_two, "frame", split_axis=1, concat_axis=0, tiled=True)
    token_query_grad, token_key_grad, token_value_grad = attention_back(
        split_heads(temporal_query),
        split_heads(temporal_key),
        split_heads(temporal_value),
        temporal_probs,
        temporal_rounded,
        split_heads(token_grad),
        True,
    )
    query_grad_two, key_grad_two, value_grad_two = (
        lax.all_to_all(
            merge_heads(token_query_grad), "frame", split_axis=0, concat_axis=1, tiled=True
        ),
        lax.all_to_all(
            merge_heads(token_key_grad).astype(jnp.bfloat16),
            "frame",
            split_axis=0,
            concat_axis=1,
            tiled=True,
        ),
        lax.all_to_all(
            merge_heads(token_value_grad).astype(jnp.bfloat16),
            "frame",
            split_axis=0,
            concat_axis=1,
            tiled=True,
        ),
    )
    normed_grad_two = (
        project_back(query_grad_two, full_time_query)
        + project_back(key_grad_two, full_time_key)
        + project_back(value_grad_two, full_time_value)
    )
    hidden_grad = (
        cotangent.astype(jnp.float32) + layer_back(centred_two, inverse_two, normed_grad_two)
    ).astype(jnp.bfloat16)
    mixed_grad_one = project_back(hidden_grad, full_space_output).astype(jnp.bfloat16)
    query_grad_one, key_joined_grad, value_joined_grad = attention_back(
        split_heads(spatial_query),
        split_heads(keys_joined),
        split_heads(values_joined),
        spatial_probs,
        spatial_rounded,
        split_heads(mixed_grad_one),
        False,
    )
    query_grad_one = merge_heads(query_grad_one)
    key_grad_one = merge_heads(key_joined_grad[:, :token_count]).astype(jnp.bfloat16)
    value_grad_one = merge_heads(value_joined_grad[:, :token_count]).astype(jnp.bfloat16)
    partial_key = merge_heads(jnp.sum(key_joined_grad[:, token_count:], 0))
    partial_value = merge_heads(jnp.sum(value_joined_grad[:, token_count:], 0))
    summed_key, summed_value = (
        lax.psum_scatter(
            partial_key.astype(jnp.bfloat16), "frame", scatter_dimension=0, tiled=True
        ).astype(jnp.float32),
        lax.psum_scatter(
            partial_value.astype(jnp.bfloat16), "frame", scatter_dimension=0, tiled=True
        ).astype(jnp.float32),
    )
    refer_key_grad = summed_key.astype(jnp.bfloat16)
    refer_value_grad = summed_value.astype(jnp.bfloat16)
    normed_grad_one = (
        project_back(query_grad_one, full_space_query)
        + project_back(key_grad_one, full_space_key)
        + project_back(value_grad_one, full_space_value)
    )
    frames_grad = (
        hidden_grad.astype(jnp.float32) + layer_back(centred_one, inverse_one, normed_grad_one)
    ).astype(jnp.bfloat16)
    refer_grad = (
        project_back(refer_key_grad, full_space_key)
        + project_back(refer_value_grad, full_space_value)
    ).astype(jnp.bfloat16)
    term_sq = outer_sum(normed_one, query_grad_one)
    term_sk = outer_sum(normed_one, key_grad_one) + outer_sum(refer, refer_key_grad)
    term_sv = outer_sum(normed_one, value_grad_one) + outer_sum(refer, refer_value_grad)
    term_so = outer_sum(spatial_mixed, hidden_grad)
    term_tq = outer_sum(normed_two, query_grad_two)
    term_tk = outer_sum(normed_two, key_grad_two)
    term_tv = outer_sum(normed_two, value_grad_two)
    term_to = outer_sum(mixed_two, cotangent)
    share_sq, share_sk, share_sv, share_so, share_tq, share_tk, share_tv, share_to = (
        lax.psum_scatter(
            term_sq.astype(jnp.bfloat16), "frame", scatter_dimension=0, tiled=True
        ).astype(jnp.float32),
        lax.psum_scatter(
            term_sk.astype(jnp.bfloat16), "frame", scatter_dimension=0, tiled=True
        ).astype(jnp.float32),
        lax.psum_scatter(
            term_sv.astype(jnp.bfloat16), "frame", scatter_dimension=0, tiled=True
        ).astype(jnp.float32),
        lax.psum_scatter(
            term_so.astype(jnp.bfloat16), "frame", scatter_dimension=0, tiled=True
        ).astype(jnp.float32),
        lax.psum_scatter(
            term_tq.astype(jnp.bfloat16), "frame", scatter_dimension=0, tiled=True
        ).astype(jnp.float32),
        lax.psum_scatter(
            term_tk.astype(jnp.bfloat16), "frame", scatter_dimension=0, tiled=True
        ).astype(jnp.float32),
        lax.psum_scatter(
            term_tv.astype(jnp.bfloat16), "frame", scatter_dimension=0, tiled=True
        ).astype(jnp.float32),
        lax.psum_scatter(
            term_to.astype(jnp.bfloat16), "frame", scatter_dimension=0, tiled=True
        ).astype(jnp.float32),
    )
    total_sq, total_sk, total_sv, total_so, total_tq, total_tk, total_tv, total_to = (
        lax.psum(share_sq.astype(jnp.bfloat16), "clip").astype(jnp.float32),
        lax.psum(share_sk.astype(jnp.bfloat16), "clip").astype(jnp.float32),
        lax.psum(share_sv.astype(jnp.bfloat16), "clip").astype(jnp.float32),
        lax.psum(share_so.astype(jnp.bfloat16), "clip").astype(jnp.float32),
        lax.psum(share_tq.astype(jnp.bfloat16), "clip").astype(jnp.float32),
        lax.psum(share_tk.astype(jnp.bfloat16), "clip").astype(jnp.float32),
        lax.psum(share_tv.astype(jnp.bfloat16), "clip").astype(jnp.float32),
        lax.psum(share_to.astype(jnp.bfloat16), "clip").astype(jnp.float32),
    )
    return (
        output[None],
        frames_grad[None],
        refer_grad[None],
        total_sq,
        total_sk,
        total_sv,
        total_so,
        total_tq,
        total_tk,
        total_tv,
        total_to,
    )


CHUNK = 32


def mm(left, right):
    return jnp.dot(left, right, preferred_element_type=F32)


def mm_bt(left, right):
    return lax.dot_general(left, right, (((1,), (1,)), ((), ())), preferred_element_type=F32)


def mm_at(left, right):
    return lax.dot_general(left, right, (((0,), (0,)), ((), ())), preferred_element_type=F32)


def wide_call(body, name, out_shape, scratch, limit_mb, flops, num_in, kept=0, late=()):
    def with_late(idx, *refs):
        body(idx, *refs[: num_in - 1], *refs[num_in - 1 + len(late) :])

    call = pl.pallas_call(
        with_late,
        name=name,
        out_shape=out_shape,
        in_specs=[pl.BlockSpec(memory_space=pltpu.SMEM)]
        + [pl.BlockSpec(memory_space=pltpu.HBM)] * kept
        + [pl.BlockSpec(memory_space=pltpu.VMEM)] * (num_in - 1 - kept)
        + [pl.BlockSpec(memory_space=pl.ANY)] * len(late),
        out_specs=tuple(pl.BlockSpec(memory_space=pltpu.VMEM) for _ in out_shape),
        scratch_shapes=scratch,
        compiler_params=pltpu.CompilerParams(vmem_limit_bytes=limit_mb * 1024 * 1024),
        cost_estimate=pl.CostEstimate(
            flops=max(flops, 1), bytes_accessed=8_000_000 if flops > 1 else 1, transcendentals=0
        ),
    )
    return lambda *operands: call(*operands, *late)


def struct(*shape, dtype=BF16):
    return jax.ShapeDtypeStruct(shape, dtype)


def flip(value, axis, bit):
    size = lax.axis_size(axis)
    return lax.ppermute(value, axis, [(i, i ^ bit) for i in range(size)])


def after(value, *others):
    corners = [o[(slice(0, 1),) * (o.ndim - 2) + (slice(0, 8), slice(0, 128))] for o in others]
    return lax.optimization_barrier((value, *corners))[0]


def load(sources, held, sems):
    copies = [pltpu.make_async_copy(w, h, sems.at[i]) for i, (w, h) in enumerate(zip(sources, held))]
    for copy in copies:
        copy.start()
    return copies


def pack_body(heads, n, per, idx, *refs):
    sources, near, (far, first, grad_own, grad_near, across) = refs[:10], refs[10:12], refs[12:17]
    packs, held, (wide, few, sems) = refs[17], refs[18:28], refs[28:]
    me, side, mine = idx[0], idx[1] & 1, idx[1] & 3
    half = far.shape[1]
    depth, inner = held[0].shape
    low = held[6].shape[0]
    width = inner // heads
    part = depth // 4
    copies = load(sources, held, sems)
    for copy in copies[:3]:
        copy.wait()
    for h in range(heads):
        parts = [held[i][:, h * width : (h + 1) * width] for i in range(3)]
        parts.append(jnp.zeros((depth, packs.shape[2] - 3 * width), BF16))
        packs[h] = jnp.concatenate(parts, 1)
    for r in range(2):
        near[r][...] = packs[me ^ r]
        far[r] = packs[me ^ (r + 2), pl.ds(pl.multiple_of(side * half, half), half), :]
    for copy in copies[3:]:
        copy.wait()
    at = pl.ds(pl.multiple_of(mine * part, part), part)
    for i in range(3):
        first[i * part : (i + 1) * part, :] = held[3 + i][at, :]
    for v in range(4):

        @pl.when(mine == v)
        def _(v=v):
            first[3 * part :, :] = held[6 + (v >> 1)][:, (v & 1) * inner : (v & 1) * inner + inner]

    wide[...] = held[8][...].astype(F32)
    count = few.shape[0]
    share = count // per
    tokens = wide.shape[0] // per
    for r in range(n):
        start = pl.multiple_of((me ^ r) * share, share)
        for j in range(per):
            few[j * share : (j + 1) * share, :] = wide[pl.ds(j * tokens + start, share), :]
        if r == 0:
            grad_own[...] = few[...].astype(BF16)
        elif r == 1:
            grad_near[:count, :] = few[...].astype(BF16)
        else:
            across[(r - 2) * count : (r - 1) * count, :] = few[...].astype(BF16)
    grad_near[count:, :] = held[9][...]
    across[2 * count :, :] = held[9][...]


def spatial_forward_body(n, tokens, width, idx, *refs):
    sources, refs = refs[: 2 * n + 8], refs[2 * n + 8 :]
    x_out, w_out, q_out, k_out, v_out, p_out = refs[:6]
    o_outs, (token_out, tall_out, flat_out) = refs[6 : n + 6], refs[n + 6 : n + 9]
    mixed, turn, few, wide, spread, sems = refs[n + 9 : n + 15]
    held = refs[n + 15 :]
    cut = tall_out.shape[0]
    copies = load(sources, held, sems)
    frames, refer, packs = held[:n], held[n : 2 * n], held[2 * n :]
    near, far = packs[:2], ((packs[2], packs[3]), (packs[4], packs[5]))
    me, side = idx[0], idx[1] & 1
    share = tokens // n
    rows = frames[0].shape[0]
    depth = near[0].shape[0]
    half = depth // 2
    lanes = q_out.shape[1]
    room = w_out.shape[1]
    total = n * rows
    for r in range(n):
        copies[r].wait()

        def norm(i, _, r=r):
            at = pl.multiple_of(i * CHUNK, CHUNK)
            centred, _ = layer_stats(frames[r][pl.ds(at, CHUNK), :])
            x_out[pl.ds(r * rows + at, CHUNK), :] = centred.astype(BF16)
            return 0

        lax.fori_loop(0, rows // CHUNK, norm, 0)
        wide[...] = frames[r][...].astype(F32)
        first = pl.multiple_of(me * share, share)
        for j in range(rows // tokens):
            at = r * (rows // tokens) * share + j * share
            spread[at : at + share, :] = wide[pl.ds(j * tokens + first, share), :]
        copies[n + r].wait()
        few[r * share : (r + 1) * share, :] = refer[r][refer[r].shape[0] - share :, :].astype(F32)
    x_out[total:, :] = few[...].astype(BF16)
    token_out[...] = spread[...].astype(BF16)
    for copy in copies[2 * n :]:
        copy.wait()
    for r in range(2):
        w_out[pl.ds(pl.multiple_of((me ^ r) * depth, depth), depth), :] = near[r][...]
        for k in range(2):
            at = pl.multiple_of((me ^ (r + 2)) * depth + (side ^ k) * half, half)
            w_out[pl.ds(at, half), :] = far[r][k][r]
    second, third = packs[6:8]
    tall_out[...] = third[:cut, :]
    flat_out[...] = second[cut:, :]
    for start, count in [(r * rows, rows) for r in range(n)] + [(total, tokens)]:
        three = mm(x_out[start : start + count, :], w_out[...])
        keep = lax.broadcasted_iota(jnp.int32, (count, lanes), 1) < width
        q_out[start : start + count, :] = jnp.where(keep, three[:, :lanes], 0.0).astype(BF16)
        k_out[start : start + count, :] = jnp.where(
            keep, pltpu.roll(three, room - width, 1)[:, :lanes], 0.0
        ).astype(BF16)
        v_out[start : start + count, :] = jnp.where(
            keep, pltpu.roll(three, room - 2 * width, 1)[:, :lanes], 0.0
        ).astype(BF16)
    scale = width**-0.5
    for b in range(total // tokens):
        at = slice(b * tokens, (b + 1) * tokens)
        keys = jnp.concatenate([k_out[at, :], k_out[total:, :]], 0)
        values = jnp.concatenate([v_out[at, :], v_out[total:, :]], 0)
        powers = jnp.exp(mm_bt(q_out[at, :], keys) * scale)
        probs = powers / jnp.sum(powers, -1, keepdims=True)
        p_out[at, :] = probs
        mixed[at, :] = mm(probs.astype(BF16), values)
    per = rows // tokens
    for r in range(n):
        first = pl.multiple_of((me ^ r) * share, share)
        for b in range(total // tokens):
            to = ((b // per) ^ r) * per + b % per
            turn[to * share : (to + 1) * share, :] = mixed[pl.ds(b * tokens + first, share), :]
        o_outs[r][...] = turn[...].astype(BF16)


def spatial_backward_body(n, tokens, width, idx, *refs):
    grads = refs[:n]
    x_ref, w_ref, q_ref, k_ref, v_ref, p_ref = refs[n : n + 6]
    keep_out, send_out, keep_term, send_term = refs[n + 6 : n + 10]
    spread, turn, packed, term = refs[n + 10 :]
    me = idx[0]
    share = tokens // n
    total = p_ref.shape[0]
    rows = total // n
    lanes = q_ref.shape[1]
    room = w_ref.shape[1]
    per = rows // tokens
    for r in range(n):
        first = pl.multiple_of((me ^ r) * share, share)
        turn[...] = grads[r][...].astype(F32)
        for b in range(total // tokens):
            to = ((b // per) ^ r) * per + b % per
            spread[pl.ds(b * tokens + first, share), :] = turn[to * share : (to + 1) * share, :]
    scale = width**-0.5

    def pack(first, second, third):
        def wide(part):
            blank = jnp.zeros((part.shape[0], room - lanes), F32)
            return jnp.concatenate([part, blank], 1)

        result = pltpu.roll(wide(second), width, 1) + pltpu.roll(wide(third), 2 * width, 1)
        return result if first is None else result + wide(first)

    key_sum = jnp.zeros((k_ref.shape[0] - total, lanes), F32)
    value_sum = key_sum
    for b in range(total // tokens):
        at = slice(b * tokens, (b + 1) * tokens)
        query = q_ref[at, :]
        keys = jnp.concatenate([k_ref[at, :], k_ref[total:, :]], 0)
        values = jnp.concatenate([v_ref[at, :], v_ref[total:, :]], 0)
        cotangent = spread[at, :].astype(BF16)
        probs = p_ref[at, :]
        back = mm_bt(cotangent, values)
        score = (probs * (back - jnp.sum(probs * back, -1, keepdims=True)) * scale).astype(BF16)
        query_grad = mm(score, keys)
        key_grad = mm_at(score, query)
        value_grad = mm_at(probs.astype(BF16), cotangent)
        key_sum = key_sum + key_grad[tokens:]
        value_sum = value_sum + value_grad[tokens:]
        packed[at, :] = pack(query_grad, key_grad[:tokens], value_grad[:tokens]).astype(BF16)
    packed[total:, :] = pack(None, key_sum, value_sum).astype(BF16)
    for r in range(n):
        part = mm_bt(packed[r * rows : (r + 1) * rows, :], w_ref[...]).astype(BF16)
        (send_out if r & 1 else keep_out)[r >> 1, :rows, :] = part
    part = mm_bt(packed[total:, :], w_ref[...])
    for r in range(n):
        few = part[r * share : (r + 1) * share].astype(BF16)
        (send_out if r & 1 else keep_out)[r >> 1, rows:, :] = few
    depth = x_ref.shape[1] // 5
    for j in range(5):
        at = slice(j * depth, (j + 1) * depth)
        term[at, :] = mm_at(x_ref[:, at], packed[...])
    side = idx[1] & 1
    count, piece = keep_term.shape[0], keep_term.shape[2]
    for j in range(n):
        for k in range(count):
            for out, half in ((keep_term, side), (send_term, 1 - side)):
                at = pl.multiple_of((j * 2 * count + half * count + k) * piece, piece)
                out[k, j] = term[pl.ds(at, piece), :].astype(BF16)


def parts_of(ref, dim, inner):
    starts = [0, dim, 2 * dim] + [3 * dim + i * inner for i in range(4)]
    parts = [ref.at[:, a : a + (dim if i < 3 else inner)] for i, a in enumerate(starts)]
    first, lanes = 3 * dim + 4 * inner, (ref.shape[1] - 3 * dim - 4 * inner) // 2
    return parts + [ref.at[:, first + i * lanes : first + (i + 1) * lanes] for i in range(2)]


def temporal_body(n, heads, per, idx, *refs):
    mixed_in, near, far, refs = refs[:n], (refs[n : n + 5], refs[n + 5 : n + 10]), refs[n + 10 :][:10], refs[n + 20 :]
    far = (far[:5], far[5:])
    frames_in, cotangents, table_in, refs = refs[0], refs[1 : n + 1], refs[n + 1], refs[n + 2 :]
    grad_outs, back_outs, kept, refs = refs[:n], refs[n : 2 * n], refs[2 * n], refs[2 * n + 1 :]
    so, tq, tk, tv, to, hidden, centred, inverse, wide, qs, gos = refs[:11]
    mixed, frames, table, sems = refs[11 : n + 11], *refs[n + 11 :]
    me, quarter = idx[0], idx[1] & 3
    rows, dim = frames.shape
    inner = tq.shape[1]
    width = inner // heads
    depth, low = dim // n, inner // n
    part = depth // 4
    few = rows // n
    share = few // per
    gh_out, n2_out, cotangent, gq_out, gk_out, gv_out, o2_out, *o_outs = parts_of(kept, dim, inner)
    first, second, chosen = [], [], []

    def bring(source, to_ref, group):
        group.append(pltpu.make_async_copy(source, to_ref, sems.at[len(first) + len(second) + len(chosen)]))

    def low_rows(r):
        return pl.ds(pl.multiple_of((me ^ r) * low, low), low)

    for r in range(n):
        bring(mixed_in[r], mixed[r], first)
        if r < 2:
            bring(near[r][3], so.at[r, pl.ds(0, low), :], first)
    bring(frames_in, frames, first)
    bring(table_in, table, first)
    for r in range(2, n):
        for s in range(4):
            flat, start = (far[r - 2][s], 3 * part) if s < 3 else (far[r - 2][4], 0)
            place = len(first) + len(second) + len(chosen)
            cases = []
            for v in range(4):
                lanes = pl.ds((v & 1) * inner, inner)
                target = so.at[r, pl.ds(0, low), lanes] if v < 2 else to.at[low_rows(r), lanes]
                source = flat.at[pl.ds(start, low), :]
                cases.append((v, pltpu.make_async_copy(source, target, sems.at[place])))
            chosen.append((quarter ^ s, cases))
    for r in range(n):
        if r < 2:
            bring(near[r][4], to.at[low_rows(r), :], second)
        for i, whole in enumerate((tq, tk, tv)):
            if r < 2:
                at = pl.ds(pl.multiple_of((me ^ r) * depth, depth), depth)
                bring(near[r][i], whole.at[at, :], second)
                continue
            for s in range(4):
                at = pl.ds(pl.multiple_of((me ^ r) * depth + (quarter ^ s) * part, part), part)
                bring(far[r - 2][s].at[pl.ds(i * part, part), :], whole.at[at, :], second)
        source = cotangents[r].at[pl.ds(few if r == 3 else 0, few), :]
        bring(source, cotangent.at[pl.ds(r * few, few), :], second)

    def choose(act):
        for which, cases in chosen:
            for v, copy in cases:

                @pl.when(which == v)
                def _(copy=copy):
                    act(copy)

    for copy in first:
        copy.start()
    choose(lambda copy: copy.start())
    for copy in second:
        copy.start()
    so[:, low:, :] = jnp.zeros((n, so.shape[1] - low, dim), BF16)
    for copy in first:
        copy.wait()
    choose(lambda copy: copy.wait())
    for i in range(2):
        o_outs[i][...] = mixed[2 * i + 1][...]
    step = dim // 5
    for j in range(5):
        at = slice(j * step, (j + 1) * step)
        acc = frames[:, at].astype(F32)
        for r in range(n):
            acc = acc + mm(mixed[r][...], so[r, :, at])
        hidden[:, at] = acc.astype(BF16).astype(F32)

    def norm(i, _):
        at = pl.ds(pl.multiple_of(i * share, share), share)
        offset, scale = layer_stats(hidden[at, :])
        centred[at, :] = offset
        inverse[at, :] = jnp.broadcast_to(scale, (share, inverse.shape[1]))
        wide[at, :] = offset + table[pl.ds(i, 1), :]
        return 0

    lax.fori_loop(0, rows // share, norm, 0)
    n2_out[...] = wide[...].astype(BF16)
    for copy in second:
        copy.wait()

    def token(axis):
        place = lax.broadcasted_iota(jnp.int32, (rows, rows), axis).astype(F32)
        return place - share * jnp.floor((place + 0.5) * (1.0 / share))

    same = token(0) == token(1)
    lane_head = lax.broadcasted_iota(jnp.int32, (rows, inner), 1)

    def own(h, value):
        inside = (lane_head >= h * width) & (lane_head < (h + 1) * width)
        return jnp.where(inside, value, 0.0)

    scale = width**-0.5
    query = mm(n2_out[...], tq[...])
    for h in range(heads):
        qs[h * rows : (h + 1) * rows, :] = own(h, query).astype(BF16)
    keys = mm(n2_out[...], tk[...]).astype(BF16)
    values = mm(n2_out[...], tv[...]).astype(BF16)
    mixed_grad = mm_bt(cotangent[...], to[...])
    for h in range(heads):
        gos[h * rows : (h + 1) * rows, :] = own(h, mixed_grad).astype(BF16)
    key_grad = jnp.zeros((rows, inner), F32)
    value_grad = jnp.zeros((rows, inner), F32)
    query_grad = jnp.zeros((rows, inner), F32)
    o2 = jnp.zeros((rows, inner), F32)
    for h in range(heads):
        at = slice(h * rows, (h + 1) * rows)
        scores = mm_bt(qs[at, :], keys) * scale
        powers = jnp.where(same, jnp.exp(scores), 0.0)
        probs = powers / jnp.sum(powers, -1, keepdims=True)
        rounded = probs.astype(BF16)
        o2 = o2 + own(h, mm(rounded, values))
        back = mm_bt(gos[at, :], values)
        score = (probs * (back - jnp.sum(probs * back, -1, keepdims=True)) * scale).astype(BF16)
        query_grad = query_grad + own(h, mm(score, keys))
        key_grad = key_grad + mm_at(score, qs[at, :])
        value_grad = value_grad + mm_at(rounded, gos[at, :])
    o2_out[...] = o2.astype(BF16)
    gq_out[...] = query_grad.astype(BF16)
    gk_out[...] = key_grad.astype(BF16)
    gv_out[...] = value_grad.astype(BF16)
    for j in range(5):
        at = slice(j * step, (j + 1) * step)
        wide[:, at] = (
            mm_bt(gq_out[...], tq[at, :]) + mm_bt(gk_out[...], tk[at, :]) + mm_bt(gv_out[...], tv[at, :])
        )

    def back_norm(i, _):
        at = pl.ds(pl.multiple_of(i * CHUNK, CHUNK), CHUNK)
        back = layer_back(centred[at, :], inverse[at, :1], wide[at, :])
        gh_out[at, :] = (cotangent[at, :].astype(F32) + back).astype(BF16)
        return 0

    lax.fori_loop(0, rows // CHUNK, back_norm, 0)
    for r in range(n):
        grad_outs[r][...] = mm_bt(gh_out[...], so[r]).astype(BF16)
    for j in range(5):
        at = slice(j * step, (j + 1) * step)
        part = (hidden[:, at] + mm(o2_out[...], to[:, at])).astype(BF16)
        for r in range(n):
            back_outs[r][:few, at] = part[r * few : (r + 1) * few]
    for r in range(n):
        back_outs[r][few:, :] = gh_out[r * few : (r + 1) * few, :]


def terms_body(n, idx, *refs):
    held, refs = refs[:4], refs[4:]
    tall_keep, tall_send, flat_keep, flat_send = refs[:4]
    n2_turned, o2_turned, tall, so = refs[4:]
    me, bit = idx[0], (idx[1] >> 1) & 1
    rows = held[0].shape[0]
    depth, inner = tall.shape
    dim, low = depth * n, inner // n
    pieces, _, piece = tall_keep.shape[:3]
    both = [parts_of(ref, dim, inner) for ref in held[:2]]
    for i in range(2):
        n2_turned[:, i * rows : (i + 1) * rows] = both[i][1][...].T
        o2_turned[:, i * rows : (i + 1) * rows] = both[i][6][...].T
    ours, theirs = both
    mixed = [*held[2:], *theirs[7:]]
    for i in range(3):
        grad = jnp.concatenate([ours[3 + i][...], theirs[3 + i][...]], 0)
        for k, out in enumerate((tall_keep, tall_send)):
            at = pl.multiple_of((me ^ (2 * k)) * depth, depth)
            tall[...] = mm(n2_turned[pl.ds(at, depth), :], grad)
            for p in range(pieces):
                out[p, i] = tall[p * piece : (p + 1) * piece, :].astype(BF16)
    half = low // 2
    for k in range(2):
        so[0] = (mm_at(mixed[k][...], ours[0][...]) + mm_at(mixed[2 + k][...], theirs[0][...]))[:low]
        at = pl.multiple_of((me ^ (2 * k)) * low, low)
        grad = jnp.concatenate([ours[2][...], theirs[2][...]], 0)
        so[1] = mm(o2_turned[pl.ds(at, low), :], grad)
        for i in range(2):
            for j in range(2):
                for out, part in ((flat_keep, bit), (flat_send, 1 - bit)):
                    at = pl.multiple_of(part * half, half)
                    out[k, i, j] = so[i, pl.ds(at, half), j * inner : (j + 1) * inner].astype(BF16)


def finish_body(n, per, idx, frames, *refs):
    parts, near, far = refs[:n], refs[n], refs[n + 1]
    out, frames_grad, refer_grad, turn, wide = refs[n + 2 :]
    me = idx[0]
    rows, few = frames.shape[0], parts[0].shape[0] // 2
    share, tokens = few // per, rows // per
    for r in range(n):
        first = pl.multiple_of((me ^ r) * share, share)
        turn[...] = parts[r][...].astype(F32)
        for which in range(2):
            for j in range(per):
                at = which * few + j * share
                wide[which, pl.ds(j * tokens + first, share), :] = turn[at : at + share, :]
    out[...] = wide[0].astype(BF16)

    def step(i, _):
        at = pl.ds(pl.multiple_of(i * CHUNK, CHUNK), CHUNK)
        centred, inverse = layer_stats(frames[at, :])
        grad = near[at, :].astype(F32) + far[at, :].astype(F32)
        back = layer_back(centred, inverse, grad)
        frames_grad[at, :] = (wide[1, at, :] + back).astype(BF16)
        return 0

    lax.fori_loop(0, rows // CHUNK, step, 0)
    refer_grad[...] = (near[rows:, :].astype(F32) + far[rows:, :].astype(F32)).astype(BF16)


def place_body(idx, near, far, *outs):
    side, low_bit = idx[1] & 1, (idx[1] >> 1) & 1
    piece = near.shape[3]
    for low, source in enumerate((near, far)):
        for high, other in itertools.product(range(2), range(2)):
            place = (side ^ other) * 4 + 2 * high + (low_bit ^ low)
            at = pl.multiple_of(place * piece, piece)
            for i, out in enumerate(outs):
                out[pl.ds(at, piece), :] = source[high, other, i].astype(F32)


def place_heads_body(width, idx, near, far, *outs):
    me, side, low_bit = idx[0], idx[1] & 1, (idx[1] >> 1) & 1
    _, _, n, piece, _ = near.shape
    for low, source in enumerate((near, far)):
        for high, other in itertools.product(range(2), range(2)):
            place = (side ^ other) * 4 + 2 * high + (low_bit ^ low)
            at = pl.multiple_of(place * piece, piece)
            heads = [source[high, other, me ^ h].astype(F32) for h in range(n)]
            for i, out in enumerate(outs):
                parts = [h[:, i * width : (i + 1) * width] for h in heads]
                out[pl.ds(at, piece), :] = jnp.concatenate(parts, 1)


def place_flat_body(idx, near, far, *outs):
    side, low_bit = idx[1] & 1, (idx[1] >> 1) & 1
    piece, inner = near.shape[2:]
    for source, half in ((near, side), (far, 1 - side)):
        for high, low in itertools.product(range(2), range(2)):
            at = pl.multiple_of((low_bit ^ low) * piece, piece)
            for i, out in enumerate(outs):

                @pl.when(half == i)
                def _(source=source, high=high, low=low, at=at, out=out):
                    lanes = slice(high * inner, (high + 1) * inner)
                    out[pl.ds(at, piece), lanes] = source[high, low].astype(F32)


def merge_body(axis, place, spread, idx, kept, moved, *outs):
    shape = kept.shape
    bit = None if axis is None else (idx[1] >> place) & 1
    for at in itertools.product(*map(range, shape[:-2])):
        if axis is not None:
            if at[axis]:
                continue
            rest = at[:axis] + at[axis + 1 :]
            for out, half in ((outs[0], bit), (outs[1], 1 - bit)):
                here = at[:axis] + (half,) + at[axis + 1 :]
                out[rest] = (kept[here].astype(F32) + moved[here].astype(F32)).astype(BF16)
        elif spread:
            here = (at[0], idx[0] ^ at[1])
            outs[at[1]][at[0]] = (kept[here].astype(F32) + moved[here].astype(F32)).astype(BF16)
        else:
            outs[0][at] = (kept[at].astype(F32) + moved[at].astype(F32)).astype(BF16)


def join_body(axis, idx, *refs):
    out = refs[-1]
    for i, part in enumerate(refs[:-1]):
        for at in itertools.product(*map(range, part.shape[:-2])):
            out[at[:axis] + (i,) + at[axis:]] = part[at]


def pick(value, index, axis=0):
    return lax.dynamic_index_in_dim(value, index, axis, keepdims=False)


class Steps:
    def __init__(self, idx):
        self.idx, self.last = idx, ()

    def call(self, body, name, out_shape, operands, scratch=(), limit_mb=12):
        def marked(idx, *refs):
            ends = len(operands) + len(out_shape)
            body(idx, *refs[:ends], *refs[ends + 1 :])
            refs[ends][...] = jnp.zeros(refs[ends].shape, F32)

        *outs, mark = wide_call(
            marked,
            name,
            list(out_shape) + [struct(8, 128, dtype=F32)],
            list(scratch),
            limit_mb,
            0,
            len(operands) + 1,
            0,
            self.last,
        )(self.idx, *operands)
        self.last = (mark,)
        return outs

    def merge(self, kept, moved, axis=None, place=0, spread=False):
        shape = kept.shape
        if axis is not None:
            shapes = [shape[:axis] + shape[axis + 1 :]] * 2
        else:
            shapes = [shape[:1] + shape[2:]] * shape[1] if spread else [shape]
        body = functools.partial(merge_body, axis, place, spread)
        outs = self.call(body, "merge", [struct(*one) for one in shapes], [kept, moved])
        return outs if len(outs) > 1 else outs[0]

    def join(self, *parts, axis=0):
        shape = parts[0].shape
        shape = shape[:axis] + (len(parts),) + shape[axis:]
        return self.call(functools.partial(join_body, axis), "join", [struct(*shape)], parts)[0]


def per_device(
    frames_in,
    ref_feats,
    out_grad,
    space_query,
    space_key,
    space_value,
    space_output,
    time_query,
    time_key,
    time_value,
    time_output,
):
    n = lax.axis_size("frame")
    clips = lax.axis_size("clip")
    me = lax.axis_index("frame")
    clip = lax.axis_index("clip")
    side, level = clip & 1, clip >> 1
    idx = jnp.stack([me, clip]).astype(jnp.int32)
    _, per, tokens, dim = frames_in.shape
    inner = space_query.shape[1]
    width = inner // HEADS
    lanes = -(-width // 128) * 128
    room = -(-3 * width // 128) * 128
    depth, low = dim // n, inner // n
    rows = per * tokens
    total = n * rows
    share = tokens // n
    few = per * share
    token_rows = n * few
    count, piece = clips // 2, depth // clips
    frames = frames_in.reshape(rows, dim)
    steps = Steps(idx)

    def exchange(parts):
        return [parts[0]] + [flip(parts[r], "frame", r) for r in range(1, n)]

    def gather(value):
        far = flip(value, "frame", 2)
        return [value, flip(value, "frame", 1), far, flip(far, "frame", 1)]

    others = (time_query, time_key, time_value, space_output, time_output)
    own, near, far_pack, first, grad_own, grad_near, across = wide_call(
        functools.partial(pack_body, HEADS, n, per),
        "pack_heads",
        [
            struct(depth, room),
            struct(depth, room),
            struct(2, depth // 2, room),
            struct(3 * depth // 4 + low, inner),
            struct(few, dim),
            struct(few + share, dim),
            struct(2 * few + share, dim),
        ],
        [pltpu.VMEM((HEADS, depth, room), BF16)]
        + [pltpu.VMEM((depth, inner), BF16)] * 6
        + [pltpu.VMEM((low, dim), BF16)] * 2
        + [
            pltpu.VMEM((rows, dim), BF16),
            pltpu.VMEM((share, dim), BF16),
            pltpu.VMEM((rows, dim), F32),
            pltpu.VMEM((few, dim), F32),
            pltpu.SemaphoreType.DMA((10,)),
        ],
        60,
        0,
        11,
        10,
    )(idx, space_query, space_key, space_value, *others, out_grad.reshape(rows, dim), ref_feats[0])
    first = flip(first, "frame", 2)
    far_pack = flip(far_pack, "frame", 2)
    far_frames = flip(after(frames, far_pack), "frame", 2)
    across = flip(after(across, far_pack), "frame", 2)
    side_pack = flip(far_pack, "clip", 1)
    second, third = flip(first, "clip", 1), flip(first, "clip", 2)
    near, grad_near, near_frames = (flip(v, "frame", 1) for v in (near, grad_near, frames))
    packs = [own, near, far_pack, side_pack, flip(far_pack, "frame", 1), flip(side_pack, "frame", 1)]
    all_frames = [frames, near_frames, far_frames, flip(far_frames, "frame", 1)]
    across_near = flip(across, "frame", 1)
    all_refer = [ref_feats[0], grad_near, across, across_near]
    token_grad = [grad_own, grad_near, across, across_near]
    far = [first, second, third]
    far_near = [flip(p, "frame", 1) for p in far]
    others_near = [flip(p, "frame", 1) for p in others]
    frame_ids = jnp.concatenate([(me ^ r) * per + jnp.arange(per) for r in range(n)])
    table = position_rows(frame_ids, dim)

    cut = 3 * depth // 4
    x_all, w_all, q_all, k_all, v_all, probs, *mixed, token_frames, tall_part, flat_part = wide_call(
        functools.partial(spatial_forward_body, n, tokens, width),
        "spatial_forward",
        [
            struct(total + tokens, dim),
            struct(dim, room),
            struct(total + tokens, lanes),
            struct(total + tokens, lanes),
            struct(total + tokens, lanes),
            struct(total, 2 * tokens, dtype=F32),
            *[struct(token_rows, lanes)] * n,
            struct(token_rows, dim),
            struct(cut, inner),
            struct(low, inner),
        ],
        [
            pltpu.VMEM((total, lanes), F32),
            pltpu.VMEM((token_rows, lanes), F32),
            pltpu.VMEM((tokens, dim), F32),
            pltpu.VMEM((rows, dim), F32),
            pltpu.VMEM((token_rows, dim), F32),
            pltpu.SemaphoreType.DMA((2 * n + 8,)),
        ]
        + [pltpu.VMEM((rows, dim), BF16)] * n
        + [pltpu.VMEM(one.shape, BF16) for one in all_refer]
        + [pltpu.VMEM((depth, room), BF16)] * 2
        + [pltpu.VMEM((2, depth // 2, room), BF16)] * 4
        + [pltpu.VMEM((cut + low, inner), BF16)] * 2,
        60,
        2_000_000_000,
        2 * n + 9,
        2 * n + 8,
        (*far_near, *others_near),
    )(idx, *all_frames, *all_refer, *packs, second, third)
    mixed = exchange(mixed)
    fourth = [flip(tall_part, "clip", 1), flip(flat_part, "clip", 2)]
    fourth_near = [flip(p, "frame", 1) for p in fourth]
    blocks = [*others, *others_near, *far, *fourth, *far_near, *fourth_near]
    outs = wide_call(
        functools.partial(temporal_body, n, HEADS, per),
        "temporal",
        [struct(token_rows, lanes)] * n
        + [struct(2 * few, dim)] * n
        + [struct(token_rows, 3 * dim + 4 * inner + 2 * lanes)],
        [
            pltpu.VMEM((n, lanes, dim), BF16),
            pltpu.VMEM((dim, inner), BF16),
            pltpu.VMEM((dim, inner), BF16),
            pltpu.VMEM((dim, inner), BF16),
            pltpu.VMEM((inner, dim), BF16),
            pltpu.VMEM((token_rows, dim), F32),
            pltpu.VMEM((token_rows, dim), F32),
            pltpu.VMEM((token_rows, 128), F32),
            pltpu.VMEM((token_rows, dim), F32),
            pltpu.VMEM((HEADS * token_rows, inner), BF16),
            pltpu.VMEM((HEADS * token_rows, inner), BF16),
        ]
        + [pltpu.VMEM((token_rows, lanes), BF16)] * n
        + [
            pltpu.VMEM((token_rows, dim), BF16),
            pltpu.VMEM(table.shape, F32),
            pltpu.SemaphoreType.DMA((60,)),
        ],
        60,
        5_000_000_000,
        2 * n + 23,
        2 * n + 22,
    )(idx, *mixed, *blocks, token_frames, *token_grad, table)
    mixed_grads = exchange(list(outs[:n]))
    backs = outs[n : 2 * n]

    ours = outs[2 * n]
    keep_tall, send_tall, keep_flat, send_flat = wide_call(
        functools.partial(terms_body, n),
        "temporal_terms",
        [struct(clips, 3, piece, inner)] * 2 + [struct(2, 2, 2, low // 2, inner)] * 2,
        [
            pltpu.VMEM((dim, 2 * token_rows), BF16),
            pltpu.VMEM((inner, 2 * token_rows), BF16),
            pltpu.VMEM((depth, inner), F32),
            pltpu.VMEM((2, low, dim), F32),
        ],
        18,
        1,
        5,
        0,
        tuple(mixed_grads[1:]),
    )(idx, ours, flip(ours, "frame", 1), mixed[0], mixed[2])
    flat_a = flip(send_flat, "clip", 2)
    tall_y = flip(send_tall, "frame", 2)

    keep_out, send_out, keep_term, send_term = wide_call(
        functools.partial(spatial_backward_body, n, tokens, width),
        "spatial_backward",
        [struct(n // 2, rows + share, dim)] * 2 + [struct(count, n, piece, room)] * 2,
        [
            pltpu.VMEM((total, lanes), F32),
            pltpu.VMEM((token_rows, lanes), F32),
            pltpu.VMEM((total + tokens, room), BF16),
            pltpu.VMEM((dim, room), F32),
        ],
        20,
        1,
        n + 7,
        0,
        (send_flat, send_tall),
    )(idx, *mixed_grads, x_all, w_all, q_all, k_all, v_all, probs)

    def to_clip(value, bit):
        return flip(value, "clip", bit)

    head_got = to_clip(send_term, 1)
    out_got = flip(send_out, "frame", 1)
    flat, flat_out = steps.merge(keep_flat, flat_a, 0, 7)
    halves = (2, 2, 2, 3, piece, inner)
    tall, tall_out = steps.merge(keep_tall.reshape(halves), tall_y.reshape(halves), 0, 0)
    tall_got = to_clip(tall_out, 1)
    flat_got = flip(flat_out, "frame", 2)
    halves = (2, 2, n, piece, room)
    head, head_out = steps.merge(keep_term.reshape(halves), head_got.reshape(halves), 1, 1)
    head_got = to_clip(head_out, 2)
    partial, partial_out = steps.merge(keep_out, out_got, 0, 7)
    head = steps.merge(head, head_got)
    head_got = to_clip(head, 4)
    flat, flat_out = steps.merge(flat, flat_got, 0, 0)
    flat_got = to_clip(flat_out, 1)
    tall, tall_out = steps.merge(tall, tall_got, 1, 1)
    tall_got = to_clip(tall_out, 2)
    head_f = exchange(steps.merge(head, head_got, spread=True))
    flat = steps.merge(flat, flat_got)
    flat_got = to_clip(flat, 4)
    tall = steps.merge(tall, tall_got)
    tall_got = to_clip(tall, 4)
    head = steps.join(*head_f, axis=1)
    head_got = to_clip(head, 1)
    backs = exchange(list(backs))
    partial_got = flip(partial_out, "frame", 2)
    head = steps.join(head, head_got, axis=1)
    head_got = to_clip(head, 2)
    output, frames_grad, refer_grad = steps.call(
        functools.partial(finish_body, n, per),
        "finish",
        [struct(rows, dim)] * 2 + [struct(share, dim)],
        [frames, *backs, partial, partial_got],
        [pltpu.VMEM((2 * few, dim), F32), pltpu.VMEM((2, rows, dim), F32)],
    )
    flat = steps.merge(flat, flat_got)
    flat_got = to_clip(flat, 2)
    tall = steps.merge(tall, tall_got)
    tall_got = to_clip(tall, 1)
    head_grads = steps.call(
        functools.partial(place_heads_body, width),
        "place_heads",
        [struct(depth, inner, dtype=F32)] * 3,
        [head, head_got],
    )
    flat = steps.join(flat, flat_got, axis=1)
    flat_got = to_clip(flat, 1)
    tall = steps.join(tall, tall_got, axis=1)
    tall_got = to_clip(tall, 2)
    flat_grads = steps.call(place_flat_body, "place_flat", [struct(low, dim, dtype=F32)] * 2, [flat, flat_got])
    tall_grads = steps.call(place_body, "place_tall", [struct(depth, inner, dtype=F32)] * 3, [tall, tall_got])
    return (
        output.reshape(frames_in.shape),
        frames_grad.reshape(frames_in.shape),
        refer_grad[None],
        *head_grads,
        flat_grads[0],
        *tall_grads,
        flat_grads[1],
    )


def solution(mesh):
    in_specs = (
        P("clip", "frame", None, None),
        P("clip", "frame", None),
        P("clip", "frame", None, None),
        P("frame", None),
        P("frame", None),
        P("frame", None),
        P("frame", None),
        P("frame", None),
        P("frame", None),
        P("frame", None),
        P("frame", None),
    )
    out_specs = (
        P("clip", "frame", None, None),
        P("clip", "frame", None, None),
        P("clip", "frame", None),
        P("frame", None),
        P("frame", None),
        P("frame", None),
        P("frame", None),
        P("frame", None),
        P("frame", None),
        P("frame", None),
        P("frame", None),
    )
    clips = mesh.shape["clip"]
    by_heads = mesh.shape["frame"] == HEADS == 4 and clips == 8
    return jax.shard_map(
        per_device if by_heads else per_device_general, mesh=mesh, in_specs=in_specs, out_specs=out_specs, check_vma=False
    )
```

```python
import math

import functools
import itertools

import jax
import jax.numpy as jnp
from jax import lax
from jax.experimental import pallas as pl
from jax.experimental.pallas import tpu as pltpu
from jax.sharding import PartitionSpec as P

HEADS = 4
F32 = jnp.float32
BF16 = jnp.bfloat16


EPSILON = 1e-05


def layer_stats(rows):
    wide = rows.astype(jnp.float32)
    centre = jnp.mean(wide, -1, keepdims=True)
    offset = wide - centre
    inverse = lax.rsqrt(jnp.mean(offset * offset, -1, keepdims=True) + EPSILON)
    return (offset * inverse, inverse)


def layer_back(centred, inverse, cotangent):
    first = jnp.mean(cotangent, -1, keepdims=True)
    second = jnp.mean(cotangent * centred, -1, keepdims=True)
    return inverse * (cotangent - first - centred * second)


def position_table(first, count, width):
    frame_ids = (first + jnp.arange(count, dtype=jnp.int32)).astype(jnp.float32)
    halves = jnp.arange(width // 2, dtype=jnp.int32).astype(jnp.float32)
    rates = jnp.exp(halves * (-2.0 * math.log(10000.0) / width))
    angles = frame_ids[:, None] * rates[None, :]
    return jnp.stack([jnp.sin(angles), jnp.cos(angles)], -1).reshape(count, width)


def position_rows(frame_ids, width):
    lane = jnp.arange(width, dtype=jnp.int32)
    rates = jnp.exp((lane // 2).astype(F32) * (-2.0 * math.log(10000.0) / width))
    angles = frame_ids.astype(F32)[:, None] * rates[None, :]
    return jnp.where(lane % 2 == 0, jnp.sin(angles), jnp.cos(angles))


def einsum_forms(temporal):
    if temporal:
        return ("qbhe,kbhe->bhqk", "bhqk,kbhe->qbhe", "bhqk,qbhe->kbhe")
    return ("bqhe,bkhe->bhqk", "bhqk,bkhe->bqhe", "bhqk,bqhe->bkhe")


def product(form, left, right):
    return jnp.einsum(form, left, right, preferred_element_type=jnp.float32)


def attention(query, keys, values, temporal):
    score_form, mix_form, back_form = einsum_forms(temporal)
    scores = product(score_form, query, keys) * query.shape[-1] ** (-0.5)
    powers = jnp.exp(scores)
    probs = powers / jnp.sum(powers, -1, keepdims=True)
    rounded = probs.astype(jnp.bfloat16)
    mixed = product(mix_form, rounded, values).astype(jnp.bfloat16)
    return (mixed, probs, rounded)


def attention_back(query, keys, values, probs, rounded, cotangent, temporal):
    score_form, mix_form, back_form = einsum_forms(temporal)
    prob_grad = product(score_form, cotangent, values)
    score_grad = probs * (prob_grad - jnp.sum(probs * prob_grad, -1, keepdims=True))
    score_rounded = (score_grad * query.shape[-1] ** (-0.5)).astype(jnp.bfloat16)
    query_grad = product(mix_form, score_rounded, keys).astype(jnp.bfloat16)
    key_grad = product(back_form, score_rounded, query)
    value_grad = product(back_form, rounded, cotangent)
    return (query_grad, key_grad, value_grad)


def split_heads(rows):
    return rows.reshape(rows.shape[:-1] + (HEADS, rows.shape[-1] // HEADS))


def merge_heads(rows):
    return rows.reshape(rows.shape[:-2] + (rows.shape[-2] * rows.shape[-1],))


def project(rows, weight):
    flat_rows = rows.reshape(-1, rows.shape[-1])
    result = jnp.dot(flat_rows, weight, preferred_element_type=jnp.float32)
    return result.reshape(rows.shape[:-1] + (weight.shape[1],))


def project_back(rows, weight):
    flat_rows = rows.reshape(-1, rows.shape[-1])
    result = lax.dot_general(
        flat_rows, weight, (((1,), (1,)), ((), ())), preferred_element_type=jnp.float32
    )
    return result.reshape(rows.shape[:-1] + (weight.shape[0],))


def outer_sum(left, right):
    left_rows = left.reshape(-1, left.shape[-1])
    right_rows = right.reshape(-1, right.shape[-1])
    return lax.dot_general(
        left_rows, right_rows, (((0,), (0,)), ((), ())), preferred_element_type=jnp.float32
    )


def per_device_general(
    frames_in,
    ref_feats,
    out_grad,
    space_query,
    space_key,
    space_value,
    space_output,
    time_query,
    time_key,
    time_value,
    time_output,
):
    block = lax.axis_index("frame")
    (
        full_space_query,
        full_space_key,
        full_space_value,
        full_space_output,
        full_time_query,
        full_time_key,
        full_time_value,
        full_time_output,
    ) = (
        lax.all_gather(space_query, "frame", axis=0, tiled=True),
        lax.all_gather(space_key, "frame", axis=0, tiled=True),
        lax.all_gather(space_value, "frame", axis=0, tiled=True),
        lax.all_gather(space_output, "frame", axis=0, tiled=True),
        lax.all_gather(time_query, "frame", axis=0, tiled=True),
        lax.all_gather(time_key, "frame", axis=0, tiled=True),
        lax.all_gather(time_value, "frame", axis=0, tiled=True),
        lax.all_gather(time_output, "frame", axis=0, tiled=True),
    )
    frames = frames_in[0]
    refer = ref_feats[0]
    cotangent = out_grad[0]
    frame_count = frames.shape[0]
    token_count = frames.shape[1]
    centred_one, inverse_one = layer_stats(frames)
    normed_one = centred_one.astype(jnp.bfloat16)
    spatial_query = project(normed_one, full_space_query).astype(jnp.bfloat16)
    spatial_key = project(normed_one, full_space_key).astype(jnp.bfloat16)
    spatial_value = project(normed_one, full_space_value).astype(jnp.bfloat16)
    own_key = project(refer, full_space_key).astype(jnp.bfloat16)
    own_value = project(refer, full_space_value).astype(jnp.bfloat16)
    refer_key, refer_value = (
        lax.all_gather(own_key, "frame", axis=0, tiled=True),
        lax.all_gather(own_value, "frame", axis=0, tiled=True),
    )
    keys_joined = jnp.concatenate(
        [spatial_key, jnp.broadcast_to(refer_key[None], spatial_key.shape)], 1
    )
    values_joined = jnp.concatenate(
        [spatial_value, jnp.broadcast_to(refer_value[None], spatial_value.shape)], 1
    )
    spatial_mixed, spatial_probs, spatial_rounded = attention(
        split_heads(spatial_query), split_heads(keys_joined), split_heads(values_joined), False
    )
    spatial_mixed = merge_heads(spatial_mixed)
    hidden_one = (frames.astype(jnp.float32) + project(spatial_mixed, full_space_output)).astype(
        jnp.bfloat16
    )
    centred_two, inverse_two = layer_stats(hidden_one)
    table = position_table(block * frame_count, frame_count, frames.shape[2])
    normed_two = (centred_two + table[:, None, :]).astype(jnp.bfloat16)
    normed_rows = lax.all_to_all(normed_two, "frame", split_axis=1, concat_axis=0, tiled=True)
    temporal_query = project(normed_rows, full_time_query).astype(jnp.bfloat16)
    temporal_key = project(normed_rows, full_time_key).astype(jnp.bfloat16)
    temporal_value = project(normed_rows, full_time_value).astype(jnp.bfloat16)
    temporal_mixed, temporal_probs, temporal_rounded = attention(
        split_heads(temporal_query), split_heads(temporal_key), split_heads(temporal_value), True
    )
    mixed_two = lax.all_to_all(
        merge_heads(temporal_mixed), "frame", split_axis=0, concat_axis=1, tiled=True
    )
    output = (hidden_one.astype(jnp.float32) + project(mixed_two, full_time_output)).astype(
        jnp.bfloat16
    )
    mixed_grad_two = project_back(cotangent, full_time_output).astype(jnp.bfloat16)
    token_grad = lax.all_to_all(mixed_grad_two, "frame", split_axis=1, concat_axis=0, tiled=True)
    token_query_grad, token_key_grad, token_value_grad = attention_back(
        split_heads(temporal_query),
        split_heads(temporal_key),
        split_heads(temporal_value),
        temporal_probs,
        temporal_rounded,
        split_heads(token_grad),
        True,
    )
    query_grad_two, key_grad_two, value_grad_two = (
        lax.all_to_all(
            merge_heads(token_query_grad), "frame", split_axis=0, concat_axis=1, tiled=True
        ),
        lax.all_to_all(
            merge_heads(token_key_grad).astype(jnp.bfloat16),
            "frame",
            split_axis=0,
            concat_axis=1,
            tiled=True,
        ),
        lax.all_to_all(
            merge_heads(token_value_grad).astype(jnp.bfloat16),
            "frame",
            split_axis=0,
            concat_axis=1,
            tiled=True,
        ),
    )
    normed_grad_two = (
        project_back(query_grad_two, full_time_query)
        + project_back(key_grad_two, full_time_key)
        + project_back(value_grad_two, full_time_value)
    )
    hidden_grad = (
        cotangent.astype(jnp.float32) + layer_back(centred_two, inverse_two, normed_grad_two)
    ).astype(jnp.bfloat16)
    mixed_grad_one = project_back(hidden_grad, full_space_output).astype(jnp.bfloat16)
    query_grad_one, key_joined_grad, value_joined_grad = attention_back(
        split_heads(spatial_query),
        split_heads(keys_joined),
        split_heads(values_joined),
        spatial_probs,
        spatial_rounded,
        split_heads(mixed_grad_one),
        False,
    )
    query_grad_one = merge_heads(query_grad_one)
    key_grad_one = merge_heads(key_joined_grad[:, :token_count]).astype(jnp.bfloat16)
    value_grad_one = merge_heads(value_joined_grad[:, :token_count]).astype(jnp.bfloat16)
    partial_key = merge_heads(jnp.sum(key_joined_grad[:, token_count:], 0))
    partial_value = merge_heads(jnp.sum(value_joined_grad[:, token_count:], 0))
    summed_key, summed_value = (
        lax.psum_scatter(
            partial_key.astype(jnp.bfloat16), "frame", scatter_dimension=0, tiled=True
        ).astype(jnp.float32),
        lax.psum_scatter(
            partial_value.astype(jnp.bfloat16), "frame", scatter_dimension=0, tiled=True
        ).astype(jnp.float32),
    )
    refer_key_grad = summed_key.astype(jnp.bfloat16)
    refer_value_grad = summed_value.astype(jnp.bfloat16)
    normed_grad_one = (
        project_back(query_grad_one, full_space_query)
        + project_back(key_grad_one, full_space_key)
        + project_back(value_grad_one, full_space_value)
    )
    frames_grad = (
        hidden_grad.astype(jnp.float32) + layer_back(centred_one, inverse_one, normed_grad_one)
    ).astype(jnp.bfloat16)
    refer_grad = (
        project_back(refer_key_grad, full_space_key)
        + project_back(refer_value_grad, full_space_value)
    ).astype(jnp.bfloat16)
    term_sq = outer_sum(normed_one, query_grad_one)
    term_sk = outer_sum(normed_one, key_grad_one) + outer_sum(refer, refer_key_grad)
    term_sv = outer_sum(normed_one, value_grad_one) + outer_sum(refer, refer_value_grad)
    term_so = outer_sum(spatial_mixed, hidden_grad)
    term_tq = outer_sum(normed_two, query_grad_two)
    term_tk = outer_sum(normed_two, key_grad_two)
    term_tv = outer_sum(normed_two, value_grad_two)
    term_to = outer_sum(mixed_two, cotangent)
    share_sq, share_sk, share_sv, share_so, share_tq, share_tk, share_tv, share_to = (
        lax.psum_scatter(
            term_sq.astype(jnp.bfloat16), "frame", scatter_dimension=0, tiled=True
        ).astype(jnp.float32),
        lax.psum_scatter(
            term_sk.astype(jnp.bfloat16), "frame", scatter_dimension=0, tiled=True
        ).astype(jnp.float32),
        lax.psum_scatter(
            term_sv.astype(jnp.bfloat16), "frame", scatter_dimension=0, tiled=True
        ).astype(jnp.float32),
        lax.psum_scatter(
            term_so.astype(jnp.bfloat16), "frame", scatter_dimension=0, tiled=True
        ).astype(jnp.float32),
        lax.psum_scatter(
            term_tq.astype(jnp.bfloat16), "frame", scatter_dimension=0, tiled=True
        ).astype(jnp.float32),
        lax.psum_scatter(
            term_tk.astype(jnp.bfloat16), "frame", scatter_dimension=0, tiled=True
        ).astype(jnp.float32),
        lax.psum_scatter(
            term_tv.astype(jnp.bfloat16), "frame", scatter_dimension=0, tiled=True
        ).astype(jnp.float32),
        lax.psum_scatter(
            term_to.astype(jnp.bfloat16), "frame", scatter_dimension=0, tiled=True
        ).astype(jnp.float32),
    )
    total_sq, total_sk, total_sv, total_so, total_tq, total_tk, total_tv, total_to = (
        lax.psum(share_sq.astype(jnp.bfloat16), "clip").astype(jnp.float32),
        lax.psum(share_sk.astype(jnp.bfloat16), "clip").astype(jnp.float32),
        lax.psum(share_sv.astype(jnp.bfloat16), "clip").astype(jnp.float32),
        lax.psum(share_so.astype(jnp.bfloat16), "clip").astype(jnp.float32),
        lax.psum(share_tq.astype(jnp.bfloat16), "clip").astype(jnp.float32),
        lax.psum(share_tk.astype(jnp.bfloat16), "clip").astype(jnp.float32),
        lax.psum(share_tv.astype(jnp.bfloat16), "clip").astype(jnp.float32),
        lax.psum(share_to.astype(jnp.bfloat16), "clip").astype(jnp.float32),
    )
    return (
        output[None],
        frames_grad[None],
        refer_grad[None],
        total_sq,
        total_sk,
        total_sv,
        total_so,
        total_tq,
        total_tk,
        total_tv,
        total_to,
    )


CHUNK = 32


def mm(left, right):
    return jnp.dot(left, right, preferred_element_type=F32)


def mm_bt(left, right):
    return lax.dot_general(left, right, (((1,), (1,)), ((), ())), preferred_element_type=F32)


def mm_at(left, right):
    return lax.dot_general(left, right, (((0,), (0,)), ((), ())), preferred_element_type=F32)


def wide_call(body, name, out_shape, scratch, limit_mb, flops, num_in, kept=0, late=()):
    def with_late(idx, *refs):
        body(idx, *refs[: num_in - 1], *refs[num_in - 1 + len(late) :])

    call = pl.pallas_call(
        with_late,
        name=name,
        out_shape=out_shape,
        in_specs=[pl.BlockSpec(memory_space=pltpu.SMEM)]
        + [pl.BlockSpec(memory_space=pltpu.HBM)] * kept
        + [pl.BlockSpec(memory_space=pltpu.VMEM)] * (num_in - 1 - kept)
        + [pl.BlockSpec(memory_space=pl.ANY)] * len(late),
        out_specs=tuple(pl.BlockSpec(memory_space=pltpu.VMEM) for _ in out_shape),
        scratch_shapes=scratch,
        compiler_params=pltpu.CompilerParams(vmem_limit_bytes=limit_mb * 1024 * 1024),
        cost_estimate=pl.CostEstimate(
            flops=max(flops, 1), bytes_accessed=8_000_000 if flops > 1 else 1, transcendentals=0
        ),
    )
    return lambda *operands: call(*operands, *late)


def struct(*shape, dtype=BF16):
    return jax.ShapeDtypeStruct(shape, dtype)


def flip(value, axis, bit):
    size = lax.axis_size(axis)
    return lax.ppermute(value, axis, [(i, i ^ bit) for i in range(size)])


def after(value, *others):
    corners = [o[(slice(0, 1),) * (o.ndim - 2) + (slice(0, 8), slice(0, 128))] for o in others]
    return lax.optimization_barrier((value, *corners))[0]


def load(sources, held, sems):
    copies = [pltpu.make_async_copy(w, h, sems.at[i]) for i, (w, h) in enumerate(zip(sources, held))]
    for copy in copies:
        copy.start()
    return copies


def pack_body(heads, n, per, idx, *refs):
    sources, near, (far, first, grad_own, grad_near, across) = refs[:10], refs[10:12], refs[12:17]
    packs, held, (wide, few, sems) = refs[17], refs[18:28], refs[28:]
    me, side, mine = idx[0], idx[1] & 1, idx[1] & 3
    half = far.shape[1]
    depth, inner = held[0].shape
    low = held[6].shape[0]
    width = inner // heads
    part = depth // 4
    copies = load(sources, held, sems)
    for copy in copies[:3]:
        copy.wait()
    for h in range(heads):
        parts = [held[i][:, h * width : (h + 1) * width] for i in range(3)]
        parts.append(jnp.zeros((depth, packs.shape[2] - 3 * width), BF16))
        packs[h] = jnp.concatenate(parts, 1)
    for r in range(2):
        near[r][...] = packs[me ^ r]
        far[r] = packs[me ^ (r + 2), pl.ds(pl.multiple_of(side * half, half), half), :]
    for copy in copies[3:]:
        copy.wait()
    at = pl.ds(pl.multiple_of(mine * part, part), part)
    for i in range(3):
        first[i * part : (i + 1) * part, :] = held[3 + i][at, :]
    for v in range(4):

        @pl.when(mine == v)
        def _(v=v):
            first[3 * part :, :] = held[6 + (v >> 1)][:, (v & 1) * inner : (v & 1) * inner + inner]

    wide[...] = held[8][...].astype(F32)
    count = few.shape[0]
    share = count // per
    tokens = wide.shape[0] // per
    for r in range(n):
        start = pl.multiple_of((me ^ r) * share, share)
        for j in range(per):
            few[j * share : (j + 1) * share, :] = wide[pl.ds(j * tokens + start, share), :]
        if r == 0:
            grad_own[...] = few[...].astype(BF16)
        elif r == 1:
            grad_near[:count, :] = few[...].astype(BF16)
        else:
            across[(r - 2) * count : (r - 1) * count, :] = few[...].astype(BF16)
    grad_near[count:, :] = held[9][...]
    across[2 * count :, :] = held[9][...]


def spatial_forward_body(n, tokens, width, idx, *refs):
    sources, refs = refs[: 2 * n + 8], refs[2 * n + 8 :]
    x_out, w_out, q_out, k_out, v_out, p_out = refs[:6]
    o_outs, (token_out, tall_out, flat_out) = refs[6 : n + 6], refs[n + 6 : n + 9]
    mixed, turn, few, wide, spread, sems = refs[n + 9 : n + 15]
    held = refs[n + 15 :]
    cut = tall_out.shape[0]
    copies = load(sources, held, sems)
    frames, refer, packs = held[:n], held[n : 2 * n], held[2 * n :]
    near, far = packs[:2], ((packs[2], packs[3]), (packs[4], packs[5]))
    me, side = idx[0], idx[1] & 1
    share = tokens // n
    rows = frames[0].shape[0]
    depth = near[0].shape[0]
    half = depth // 2
    lanes = q_out.shape[1]
    room = w_out.shape[1]
    total = n * rows
    for r in range(n):
        copies[r].wait()

        def norm(i, _, r=r):
            at = pl.multiple_of(i * CHUNK, CHUNK)
            centred, _ = layer_stats(frames[r][pl.ds(at, CHUNK), :])
            x_out[pl.ds(r * rows + at, CHUNK), :] = centred.astype(BF16)
            return 0

        lax.fori_loop(0, rows // CHUNK, norm, 0)
        wide[...] = frames[r][...].astype(F32)
        first = pl.multiple_of(me * share, share)
        for j in range(rows // tokens):
            at = r * (rows // tokens) * share + j * share
            spread[at : at + share, :] = wide[pl.ds(j * tokens + first, share), :]
        copies[n + r].wait()
        few[r * share : (r + 1) * share, :] = refer[r][refer[r].shape[0] - share :, :].astype(F32)
    x_out[total:, :] = few[...].astype(BF16)
    token_out[...] = spread[...].astype(BF16)
    for copy in copies[2 * n :]:
        copy.wait()
    for r in range(2):
        w_out[pl.ds(pl.multiple_of((me ^ r) * depth, depth), depth), :] = near[r][...]
        for k in range(2):
            at = pl.multiple_of((me ^ (r + 2)) * depth + (side ^ k) * half, half)
            w_out[pl.ds(at, half), :] = far[r][k][r]
    second, third = packs[6:8]
    tall_out[...] = third[:cut, :]
    flat_out[...] = second[cut:, :]
    for start, count in [(r * rows, rows) for r in range(n)] + [(total, tokens)]:
        three = mm(x_out[start : start + count, :], w_out[...])
        keep = lax.broadcasted_iota(jnp.int32, (count, lanes), 1) < width
        q_out[start : start + count, :] = jnp.where(keep, three[:, :lanes], 0.0).astype(BF16)
        k_out[start : start + count, :] = jnp.where(
            keep, pltpu.roll(three, room - width, 1)[:, :lanes], 0.0
        ).astype(BF16)
        v_out[start : start + count, :] = jnp.where(
            keep, pltpu.roll(three, room - 2 * width, 1)[:, :lanes], 0.0
        ).astype(BF16)
    scale = width**-0.5
    for b in range(total // tokens):
        at = slice(b * tokens, (b + 1) * tokens)
        keys = jnp.concatenate([k_out[at, :], k_out[total:, :]], 0)
        values = jnp.concatenate([v_out[at, :], v_out[total:, :]], 0)
        powers = jnp.exp(mm_bt(q_out[at, :], keys) * scale)
        probs = powers / jnp.sum(powers, -1, keepdims=True)
        p_out[at, :] = probs
        mixed[at, :] = mm(probs.astype(BF16), values)
    per = rows // tokens
    for r in range(n):
        first = pl.multiple_of((me ^ r) * share, share)
        for b in range(total // tokens):
            to = ((b // per) ^ r) * per + b % per
            turn[to * share : (to + 1) * share, :] = mixed[pl.ds(b * tokens + first, share), :]
        o_outs[r][...] = turn[...].astype(BF16)


def spatial_backward_body(n, tokens, width, idx, *refs):
    grads = refs[:n]
    x_ref, w_ref, q_ref, k_ref, v_ref, p_ref = refs[n : n + 6]
    keep_out, send_out, keep_term, send_term = refs[n + 6 : n + 10]
    spread, turn, packed, term = refs[n + 10 :]
    me = idx[0]
    share = tokens // n
    total = p_ref.shape[0]
    rows = total // n
    lanes = q_ref.shape[1]
    room = w_ref.shape[1]
    per = rows // tokens
    for r in range(n):
        first = pl.multiple_of((me ^ r) * share, share)
        turn[...] = grads[r][...].astype(F32)
        for b in range(total // tokens):
            to = ((b // per) ^ r) * per + b % per
            spread[pl.ds(b * tokens + first, share), :] = turn[to * share : (to + 1) * share, :]
    scale = width**-0.5

    def pack(first, second, third):
        def wide(part):
            blank = jnp.zeros((part.shape[0], room - lanes), F32)
            return jnp.concatenate([part, blank], 1)

        result = pltpu.roll(wide(second), width, 1) + pltpu.roll(wide(third), 2 * width, 1)
        return result if first is None else result + wide(first)

    key_sum = jnp.zeros((k_ref.shape[0] - total, lanes), F32)
    value_sum = key_sum
    for b in range(total // tokens):
        at = slice(b * tokens, (b + 1) * tokens)
        query = q_ref[at, :]
        keys = jnp.concatenate([k_ref[at, :], k_ref[total:, :]], 0)
        values = jnp.concatenate([v_ref[at, :], v_ref[total:, :]], 0)
        cotangent = spread[at, :].astype(BF16)
        probs = p_ref[at, :]
        back = mm_bt(cotangent, values)
        score = (probs * (back - jnp.sum(probs * back, -1, keepdims=True)) * scale).astype(BF16)
        query_grad = mm(score, keys)
        key_grad = mm_at(score, query)
        value_grad = mm_at(probs.astype(BF16), cotangent)
        key_sum = key_sum + key_grad[tokens:]
        value_sum = value_sum + value_grad[tokens:]
        packed[at, :] = pack(query_grad, key_grad[:tokens], value_grad[:tokens]).astype(BF16)
    packed[total:, :] = pack(None, key_sum, value_sum).astype(BF16)
    for r in range(n):
        part = mm_bt(packed[r * rows : (r + 1) * rows, :], w_ref[...]).astype(BF16)
        (send_out if r & 1 else keep_out)[r >> 1, :rows, :] = part
    part = mm_bt(packed[total:, :], w_ref[...])
    for r in range(n):
        few = part[r * share : (r + 1) * share].astype(BF16)
        (send_out if r & 1 else keep_out)[r >> 1, rows:, :] = few
    depth = x_ref.shape[1] // 5
    for j in range(5):
        at = slice(j * depth, (j + 1) * depth)
        term[at, :] = mm_at(x_ref[:, at], packed[...])
    side = idx[1] & 1
    count, piece = keep_term.shape[0], keep_term.shape[2]
    for j in range(n):
        for k in range(count):
            for out, half in ((keep_term, side), (send_term, 1 - side)):
                at = pl.multiple_of((j * 2 * count + half * count + k) * piece, piece)
                out[k, j] = term[pl.ds(at, piece), :].astype(BF16)


def parts_of(ref, dim, inner):
    starts = [0, dim, 2 * dim] + [3 * dim + i * inner for i in range(4)]
    parts = [ref.at[:, a : a + (dim if i < 3 else inner)] for i, a in enumerate(starts)]
    first, lanes = 3 * dim + 4 * inner, (ref.shape[1] - 3 * dim - 4 * inner) // 2
    return parts + [ref.at[:, first + i * lanes : first + (i + 1) * lanes] for i in range(2)]


def temporal_body(n, heads, per, idx, *refs):
    mixed_in, near, far, refs = refs[:n], (refs[n : n + 5], refs[n + 5 : n + 10]), refs[n + 10 :][:10], refs[n + 20 :]
    far = (far[:5], far[5:])
    frames_in, cotangents, table_in, refs = refs[0], refs[1 : n + 1], refs[n + 1], refs[n + 2 :]
    grad_outs, back_outs, kept, refs = refs[:n], refs[n : 2 * n], refs[2 * n], refs[2 * n + 1 :]
    so, tq, tk, tv, to, hidden, centred, inverse, wide, qs, gos = refs[:11]
    mixed, frames, table, sems = refs[11 : n + 11], *refs[n + 11 :]
    me, quarter = idx[0], idx[1] & 3
    rows, dim = frames.shape
    inner = tq.shape[1]
    width = inner // heads
    depth, low = dim // n, inner // n
    part = depth // 4
    few = rows // n
    share = few // per
    gh_out, n2_out, cotangent, gq_out, gk_out, gv_out, o2_out, *o_outs = parts_of(kept, dim, inner)
    first, second, chosen = [], [], []

    def bring(source, to_ref, group):
        group.append(pltpu.make_async_copy(source, to_ref, sems.at[len(first) + len(second) + len(chosen)]))

    def low_rows(r):
        return pl.ds(pl.multiple_of((me ^ r) * low, low), low)

    for r in range(n):
        bring(mixed_in[r], mixed[r], first)
        if r < 2:
            bring(near[r][3], so.at[r, pl.ds(0, low), :], first)
    bring(frames_in, frames, first)
    bring(table_in, table, first)
    for r in range(2, n):
        for s in range(4):
            flat, start = (far[r - 2][s], 3 * part) if s < 3 else (far[r - 2][4], 0)
            place = len(first) + len(second) + len(chosen)
            cases = []
            for v in range(4):
                lanes = pl.ds((v & 1) * inner, inner)
                target = so.at[r, pl.ds(0, low), lanes] if v < 2 else to.at[low_rows(r), lanes]
                source = flat.at[pl.ds(start, low), :]
                cases.append((v, pltpu.make_async_copy(source, target, sems.at[place])))
            chosen.append((quarter ^ s, cases))
    for r in range(n):
        if r < 2:
            bring(near[r][4], to.at[low_rows(r), :], second)
        for i, whole in enumerate((tq, tk, tv)):
            if r < 2:
                at = pl.ds(pl.multiple_of((me ^ r) * depth, depth), depth)
                bring(near[r][i], whole.at[at, :], second)
                continue
            for s in range(4):
                at = pl.ds(pl.multiple_of((me ^ r) * depth + (quarter ^ s) * part, part), part)
                bring(far[r - 2][s].at[pl.ds(i * part, part), :], whole.at[at, :], second)
        source = cotangents[r].at[pl.ds(few if r == 3 else 0, few), :]
        bring(source, cotangent.at[pl.ds(r * few, few), :], second)

    def choose(act):
        for which, cases in chosen:
            for v, copy in cases:

                @pl.when(which == v)
                def _(copy=copy):
                    act(copy)

    for copy in first:
        copy.start()
    choose(lambda copy: copy.start())
    for copy in second:
        copy.start()
    so[:, low:, :] = jnp.zeros((n, so.shape[1] - low, dim), BF16)
    for copy in first:
        copy.wait()
    choose(lambda copy: copy.wait())
    for i in range(2):
        o_outs[i][...] = mixed[2 * i + 1][...]
    step = dim // 5
    for j in range(5):
        at = slice(j * step, (j + 1) * step)
        acc = frames[:, at].astype(F32)
        for r in range(n):
            acc = acc + mm(mixed[r][...], so[r, :, at])
        hidden[:, at] = acc.astype(BF16).astype(F32)

    def norm(i, _):
        at = pl.ds(pl.multiple_of(i * share, share), share)
        offset, scale = layer_stats(hidden[at, :])
        centred[at, :] = offset
        inverse[at, :] = jnp.broadcast_to(scale, (share, inverse.shape[1]))
        wide[at, :] = offset + table[pl.ds(i, 1), :]
        return 0

    lax.fori_loop(0, rows // share, norm, 0)
    n2_out[...] = wide[...].astype(BF16)
    for copy in second:
        copy.wait()

    def token(axis):
        place = lax.broadcasted_iota(jnp.int32, (rows, rows), axis).astype(F32)
        return place - share * jnp.floor((place + 0.5) * (1.0 / share))

    same = token(0) == token(1)
    lane_head = lax.broadcasted_iota(jnp.int32, (rows, inner), 1)

    def own(h, value):
        inside = (lane_head >= h * width) & (lane_head < (h + 1) * width)
        return jnp.where(inside, value, 0.0)

    scale = width**-0.5
    query = mm(n2_out[...], tq[...])
    for h in range(heads):
        qs[h * rows : (h + 1) * rows, :] = own(h, query).astype(BF16)
    keys = mm(n2_out[...], tk[...]).astype(BF16)
    values = mm(n2_out[...], tv[...]).astype(BF16)
    mixed_grad = mm_bt(cotangent[...], to[...])
    for h in range(heads):
        gos[h * rows : (h + 1) * rows, :] = own(h, mixed_grad).astype(BF16)
    key_grad = jnp.zeros((rows, inner), F32)
    value_grad = jnp.zeros((rows, inner), F32)
    query_grad = jnp.zeros((rows, inner), F32)
    o2 = jnp.zeros((rows, inner), F32)
    for h in range(heads):
        at = slice(h * rows, (h + 1) * rows)
        scores = mm_bt(qs[at, :], keys) * scale
        powers = jnp.where(same, jnp.exp(scores), 0.0)
        probs = powers / jnp.sum(powers, -1, keepdims=True)
        rounded = probs.astype(BF16)
        o2 = o2 + own(h, mm(rounded, values))
        back = mm_bt(gos[at, :], values)
        score = (probs * (back - jnp.sum(probs * back, -1, keepdims=True)) * scale).astype(BF16)
        query_grad = query_grad + own(h, mm(score, keys))
        key_grad = key_grad + mm_at(score, qs[at, :])
        value_grad = value_grad + mm_at(rounded, gos[at, :])
    o2_out[...] = o2.astype(BF16)
    gq_out[...] = query_grad.astype(BF16)
    gk_out[...] = key_grad.astype(BF16)
    gv_out[...] = value_grad.astype(BF16)
    for j in range(5):
        at = slice(j * step, (j + 1) * step)
        wide[:, at] = (
            mm_bt(gq_out[...], tq[at, :]) + mm_bt(gk_out[...], tk[at, :]) + mm_bt(gv_out[...], tv[at, :])
        )

    def back_norm(i, _):
        at = pl.ds(pl.multiple_of(i * CHUNK, CHUNK), CHUNK)
        back = layer_back(centred[at, :], inverse[at, :1], wide[at, :])
        gh_out[at, :] = (cotangent[at, :].astype(F32) + back).astype(BF16)
        return 0

    lax.fori_loop(0, rows // CHUNK, back_norm, 0)
    for r in range(n):
        grad_outs[r][...] = mm_bt(gh_out[...], so[r]).astype(BF16)
    for j in range(5):
        at = slice(j * step, (j + 1) * step)
        part = (hidden[:, at] + mm(o2_out[...], to[:, at])).astype(BF16)
        for r in range(n):
            back_outs[r][:few, at] = part[r * few : (r + 1) * few]
    for r in range(n):
        back_outs[r][few:, :] = gh_out[r * few : (r + 1) * few, :]


def terms_body(n, idx, *refs):
    held, refs = refs[:4], refs[4:]
    tall_keep, tall_send, flat_keep, flat_send = refs[:4]
    n2_turned, o2_turned, tall, so = refs[4:]
    me, bit = idx[0], (idx[1] >> 1) & 1
    rows = held[0].shape[0]
    depth, inner = tall.shape
    dim, low = depth * n, inner // n
    pieces, _, piece = tall_keep.shape[:3]
    both = [parts_of(ref, dim, inner) for ref in held[:2]]
    for i in range(2):
        n2_turned[:, i * rows : (i + 1) * rows] = both[i][1][...].T
        o2_turned[:, i * rows : (i + 1) * rows] = both[i][6][...].T
    ours, theirs = both
    mixed = [*held[2:], *theirs[7:]]
    for i in range(3):
        grad = jnp.concatenate([ours[3 + i][...], theirs[3 + i][...]], 0)
        for k, out in enumerate((tall_keep, tall_send)):
            at = pl.multiple_of((me ^ (2 * k)) * depth, depth)
            tall[...] = mm(n2_turned[pl.ds(at, depth), :], grad)
            for p in range(pieces):
                out[p, i] = tall[p * piece : (p + 1) * piece, :].astype(BF16)
    half = low // 2
    for k in range(2):
        so[0] = (mm_at(mixed[k][...], ours[0][...]) + mm_at(mixed[2 + k][...], theirs[0][...]))[:low]
        at = pl.multiple_of((me ^ (2 * k)) * low, low)
        grad = jnp.concatenate([ours[2][...], theirs[2][...]], 0)
        so[1] = mm(o2_turned[pl.ds(at, low), :], grad)
        for i in range(2):
            for j in range(2):
                for out, part in ((flat_keep, bit), (flat_send, 1 - bit)):
                    at = pl.multiple_of(part * half, half)
                    out[k, i, j] = so[i, pl.ds(at, half), j * inner : (j + 1) * inner].astype(BF16)


def finish_body(n, per, idx, frames, *refs):
    parts, near, far = refs[:n], refs[n], refs[n + 1]
    out, frames_grad, refer_grad, turn, wide = refs[n + 2 :]
    me = idx[0]
    rows, few = frames.shape[0], parts[0].shape[0] // 2
    share, tokens = few // per, rows // per
    for r in range(n):
        first = pl.multiple_of((me ^ r) * share, share)
        turn[...] = parts[r][...].astype(F32)
        for which in range(2):
            for j in range(per):
                at = which * few + j * share
                wide[which, pl.ds(j * tokens + first, share), :] = turn[at : at + share, :]
    out[...] = wide[0].astype(BF16)

    def step(i, _):
        at = pl.ds(pl.multiple_of(i * CHUNK, CHUNK), CHUNK)
        centred, inverse = layer_stats(frames[at, :])
        grad = near[at, :].astype(F32) + far[at, :].astype(F32)
        back = layer_back(centred, inverse, grad)
        frames_grad[at, :] = (wide[1, at, :] + back).astype(BF16)
        return 0

    lax.fori_loop(0, rows // CHUNK, step, 0)
    refer_grad[...] = (near[rows:, :].astype(F32) + far[rows:, :].astype(F32)).astype(BF16)


def place_body(idx, near, far, *outs):
    side, low_bit = idx[1] & 1, (idx[1] >> 1) & 1
    piece = near.shape[3]
    for low, source in enumerate((near, far)):
        for high, other in itertools.product(range(2), range(2)):
            place = (side ^ other) * 4 + 2 * high + (low_bit ^ low)
            at = pl.multiple_of(place * piece, piece)
            for i, out in enumerate(outs):
                out[pl.ds(at, piece), :] = source[high, other, i].astype(F32)


def place_heads_body(width, idx, near, far, *outs):
    me, side, low_bit = idx[0], idx[1] & 1, (idx[1] >> 1) & 1
    _, _, n, piece, _ = near.shape
    for low, source in enumerate((near, far)):
        for high, other in itertools.product(range(2), range(2)):
            place = (side ^ other) * 4 + 2 * high + (low_bit ^ low)
            at = pl.multiple_of(place * piece, piece)
            heads = [source[high, other, me ^ h].astype(F32) for h in range(n)]
            for i, out in enumerate(outs):
                parts = [h[:, i * width : (i + 1) * width] for h in heads]
                out[pl.ds(at, piece), :] = jnp.concatenate(parts, 1)


def place_flat_body(idx, near, far, *outs):
    side, low_bit = idx[1] & 1, (idx[1] >> 1) & 1
    piece, inner = near.shape[2:]
    for source, half in ((near, side), (far, 1 - side)):
        for high, low in itertools.product(range(2), range(2)):
            at = pl.multiple_of((low_bit ^ low) * piece, piece)
            for i, out in enumerate(outs):

                @pl.when(half == i)
                def _(source=source, high=high, low=low, at=at, out=out):
                    lanes = slice(high * inner, (high + 1) * inner)
                    out[pl.ds(at, piece), lanes] = source[high, low].astype(F32)


def merge_body(axis, place, spread, idx, kept, moved, *outs):
    shape = kept.shape
    bit = None if axis is None else (idx[1] >> place) & 1
    for at in itertools.product(*map(range, shape[:-2])):
        if axis is not None:
            if at[axis]:
                continue
            rest = at[:axis] + at[axis + 1 :]
            for out, half in ((outs[0], bit), (outs[1], 1 - bit)):
                here = at[:axis] + (half,) + at[axis + 1 :]
                out[rest] = (kept[here].astype(F32) + moved[here].astype(F32)).astype(BF16)
        elif spread:
            here = (at[0], idx[0] ^ at[1])
            outs[at[1]][at[0]] = (kept[here].astype(F32) + moved[here].astype(F32)).astype(BF16)
        else:
            outs[0][at] = (kept[at].astype(F32) + moved[at].astype(F32)).astype(BF16)


def join_body(axis, idx, *refs):
    out = refs[-1]
    for i, part in enumerate(refs[:-1]):
        for at in itertools.product(*map(range, part.shape[:-2])):
            out[at[:axis] + (i,) + at[axis:]] = part[at]


def pick(value, index, axis=0):
    return lax.dynamic_index_in_dim(value, index, axis, keepdims=False)


class Steps:
    def __init__(self, idx):
        self.idx, self.last = idx, ()

    def call(self, body, name, out_shape, operands, scratch=(), limit_mb=12):
        def marked(idx, *refs):
            ends = len(operands) + len(out_shape)
            body(idx, *refs[:ends], *refs[ends + 1 :])
            refs[ends][...] = jnp.zeros(refs[ends].shape, F32)

        *outs, mark = wide_call(
            marked,
            name,
            list(out_shape) + [struct(8, 128, dtype=F32)],
            list(scratch),
            limit_mb,
            0,
            len(operands) + 1,
            0,
            self.last,
        )(self.idx, *operands)
        self.last = (mark,)
        return outs

    def merge(self, kept, moved, axis=None, place=0, spread=False):
        shape = kept.shape
        if axis is not None:
            shapes = [shape[:axis] + shape[axis + 1 :]] * 2
        else:
            shapes = [shape[:1] + shape[2:]] * shape[1] if spread else [shape]
        body = functools.partial(merge_body, axis, place, spread)
        outs = self.call(body, "merge", [struct(*one) for one in shapes], [kept, moved])
        return outs if len(outs) > 1 else outs[0]

    def join(self, *parts, axis=0):
        shape = parts[0].shape
        shape = shape[:axis] + (len(parts),) + shape[axis:]
        return self.call(functools.partial(join_body, axis), "join", [struct(*shape)], parts)[0]


def per_device(
    frames_in,
    ref_feats,
    out_grad,
    space_query,
    space_key,
    space_value,
    space_output,
    time_query,
    time_key,
    time_value,
    time_output,
):
    n = lax.axis_size("frame")
    clips = lax.axis_size("clip")
    me = lax.axis_index("frame")
    clip = lax.axis_index("clip")
    side, level = clip & 1, clip >> 1
    idx = jnp.stack([me, clip]).astype(jnp.int32)
    _, per, tokens, dim = frames_in.shape
    inner = space_query.shape[1]
    width = inner // HEADS
    lanes = -(-width // 128) * 128
    room = -(-3 * width // 128) * 128
    depth, low = dim // n, inner // n
    rows = per * tokens
    total = n * rows
    share = tokens // n
    few = per * share
    token_rows = n * few
    count, piece = clips // 2, depth // clips
    frames = frames_in.reshape(rows, dim)
    steps = Steps(idx)

    def exchange(parts):
        return [parts[0]] + [flip(parts[r], "frame", r) for r in range(1, n)]

    def gather(value):
        far = flip(value, "frame", 2)
        return [value, flip(value, "frame", 1), far, flip(far, "frame", 1)]

    others = (time_query, time_key, time_value, space_output, time_output)
    own, near, far_pack, first, grad_own, grad_near, across = wide_call(
        functools.partial(pack_body, HEADS, n, per),
        "pack_heads",
        [
            struct(depth, room),
            struct(depth, room),
            struct(2, depth // 2, room),
            struct(3 * depth // 4 + low, inner),
            struct(few, dim),
            struct(few + share, dim),
            struct(2 * few + share, dim),
        ],
        [pltpu.VMEM((HEADS, depth, room), BF16)]
        + [pltpu.VMEM((depth, inner), BF16)] * 6
        + [pltpu.VMEM((low, dim), BF16)] * 2
        + [
            pltpu.VMEM((rows, dim), BF16),
            pltpu.VMEM((share, dim), BF16),
            pltpu.VMEM((rows, dim), F32),
            pltpu.VMEM((few, dim), F32),
            pltpu.SemaphoreType.DMA((10,)),
        ],
        60,
        0,
        11,
        10,
    )(idx, space_query, space_key, space_value, *others, out_grad.reshape(rows, dim), ref_feats[0])
    first = flip(first, "frame", 2)
    far_pack = flip(far_pack, "frame", 2)
    far_frames = flip(after(frames, far_pack), "frame", 2)
    across = flip(after(across, far_pack), "frame", 2)
    side_pack = flip(far_pack, "clip", 1)
    second, third = flip(first, "clip", 1), flip(first, "clip", 2)
    near, grad_near, near_frames = (flip(v, "frame", 1) for v in (near, grad_near, frames))
    packs = [own, near, far_pack, side_pack, flip(far_pack, "frame", 1), flip(side_pack, "frame", 1)]
    all_frames = [frames, near_frames, far_frames, flip(far_frames, "frame", 1)]
    across_near = flip(across, "frame", 1)
    all_refer = [ref_feats[0], grad_near, across, across_near]
    token_grad = [grad_own, grad_near, across, across_near]
    far = [first, second, third]
    far_near = [flip(p, "frame", 1) for p in far]
    others_near = [flip(p, "frame", 1) for p in others]
    frame_ids = jnp.concatenate([(me ^ r) * per + jnp.arange(per) for r in range(n)])
    table = position_rows(frame_ids, dim)

    cut = 3 * depth // 4
    x_all, w_all, q_all, k_all, v_all, probs, *mixed, token_frames, tall_part, flat_part = wide_call(
        functools.partial(spatial_forward_body, n, tokens, width),
        "spatial_forward",
        [
            struct(total + tokens, dim),
            struct(dim, room),
            struct(total + tokens, lanes),
            struct(total + tokens, lanes),
            struct(total + tokens, lanes),
            struct(total, 2 * tokens, dtype=F32),
            *[struct(token_rows, lanes)] * n,
            struct(token_rows, dim),
            struct(cut, inner),
            struct(low, inner),
        ],
        [
            pltpu.VMEM((total, lanes), F32),
            pltpu.VMEM((token_rows, lanes), F32),
            pltpu.VMEM((tokens, dim), F32),
            pltpu.VMEM((rows, dim), F32),
            pltpu.VMEM((token_rows, dim), F32),
            pltpu.SemaphoreType.DMA((2 * n + 8,)),
        ]
        + [pltpu.VMEM((rows, dim), BF16)] * n
        + [pltpu.VMEM(one.shape, BF16) for one in all_refer]
        + [pltpu.VMEM((depth, room), BF16)] * 2
        + [pltpu.VMEM((2, depth // 2, room), BF16)] * 4
        + [pltpu.VMEM((cut + low, inner), BF16)] * 2,
        60,
        2_000_000_000,
        2 * n + 9,
        2 * n + 8,
        (*far_near, *others_near),
    )(idx, *all_frames, *all_refer, *packs, second, third)
    mixed = exchange(mixed)
    fourth = [flip(tall_part, "clip", 1), flip(flat_part, "clip", 2)]
    fourth_near = [flip(p, "frame", 1) for p in fourth]
    blocks = [*others, *others_near, *far, *fourth, *far_near, *fourth_near]
    outs = wide_call(
        functools.partial(temporal_body, n, HEADS, per),
        "temporal",
        [struct(token_rows, lanes)] * n
        + [struct(2 * few, dim)] * n
        + [struct(token_rows, 3 * dim + 4 * inner + 2 * lanes)],
        [
            pltpu.VMEM((n, lanes, dim), BF16),
            pltpu.VMEM((dim, inner), BF16),
            pltpu.VMEM((dim, inner), BF16),
            pltpu.VMEM((dim, inner), BF16),
            pltpu.VMEM((inner, dim), BF16),
            pltpu.VMEM((token_rows, dim), F32),
            pltpu.VMEM((token_rows, dim), F32),
            pltpu.VMEM((token_rows, 128), F32),
            pltpu.VMEM((token_rows, dim), F32),
            pltpu.VMEM((HEADS * token_rows, inner), BF16),
            pltpu.VMEM((HEADS * token_rows, inner), BF16),
        ]
        + [pltpu.VMEM((token_rows, lanes), BF16)] * n
        + [
            pltpu.VMEM((token_rows, dim), BF16),
            pltpu.VMEM(table.shape, F32),
            pltpu.SemaphoreType.DMA((60,)),
        ],
        60,
        5_000_000_000,
        2 * n + 23,
        2 * n + 22,
    )(idx, *mixed, *blocks, token_frames, *token_grad, table)
    mixed_grads = exchange(list(outs[:n]))
    backs = outs[n : 2 * n]

    ours = outs[2 * n]
    keep_tall, send_tall, keep_flat, send_flat = wide_call(
        functools.partial(terms_body, n),
        "temporal_terms",
        [struct(clips, 3, piece, inner)] * 2 + [struct(2, 2, 2, low // 2, inner)] * 2,
        [
            pltpu.VMEM((dim, 2 * token_rows), BF16),
            pltpu.VMEM((inner, 2 * token_rows), BF16),
            pltpu.VMEM((depth, inner), F32),
            pltpu.VMEM((2, low, dim), F32),
        ],
        18,
        1,
        5,
        0,
        tuple(mixed_grads[1:]),
    )(idx, ours, flip(ours, "frame", 1), mixed[0], mixed[2])
    flat_a = flip(send_flat, "clip", 2)
    tall_y = flip(send_tall, "frame", 2)

    keep_out, send_out, keep_term, send_term = wide_call(
        functools.partial(spatial_backward_body, n, tokens, width),
        "spatial_backward",
        [struct(n // 2, rows + share, dim)] * 2 + [struct(count, n, piece, room)] * 2,
        [
            pltpu.VMEM((total, lanes), F32),
            pltpu.VMEM((token_rows, lanes), F32),
            pltpu.VMEM((total + tokens, room), BF16),
            pltpu.VMEM((dim, room), F32),
        ],
        20,
        1,
        n + 7,
        0,
        (send_flat, send_tall),
    )(idx, *mixed_grads, x_all, w_all, q_all, k_all, v_all, probs)

    def to_clip(value, bit):
        return flip(value, "clip", bit)

    head_got = to_clip(send_term, 1)
    out_got = flip(send_out, "frame", 1)
    flat, flat_out = steps.merge(keep_flat, flat_a, 0, 7)
    halves = (2, 2, 2, 3, piece, inner)
    tall, tall_out = steps.merge(keep_tall.reshape(halves), tall_y.reshape(halves), 0, 0)
    tall_got = to_clip(tall_out, 1)
    flat_got = flip(flat_out, "frame", 2)
    halves = (2, 2, n, piece, room)
    head, head_out = steps.merge(keep_term.reshape(halves), head_got.reshape(halves), 1, 1)
    head_got = to_clip(head_out, 2)
    partial, partial_out = steps.merge(keep_out, out_got, 0, 7)
    head = steps.merge(head, head_got)
    head_got = to_clip(head, 4)
    flat, flat_out = steps.merge(flat, flat_got, 0, 0)
    flat_got = to_clip(flat_out, 1)
    tall, tall_out = steps.merge(tall, tall_got, 1, 1)
    tall_got = to_clip(tall_out, 2)
    head_f = exchange(steps.merge(head, head_got, spread=True))
    flat = steps.merge(flat, flat_got)
    flat_got = to_clip(flat, 4)
    tall = steps.merge(tall, tall_got)
    tall_got = to_clip(tall, 4)
    head = steps.join(*head_f, axis=1)
    head_got = to_clip(head, 1)
    backs = exchange(list(backs))
    partial_got = flip(partial_out, "frame", 2)
    head = steps.join(head, head_got, axis=1)
    head_got = to_clip(head, 2)
    flat = steps.merge(flat, flat_got)
    flat_got = to_clip(flat, 2)
    output, frames_grad, refer_grad = steps.call(
        functools.partial(finish_body, n, per),
        "finish",
        [struct(rows, dim)] * 2 + [struct(share, dim)],
        [frames, *backs, partial, partial_got],
        [pltpu.VMEM((2 * few, dim), F32), pltpu.VMEM((2, rows, dim), F32)],
    )
    tall = steps.merge(tall, tall_got)
    tall_got = to_clip(tall, 1)
    head_grads = steps.call(
        functools.partial(place_heads_body, width),
        "place_heads",
        [struct(depth, inner, dtype=F32)] * 3,
        [head, head_got],
    )
    flat = steps.join(flat, flat_got, axis=1)
    flat_got = to_clip(flat, 1)
    tall = steps.join(tall, tall_got, axis=1)
    tall_got = to_clip(tall, 2)
    flat_grads = steps.call(place_flat_body, "place_flat", [struct(low, dim, dtype=F32)] * 2, [flat, flat_got])
    tall_grads = steps.call(place_body, "place_tall", [struct(depth, inner, dtype=F32)] * 3, [tall, tall_got])
    return (
        output.reshape(frames_in.shape),
        frames_grad.reshape(frames_in.shape),
        refer_grad[None],
        *head_grads,
        flat_grads[0],
        *tall_grads,
        flat_grads[1],
    )


def solution(mesh):
    in_specs = (
        P("clip", "frame", None, None),
        P("clip", "frame", None),
        P("clip", "frame", None, None),
        P("frame", None),
        P("frame", None),
        P("frame", None),
        P("frame", None),
        P("frame", None),
        P("frame", None),
        P("frame", None),
        P("frame", None),
    )
    out_specs = (
        P("clip", "frame", None, None),
        P("clip", "frame", None, None),
        P("clip", "frame", None),
        P("frame", None),
        P("frame", None),
        P("frame", None),
        P("frame", None),
        P("frame", None),
        P("frame", None),
        P("frame", None),
        P("frame", None),
    )
    clips = mesh.shape["clip"]
    by_heads = mesh.shape["frame"] == HEADS == 4 and clips == 8
    return jax.shard_map(
        per_device if by_heads else per_device_general, mesh=mesh, in_specs=in_specs, out_specs=out_specs, check_vma=False
    )
```

```python
import math

import functools
import itertools

import jax
import jax.numpy as jnp
from jax import lax
from jax.experimental import pallas as pl
from jax.experimental.pallas import tpu as pltpu
from jax.sharding import PartitionSpec as P

HEADS = 4
F32 = jnp.float32
BF16 = jnp.bfloat16


EPSILON = 1e-05


def layer_stats(rows):
    wide = rows.astype(jnp.float32)
    centre = jnp.mean(wide, -1, keepdims=True)
    offset = wide - centre
    inverse = lax.rsqrt(jnp.mean(offset * offset, -1, keepdims=True) + EPSILON)
    return (offset * inverse, inverse)


def layer_back(centred, inverse, cotangent):
    first = jnp.mean(cotangent, -1, keepdims=True)
    second = jnp.mean(cotangent * centred, -1, keepdims=True)
    return inverse * (cotangent - first - centred * second)


def position_table(first, count, width):
    frame_ids = (first + jnp.arange(count, dtype=jnp.int32)).astype(jnp.float32)
    halves = jnp.arange(width // 2, dtype=jnp.int32).astype(jnp.float32)
    rates = jnp.exp(halves * (-2.0 * math.log(10000.0) / width))
    angles = frame_ids[:, None] * rates[None, :]
    return jnp.stack([jnp.sin(angles), jnp.cos(angles)], -1).reshape(count, width)


def position_rows(frame_ids, width):
    lane = jnp.arange(width, dtype=jnp.int32)
    rates = jnp.exp((lane // 2).astype(F32) * (-2.0 * math.log(10000.0) / width))
    angles = frame_ids.astype(F32)[:, None] * rates[None, :]
    return jnp.where(lane % 2 == 0, jnp.sin(angles), jnp.cos(angles))


def einsum_forms(temporal):
    if temporal:
        return ("qbhe,kbhe->bhqk", "bhqk,kbhe->qbhe", "bhqk,qbhe->kbhe")
    return ("bqhe,bkhe->bhqk", "bhqk,bkhe->bqhe", "bhqk,bqhe->bkhe")


def product(form, left, right):
    return jnp.einsum(form, left, right, preferred_element_type=jnp.float32)


def attention(query, keys, values, temporal):
    score_form, mix_form, back_form = einsum_forms(temporal)
    scores = product(score_form, query, keys) * query.shape[-1] ** (-0.5)
    powers = jnp.exp(scores)
    probs = powers / jnp.sum(powers, -1, keepdims=True)
    rounded = probs.astype(jnp.bfloat16)
    mixed = product(mix_form, rounded, values).astype(jnp.bfloat16)
    return (mixed, probs, rounded)


def attention_back(query, keys, values, probs, rounded, cotangent, temporal):
    score_form, mix_form, back_form = einsum_forms(temporal)
    prob_grad = product(score_form, cotangent, values)
    score_grad = probs * (prob_grad - jnp.sum(probs * prob_grad, -1, keepdims=True))
    score_rounded = (score_grad * query.shape[-1] ** (-0.5)).astype(jnp.bfloat16)
    query_grad = product(mix_form, score_rounded, keys).astype(jnp.bfloat16)
    key_grad = product(back_form, score_rounded, query)
    value_grad = product(back_form, rounded, cotangent)
    return (query_grad, key_grad, value_grad)


def split_heads(rows):
    return rows.reshape(rows.shape[:-1] + (HEADS, rows.shape[-1] // HEADS))


def merge_heads(rows):
    return rows.reshape(rows.shape[:-2] + (rows.shape[-2] * rows.shape[-1],))


def project(rows, weight):
    flat_rows = rows.reshape(-1, rows.shape[-1])
    result = jnp.dot(flat_rows, weight, preferred_element_type=jnp.float32)
    return result.reshape(rows.shape[:-1] + (weight.shape[1],))


def project_back(rows, weight):
    flat_rows = rows.reshape(-1, rows.shape[-1])
    result = lax.dot_general(
        flat_rows, weight, (((1,), (1,)), ((), ())), preferred_element_type=jnp.float32
    )
    return result.reshape(rows.shape[:-1] + (weight.shape[0],))


def outer_sum(left, right):
    left_rows = left.reshape(-1, left.shape[-1])
    right_rows = right.reshape(-1, right.shape[-1])
    return lax.dot_general(
        left_rows, right_rows, (((0,), (0,)), ((), ())), preferred_element_type=jnp.float32
    )


def per_device_general(
    frames_in,
    ref_feats,
    out_grad,
    space_query,
    space_key,
    space_value,
    space_output,
    time_query,
    time_key,
    time_value,
    time_output,
):
    block = lax.axis_index("frame")
    (
        full_space_query,
        full_space_key,
        full_space_value,
        full_space_output,
        full_time_query,
        full_time_key,
        full_time_value,
        full_time_output,
    ) = (
        lax.all_gather(space_query, "frame", axis=0, tiled=True),
        lax.all_gather(space_key, "frame", axis=0, tiled=True),
        lax.all_gather(space_value, "frame", axis=0, tiled=True),
        lax.all_gather(space_output, "frame", axis=0, tiled=True),
        lax.all_gather(time_query, "frame", axis=0, tiled=True),
        lax.all_gather(time_key, "frame", axis=0, tiled=True),
        lax.all_gather(time_value, "frame", axis=0, tiled=True),
        lax.all_gather(time_output, "frame", axis=0, tiled=True),
    )
    frames = frames_in[0]
    refer = ref_feats[0]
    cotangent = out_grad[0]
    frame_count = frames.shape[0]
    token_count = frames.shape[1]
    centred_one, inverse_one = layer_stats(frames)
    normed_one = centred_one.astype(jnp.bfloat16)
    spatial_query = project(normed_one, full_space_query).astype(jnp.bfloat16)
    spatial_key = project(normed_one, full_space_key).astype(jnp.bfloat16)
    spatial_value = project(normed_one, full_space_value).astype(jnp.bfloat16)
    own_key = project(refer, full_space_key).astype(jnp.bfloat16)
    own_value = project(refer, full_space_value).astype(jnp.bfloat16)
    refer_key, refer_value = (
        lax.all_gather(own_key, "frame", axis=0, tiled=True),
        lax.all_gather(own_value, "frame", axis=0, tiled=True),
    )
    keys_joined = jnp.concatenate(
        [spatial_key, jnp.broadcast_to(refer_key[None], spatial_key.shape)], 1
    )
    values_joined = jnp.concatenate(
        [spatial_value, jnp.broadcast_to(refer_value[None], spatial_value.shape)], 1
    )
    spatial_mixed, spatial_probs, spatial_rounded = attention(
        split_heads(spatial_query), split_heads(keys_joined), split_heads(values_joined), False
    )
    spatial_mixed = merge_heads(spatial_mixed)
    hidden_one = (frames.astype(jnp.float32) + project(spatial_mixed, full_space_output)).astype(
        jnp.bfloat16
    )
    centred_two, inverse_two = layer_stats(hidden_one)
    table = position_table(block * frame_count, frame_count, frames.shape[2])
    normed_two = (centred_two + table[:, None, :]).astype(jnp.bfloat16)
    normed_rows = lax.all_to_all(normed_two, "frame", split_axis=1, concat_axis=0, tiled=True)
    temporal_query = project(normed_rows, full_time_query).astype(jnp.bfloat16)
    temporal_key = project(normed_rows, full_time_key).astype(jnp.bfloat16)
    temporal_value = project(normed_rows, full_time_value).astype(jnp.bfloat16)
    temporal_mixed, temporal_probs, temporal_rounded = attention(
        split_heads(temporal_query), split_heads(temporal_key), split_heads(temporal_value), True
    )
    mixed_two = lax.all_to_all(
        merge_heads(temporal_mixed), "frame", split_axis=0, concat_axis=1, tiled=True
    )
    output = (hidden_one.astype(jnp.float32) + project(mixed_two, full_time_output)).astype(
        jnp.bfloat16
    )
    mixed_grad_two = project_back(cotangent, full_time_output).astype(jnp.bfloat16)
    token_grad = lax.all_to_all(mixed_grad_two, "frame", split_axis=1, concat_axis=0, tiled=True)
    token_query_grad, token_key_grad, token_value_grad = attention_back(
        split_heads(temporal_query),
        split_heads(temporal_key),
        split_heads(temporal_value),
        temporal_probs,
        temporal_rounded,
        split_heads(token_grad),
        True,
    )
    query_grad_two, key_grad_two, value_grad_two = (
        lax.all_to_all(
            merge_heads(token_query_grad), "frame", split_axis=0, concat_axis=1, tiled=True
        ),
        lax.all_to_all(
            merge_heads(token_key_grad).astype(jnp.bfloat16),
            "frame",
            split_axis=0,
            concat_axis=1,
            tiled=True,
        ),
        lax.all_to_all(
            merge_heads(token_value_grad).astype(jnp.bfloat16),
            "frame",
            split_axis=0,
            concat_axis=1,
            tiled=True,
        ),
    )
    normed_grad_two = (
        project_back(query_grad_two, full_time_query)
        + project_back(key_grad_two, full_time_key)
        + project_back(value_grad_two, full_time_value)
    )
    hidden_grad = (
        cotangent.astype(jnp.float32) + layer_back(centred_two, inverse_two, normed_grad_two)
    ).astype(jnp.bfloat16)
    mixed_grad_one = project_back(hidden_grad, full_space_output).astype(jnp.bfloat16)
    query_grad_one, key_joined_grad, value_joined_grad = attention_back(
        split_heads(spatial_query),
        split_heads(keys_joined),
        split_heads(values_joined),
        spatial_probs,
        spatial_rounded,
        split_heads(mixed_grad_one),
        False,
    )
    query_grad_one = merge_heads(query_grad_one)
    key_grad_one = merge_heads(key_joined_grad[:, :token_count]).astype(jnp.bfloat16)
    value_grad_one = merge_heads(value_joined_grad[:, :token_count]).astype(jnp.bfloat16)
    partial_key = merge_heads(jnp.sum(key_joined_grad[:, token_count:], 0))
    partial_value = merge_heads(jnp.sum(value_joined_grad[:, token_count:], 0))
    summed_key, summed_value = (
        lax.psum_scatter(
            partial_key.astype(jnp.bfloat16), "frame", scatter_dimension=0, tiled=True
        ).astype(jnp.float32),
        lax.psum_scatter(
            partial_value.astype(jnp.bfloat16), "frame", scatter_dimension=0, tiled=True
        ).astype(jnp.float32),
    )
    refer_key_grad = summed_key.astype(jnp.bfloat16)
    refer_value_grad = summed_value.astype(jnp.bfloat16)
    normed_grad_one = (
        project_back(query_grad_one, full_space_query)
        + project_back(key_grad_one, full_space_key)
        + project_back(value_grad_one, full_space_value)
    )
    frames_grad = (
        hidden_grad.astype(jnp.float32) + layer_back(centred_one, inverse_one, normed_grad_one)
    ).astype(jnp.bfloat16)
    refer_grad = (
        project_back(refer_key_grad, full_space_key)
        + project_back(refer_value_grad, full_space_value)
    ).astype(jnp.bfloat16)
    term_sq = outer_sum(normed_one, query_grad_one)
    term_sk = outer_sum(normed_one, key_grad_one) + outer_sum(refer, refer_key_grad)
    term_sv = outer_sum(normed_one, value_grad_one) + outer_sum(refer, refer_value_grad)
    term_so = outer_sum(spatial_mixed, hidden_grad)
    term_tq = outer_sum(normed_two, query_grad_two)
    term_tk = outer_sum(normed_two, key_grad_two)
    term_tv = outer_sum(normed_two, value_grad_two)
    term_to = outer_sum(mixed_two, cotangent)
    share_sq, share_sk, share_sv, share_so, share_tq, share_tk, share_tv, share_to = (
        lax.psum_scatter(
            term_sq.astype(jnp.bfloat16), "frame", scatter_dimension=0, tiled=True
        ).astype(jnp.float32),
        lax.psum_scatter(
            term_sk.astype(jnp.bfloat16), "frame", scatter_dimension=0, tiled=True
        ).astype(jnp.float32),
        lax.psum_scatter(
            term_sv.astype(jnp.bfloat16), "frame", scatter_dimension=0, tiled=True
        ).astype(jnp.float32),
        lax.psum_scatter(
            term_so.astype(jnp.bfloat16), "frame", scatter_dimension=0, tiled=True
        ).astype(jnp.float32),
        lax.psum_scatter(
            term_tq.astype(jnp.bfloat16), "frame", scatter_dimension=0, tiled=True
        ).astype(jnp.float32),
        lax.psum_scatter(
            term_tk.astype(jnp.bfloat16), "frame", scatter_dimension=0, tiled=True
        ).astype(jnp.float32),
        lax.psum_scatter(
            term_tv.astype(jnp.bfloat16), "frame", scatter_dimension=0, tiled=True
        ).astype(jnp.float32),
        lax.psum_scatter(
            term_to.astype(jnp.bfloat16), "frame", scatter_dimension=0, tiled=True
        ).astype(jnp.float32),
    )
    total_sq, total_sk, total_sv, total_so, total_tq, total_tk, total_tv, total_to = (
        lax.psum(share_sq.astype(jnp.bfloat16), "clip").astype(jnp.float32),
        lax.psum(share_sk.astype(jnp.bfloat16), "clip").astype(jnp.float32),
        lax.psum(share_sv.astype(jnp.bfloat16), "clip").astype(jnp.float32),
        lax.psum(share_so.astype(jnp.bfloat16), "clip").astype(jnp.float32),
        lax.psum(share_tq.astype(jnp.bfloat16), "clip").astype(jnp.float32),
        lax.psum(share_tk.astype(jnp.bfloat16), "clip").astype(jnp.float32),
        lax.psum(share_tv.astype(jnp.bfloat16), "clip").astype(jnp.float32),
        lax.psum(share_to.astype(jnp.bfloat16), "clip").astype(jnp.float32),
    )
    return (
        output[None],
        frames_grad[None],
        refer_grad[None],
        total_sq,
        total_sk,
        total_sv,
        total_so,
        total_tq,
        total_tk,
        total_tv,
        total_to,
    )


CHUNK = 32


def mm(left, right):
    return jnp.dot(left, right, preferred_element_type=F32)


def mm_bt(left, right):
    return lax.dot_general(left, right, (((1,), (1,)), ((), ())), preferred_element_type=F32)


def mm_at(left, right):
    return lax.dot_general(left, right, (((0,), (0,)), ((), ())), preferred_element_type=F32)


def wide_call(body, name, out_shape, scratch, limit_mb, flops, num_in, kept=0, late=()):
    def with_late(idx, *refs):
        body(idx, *refs[: num_in - 1], *refs[num_in - 1 + len(late) :])

    call = pl.pallas_call(
        with_late,
        name=name,
        out_shape=out_shape,
        in_specs=[pl.BlockSpec(memory_space=pltpu.SMEM)]
        + [pl.BlockSpec(memory_space=pltpu.HBM)] * kept
        + [pl.BlockSpec(memory_space=pltpu.VMEM)] * (num_in - 1 - kept)
        + [pl.BlockSpec(memory_space=pl.ANY)] * len(late),
        out_specs=tuple(pl.BlockSpec(memory_space=pltpu.VMEM) for _ in out_shape),
        scratch_shapes=scratch,
        compiler_params=pltpu.CompilerParams(vmem_limit_bytes=limit_mb * 1024 * 1024),
        cost_estimate=pl.CostEstimate(
            flops=max(flops, 1), bytes_accessed=8_000_000 if flops > 1 else 1, transcendentals=0
        ),
    )
    return lambda *operands: call(*operands, *late)


def struct(*shape, dtype=BF16):
    return jax.ShapeDtypeStruct(shape, dtype)


def flip(value, axis, bit):
    size = lax.axis_size(axis)
    return lax.ppermute(value, axis, [(i, i ^ bit) for i in range(size)])


def after(value, *others):
    corners = [o[(slice(0, 1),) * (o.ndim - 2) + (slice(0, 8), slice(0, 128))] for o in others]
    return lax.optimization_barrier((value, *corners))[0]


def load(sources, held, sems):
    copies = [pltpu.make_async_copy(w, h, sems.at[i]) for i, (w, h) in enumerate(zip(sources, held))]
    for copy in copies:
        copy.start()
    return copies


def pack_body(heads, n, per, idx, *refs):
    sources, near, (far, first, grad_own, grad_near, across) = refs[:10], refs[10:12], refs[12:17]
    packs, held, (wide, few, sems) = refs[17], refs[18:28], refs[28:]
    me, side, mine = idx[0], idx[1] & 1, idx[1] & 3
    half = far.shape[1]
    depth, inner = held[0].shape
    low = held[6].shape[0]
    width = inner // heads
    part = depth // 4
    copies = load(sources, held, sems)
    for copy in copies[:3]:
        copy.wait()
    for h in range(heads):
        parts = [held[i][:, h * width : (h + 1) * width] for i in range(3)]
        parts.append(jnp.zeros((depth, packs.shape[2] - 3 * width), BF16))
        packs[h] = jnp.concatenate(parts, 1)
    for r in range(2):
        near[r][...] = packs[me ^ r]
        far[r] = packs[me ^ (r + 2), pl.ds(pl.multiple_of(side * half, half), half), :]
    for copy in copies[3:]:
        copy.wait()
    at = pl.ds(pl.multiple_of(mine * part, part), part)
    for i in range(3):
        first[i * part : (i + 1) * part, :] = held[3 + i][at, :]
    for v in range(4):

        @pl.when(mine == v)
        def _(v=v):
            first[3 * part :, :] = held[6 + (v >> 1)][:, (v & 1) * inner : (v & 1) * inner + inner]

    wide[...] = held[8][...].astype(F32)
    count = few.shape[0]
    share = count // per
    tokens = wide.shape[0] // per
    for r in range(n):
        start = pl.multiple_of((me ^ r) * share, share)
        for j in range(per):
            few[j * share : (j + 1) * share, :] = wide[pl.ds(j * tokens + start, share), :]
        if r == 0:
            grad_own[...] = few[...].astype(BF16)
        elif r == 1:
            grad_near[:count, :] = few[...].astype(BF16)
        else:
            across[(r - 2) * count : (r - 1) * count, :] = few[...].astype(BF16)
    grad_near[count:, :] = held[9][...]
    across[2 * count :, :] = held[9][...]


def spatial_forward_body(n, tokens, width, idx, *refs):
    sources, refs = refs[: 2 * n + 8], refs[2 * n + 8 :]
    x_out, w_out, q_out, k_out, v_out, p_out = refs[:6]
    o_outs, (token_out, tall_out, flat_out) = refs[6 : n + 6], refs[n + 6 : n + 9]
    mixed, turn, few, wide, spread, sems = refs[n + 9 : n + 15]
    held = refs[n + 15 :]
    cut = tall_out.shape[0]
    copies = load(sources, held, sems)
    frames, refer, packs = held[:n], held[n : 2 * n], held[2 * n :]
    near, far = packs[:2], ((packs[2], packs[3]), (packs[4], packs[5]))
    me, side = idx[0], idx[1] & 1
    share = tokens // n
    rows = frames[0].shape[0]
    depth = near[0].shape[0]
    half = depth // 2
    lanes = q_out.shape[1]
    room = w_out.shape[1]
    total = n * rows
    for r in range(n):
        copies[r].wait()

        def norm(i, _, r=r):
            at = pl.multiple_of(i * CHUNK, CHUNK)
            centred, _ = layer_stats(frames[r][pl.ds(at, CHUNK), :])
            x_out[pl.ds(r * rows + at, CHUNK), :] = centred.astype(BF16)
            return 0

        lax.fori_loop(0, rows // CHUNK, norm, 0)
        wide[...] = frames[r][...].astype(F32)
        first = pl.multiple_of(me * share, share)
        for j in range(rows // tokens):
            at = r * (rows // tokens) * share + j * share
            spread[at : at + share, :] = wide[pl.ds(j * tokens + first, share), :]
        copies[n + r].wait()
        few[r * share : (r + 1) * share, :] = refer[r][refer[r].shape[0] - share :, :].astype(F32)
    x_out[total:, :] = few[...].astype(BF16)
    token_out[...] = spread[...].astype(BF16)
    for copy in copies[2 * n :]:
        copy.wait()
    for r in range(2):
        w_out[pl.ds(pl.multiple_of((me ^ r) * depth, depth), depth), :] = near[r][...]
        for k in range(2):
            at = pl.multiple_of((me ^ (r + 2)) * depth + (side ^ k) * half, half)
            w_out[pl.ds(at, half), :] = far[r][k][r]
    second, third = packs[6:8]
    tall_out[...] = third[:cut, :]
    flat_out[...] = second[cut:, :]
    for start, count in [(r * rows, rows) for r in range(n)] + [(total, tokens)]:
        three = mm(x_out[start : start + count, :], w_out[...])
        keep = lax.broadcasted_iota(jnp.int32, (count, lanes), 1) < width
        q_out[start : start + count, :] = jnp.where(keep, three[:, :lanes], 0.0).astype(BF16)
        k_out[start : start + count, :] = jnp.where(
            keep, pltpu.roll(three, room - width, 1)[:, :lanes], 0.0
        ).astype(BF16)
        v_out[start : start + count, :] = jnp.where(
            keep, pltpu.roll(three, room - 2 * width, 1)[:, :lanes], 0.0
        ).astype(BF16)
    scale = width**-0.5
    for b in range(total // tokens):
        at = slice(b * tokens, (b + 1) * tokens)
        keys = jnp.concatenate([k_out[at, :], k_out[total:, :]], 0)
        values = jnp.concatenate([v_out[at, :], v_out[total:, :]], 0)
        powers = jnp.exp(mm_bt(q_out[at, :], keys) * scale)
        probs = powers / jnp.sum(powers, -1, keepdims=True)
        p_out[at, :] = probs
        mixed[at, :] = mm(probs.astype(BF16), values)
    per = rows // tokens
    for r in range(n):
        first = pl.multiple_of((me ^ r) * share, share)
        for b in range(total // tokens):
            to = ((b // per) ^ r) * per + b % per
            turn[to * share : (to + 1) * share, :] = mixed[pl.ds(b * tokens + first, share), :]
        o_outs[r][...] = turn[...].astype(BF16)


def spatial_backward_body(n, tokens, width, idx, *refs):
    grads = refs[:n]
    x_ref, w_ref, q_ref, k_ref, v_ref, p_ref = refs[n : n + 6]
    keep_out, send_out, keep_term, send_term = refs[n + 6 : n + 10]
    spread, turn, packed, term = refs[n + 10 :]
    me = idx[0]
    share = tokens // n
    total = p_ref.shape[0]
    rows = total // n
    lanes = q_ref.shape[1]
    room = w_ref.shape[1]
    per = rows // tokens
    for r in range(n):
        first = pl.multiple_of((me ^ r) * share, share)
        turn[...] = grads[r][...].astype(F32)
        for b in range(total // tokens):
            to = ((b // per) ^ r) * per + b % per
            spread[pl.ds(b * tokens + first, share), :] = turn[to * share : (to + 1) * share, :]
    scale = width**-0.5

    def pack(first, second, third):
        def wide(part):
            blank = jnp.zeros((part.shape[0], room - lanes), F32)
            return jnp.concatenate([part, blank], 1)

        result = pltpu.roll(wide(second), width, 1) + pltpu.roll(wide(third), 2 * width, 1)
        return result if first is None else result + wide(first)

    key_sum = jnp.zeros((k_ref.shape[0] - total, lanes), F32)
    value_sum = key_sum
    for b in range(total // tokens):
        at = slice(b * tokens, (b + 1) * tokens)
        query = q_ref[at, :]
        keys = jnp.concatenate([k_ref[at, :], k_ref[total:, :]], 0)
        values = jnp.concatenate([v_ref[at, :], v_ref[total:, :]], 0)
        cotangent = spread[at, :].astype(BF16)
        probs = p_ref[at, :]
        back = mm_bt(cotangent, values)
        score = (probs * (back - jnp.sum(probs * back, -1, keepdims=True)) * scale).astype(BF16)
        query_grad = mm(score, keys)
        key_grad = mm_at(score, query)
        value_grad = mm_at(probs.astype(BF16), cotangent)
        key_sum = key_sum + key_grad[tokens:]
        value_sum = value_sum + value_grad[tokens:]
        packed[at, :] = pack(query_grad, key_grad[:tokens], value_grad[:tokens]).astype(BF16)
    packed[total:, :] = pack(None, key_sum, value_sum).astype(BF16)
    for r in range(n):
        part = mm_bt(packed[r * rows : (r + 1) * rows, :], w_ref[...]).astype(BF16)
        (send_out if r & 1 else keep_out)[r >> 1, :rows, :] = part
    part = mm_bt(packed[total:, :], w_ref[...])
    for r in range(n):
        few = part[r * share : (r + 1) * share].astype(BF16)
        (send_out if r & 1 else keep_out)[r >> 1, rows:, :] = few
    depth = x_ref.shape[1] // 5
    for j in range(5):
        at = slice(j * depth, (j + 1) * depth)
        term[at, :] = mm_at(x_ref[:, at], packed[...])
    side = idx[1] & 1
    count, piece = keep_term.shape[0], keep_term.shape[2]
    for j in range(n):
        for k in range(count):
            for out, half in ((keep_term, side), (send_term, 1 - side)):
                at = pl.multiple_of((j * 2 * count + half * count + k) * piece, piece)
                out[k, j] = term[pl.ds(at, piece), :].astype(BF16)


def parts_of(ref, dim, inner):
    starts = [0, dim, 2 * dim] + [3 * dim + i * inner for i in range(4)]
    parts = [ref.at[:, a : a + (dim if i < 3 else inner)] for i, a in enumerate(starts)]
    first, lanes = 3 * dim + 4 * inner, (ref.shape[1] - 3 * dim - 4 * inner) // 2
    return parts + [ref.at[:, first + i * lanes : first + (i + 1) * lanes] for i in range(2)]


def temporal_body(n, heads, per, idx, *refs):
    mixed_in, near, far, refs = refs[:n], (refs[n : n + 5], refs[n + 5 : n + 10]), refs[n + 10 :][:10], refs[n + 20 :]
    far = (far[:5], far[5:])
    frames_in, cotangents, table_in, refs = refs[0], refs[1 : n + 1], refs[n + 1], refs[n + 2 :]
    grad_outs, back_outs, kept, refs = refs[:n], refs[n : 2 * n], refs[2 * n], refs[2 * n + 1 :]
    so, tq, tk, tv, to, hidden, centred, inverse, wide, qs, gos = refs[:11]
    mixed, frames, table, sems = refs[11 : n + 11], *refs[n + 11 :]
    me, quarter = idx[0], idx[1] & 3
    rows, dim = frames.shape
    inner = tq.shape[1]
    width = inner // heads
    depth, low = dim // n, inner // n
    part = depth // 4
    few = rows // n
    share = few // per
    gh_out, n2_out, cotangent, gq_out, gk_out, gv_out, o2_out, *o_outs = parts_of(kept, dim, inner)
    first, second, chosen = [], [], []

    def bring(source, to_ref, group):
        group.append(pltpu.make_async_copy(source, to_ref, sems.at[len(first) + len(second) + len(chosen)]))

    def low_rows(r):
        return pl.ds(pl.multiple_of((me ^ r) * low, low), low)

    for r in range(n):
        bring(mixed_in[r], mixed[r], first)
        if r < 2:
            bring(near[r][3], so.at[r, pl.ds(0, low), :], first)
    bring(frames_in, frames, first)
    bring(table_in, table, first)
    for r in range(2, n):
        for s in range(4):
            flat, start = (far[r - 2][s], 3 * part) if s < 3 else (far[r - 2][4], 0)
            place = len(first) + len(second) + len(chosen)
            cases = []
            for v in range(4):
                lanes = pl.ds((v & 1) * inner, inner)
                target = so.at[r, pl.ds(0, low), lanes] if v < 2 else to.at[low_rows(r), lanes]
                source = flat.at[pl.ds(start, low), :]
                cases.append((v, pltpu.make_async_copy(source, target, sems.at[place])))
            chosen.append((quarter ^ s, cases))
    for r in range(n):
        if r < 2:
            bring(near[r][4], to.at[low_rows(r), :], second)
        for i, whole in enumerate((tq, tk, tv)):
            if r < 2:
                at = pl.ds(pl.multiple_of((me ^ r) * depth, depth), depth)
                bring(near[r][i], whole.at[at, :], second)
                continue
            for s in range(4):
                at = pl.ds(pl.multiple_of((me ^ r) * depth + (quarter ^ s) * part, part), part)
                bring(far[r - 2][s].at[pl.ds(i * part, part), :], whole.at[at, :], second)
        source = cotangents[r].at[pl.ds(few if r == 3 else 0, few), :]
        bring(source, cotangent.at[pl.ds(r * few, few), :], second)

    def choose(act):
        for which, cases in chosen:
            for v, copy in cases:

                @pl.when(which == v)
                def _(copy=copy):
                    act(copy)

    for copy in first:
        copy.start()
    choose(lambda copy: copy.start())
    for copy in second:
        copy.start()
    so[:, low:, :] = jnp.zeros((n, so.shape[1] - low, dim), BF16)
    for copy in first:
        copy.wait()
    choose(lambda copy: copy.wait())
    for i in range(2):
        o_outs[i][...] = mixed[2 * i + 1][...]
    step = dim // 5
    for j in range(5):
        at = slice(j * step, (j + 1) * step)
        acc = frames[:, at].astype(F32)
        for r in range(n):
            acc = acc + mm(mixed[r][...], so[r, :, at])
        hidden[:, at] = acc.astype(BF16).astype(F32)

    def norm(i, _):
        at = pl.ds(pl.multiple_of(i * share, share), share)
        offset, scale = layer_stats(hidden[at, :])
        centred[at, :] = offset
        inverse[at, :] = jnp.broadcast_to(scale, (share, inverse.shape[1]))
        wide[at, :] = offset + table[pl.ds(i, 1), :]
        return 0

    lax.fori_loop(0, rows // share, norm, 0)
    n2_out[...] = wide[...].astype(BF16)
    for copy in second:
        copy.wait()

    def token(axis):
        place = lax.broadcasted_iota(jnp.int32, (rows, rows), axis).astype(F32)
        return place - share * jnp.floor((place + 0.5) * (1.0 / share))

    same = token(0) == token(1)
    lane_head = lax.broadcasted_iota(jnp.int32, (rows, inner), 1)

    def own(h, value):
        inside = (lane_head >= h * width) & (lane_head < (h + 1) * width)
        return jnp.where(inside, value, 0.0)

    scale = width**-0.5
    query = mm(n2_out[...], tq[...])
    for h in range(heads):
        qs[h * rows : (h + 1) * rows, :] = own(h, query).astype(BF16)
    keys = mm(n2_out[...], tk[...]).astype(BF16)
    values = mm(n2_out[...], tv[...]).astype(BF16)
    mixed_grad = mm_bt(cotangent[...], to[...])
    for h in range(heads):
        gos[h * rows : (h + 1) * rows, :] = own(h, mixed_grad).astype(BF16)
    key_grad = jnp.zeros((rows, inner), F32)
    value_grad = jnp.zeros((rows, inner), F32)
    query_grad = jnp.zeros((rows, inner), F32)
    o2 = jnp.zeros((rows, inner), F32)
    for h in range(heads):
        at = slice(h * rows, (h + 1) * rows)
        scores = mm_bt(qs[at, :], keys) * scale
        powers = jnp.where(same, jnp.exp(scores), 0.0)
        probs = powers / jnp.sum(powers, -1, keepdims=True)
        rounded = probs.astype(BF16)
        o2 = o2 + own(h, mm(rounded, values))
        back = mm_bt(gos[at, :], values)
        score = (probs * (back - jnp.sum(probs * back, -1, keepdims=True)) * scale).astype(BF16)
        query_grad = query_grad + own(h, mm(score, keys))
        key_grad = key_grad + mm_at(score, qs[at, :])
        value_grad = value_grad + mm_at(rounded, gos[at, :])
    o2_out[...] = o2.astype(BF16)
    gq_out[...] = query_grad.astype(BF16)
    gk_out[...] = key_grad.astype(BF16)
    gv_out[...] = value_grad.astype(BF16)
    for j in range(5):
        at = slice(j * step, (j + 1) * step)
        wide[:, at] = (
            mm_bt(gq_out[...], tq[at, :]) + mm_bt(gk_out[...], tk[at, :]) + mm_bt(gv_out[...], tv[at, :])
        )

    def back_norm(i, _):
        at = pl.ds(pl.multiple_of(i * CHUNK, CHUNK), CHUNK)
        back = layer_back(centred[at, :], inverse[at, :1], wide[at, :])
        gh_out[at, :] = (cotangent[at, :].astype(F32) + back).astype(BF16)
        return 0

    lax.fori_loop(0, rows // CHUNK, back_norm, 0)
    for r in range(n):
        grad_outs[r][...] = mm_bt(gh_out[...], so[r]).astype(BF16)
    for j in range(5):
        at = slice(j * step, (j + 1) * step)
        part = (hidden[:, at] + mm(o2_out[...], to[:, at])).astype(BF16)
        for r in range(n):
            back_outs[r][:few, at] = part[r * few : (r + 1) * few]
    for r in range(n):
        back_outs[r][few:, :] = gh_out[r * few : (r + 1) * few, :]


def terms_body(n, idx, *refs):
    held, refs = refs[:4], refs[4:]
    tall_keep, tall_send, flat_keep, flat_send = refs[:4]
    n2_turned, o2_turned, tall, so = refs[4:]
    me, bit = idx[0], (idx[1] >> 1) & 1
    rows = held[0].shape[0]
    depth, inner = tall.shape
    dim, low = depth * n, inner // n
    pieces, _, piece = tall_keep.shape[:3]
    both = [parts_of(ref, dim, inner) for ref in held[:2]]
    for i in range(2):
        n2_turned[:, i * rows : (i + 1) * rows] = both[i][1][...].T
        o2_turned[:, i * rows : (i + 1) * rows] = both[i][6][...].T
    ours, theirs = both
    mixed = [*held[2:], *theirs[7:]]
    for i in range(3):
        grad = jnp.concatenate([ours[3 + i][...], theirs[3 + i][...]], 0)
        for k, out in enumerate((tall_keep, tall_send)):
            at = pl.multiple_of((me ^ (2 * k)) * depth, depth)
            tall[...] = mm(n2_turned[pl.ds(at, depth), :], grad)
            for p in range(pieces):
                out[p, i] = tall[p * piece : (p + 1) * piece, :].astype(BF16)
    half = low // 2
    for k in range(2):
        so[0] = (mm_at(mixed[k][...], ours[0][...]) + mm_at(mixed[2 + k][...], theirs[0][...]))[:low]
        at = pl.multiple_of((me ^ (2 * k)) * low, low)
        grad = jnp.concatenate([ours[2][...], theirs[2][...]], 0)
        so[1] = mm(o2_turned[pl.ds(at, low), :], grad)
        for i in range(2):
            for j in range(2):
                for out, part in ((flat_keep, bit), (flat_send, 1 - bit)):
                    at = pl.multiple_of(part * half, half)
                    out[k, i, j] = so[i, pl.ds(at, half), j * inner : (j + 1) * inner].astype(BF16)


def finish_body(n, per, idx, frames, *refs):
    parts, near, far = refs[:n], refs[n], refs[n + 1]
    out, frames_grad, refer_grad, turn, wide = refs[n + 2 :]
    me = idx[0]
    rows, few = frames.shape[0], parts[0].shape[0] // 2
    share, tokens = few // per, rows // per
    for r in range(n):
        first = pl.multiple_of((me ^ r) * share, share)
        turn[...] = parts[r][...].astype(F32)
        for which in range(2):
            for j in range(per):
                at = which * few + j * share
                wide[which, pl.ds(j * tokens + first, share), :] = turn[at : at + share, :]
    out[...] = wide[0].astype(BF16)

    def step(i, _):
        at = pl.ds(pl.multiple_of(i * CHUNK, CHUNK), CHUNK)
        centred, inverse = layer_stats(frames[at, :])
        grad = near[at, :].astype(F32) + far[at, :].astype(F32)
        back = layer_back(centred, inverse, grad)
        frames_grad[at, :] = (wide[1, at, :] + back).astype(BF16)
        return 0

    lax.fori_loop(0, rows // CHUNK, step, 0)
    refer_grad[...] = (near[rows:, :].astype(F32) + far[rows:, :].astype(F32)).astype(BF16)


def place_body(idx, near, far, *outs):
    side, low_bit = idx[1] & 1, (idx[1] >> 1) & 1
    piece = near.shape[3]
    for low, source in enumerate((near, far)):
        for high, other in itertools.product(range(2), range(2)):
            place = (side ^ other) * 4 + 2 * high + (low_bit ^ low)
            at = pl.multiple_of(place * piece, piece)
            for i, out in enumerate(outs):
                out[pl.ds(at, piece), :] = source[high, other, i].astype(F32)


def place_heads_body(width, idx, near, far, *outs):
    me, side, low_bit = idx[0], idx[1] & 1, (idx[1] >> 1) & 1
    _, _, n, piece, _ = near.shape
    for low, source in enumerate((near, far)):
        for high, other in itertools.product(range(2), range(2)):
            place = (side ^ other) * 4 + 2 * high + (low_bit ^ low)
            at = pl.multiple_of(place * piece, piece)
            heads = [source[high, other, me ^ h].astype(F32) for h in range(n)]
            for i, out in enumerate(outs):
                parts = [h[:, i * width : (i + 1) * width] for h in heads]
                out[pl.ds(at, piece), :] = jnp.concatenate(parts, 1)


def place_flat_body(idx, near, far, *outs):
    side, low_bit = idx[1] & 1, (idx[1] >> 1) & 1
    piece, inner = near.shape[2:]
    for source, half in ((near, side), (far, 1 - side)):
        for high, low in itertools.product(range(2), range(2)):
            at = pl.multiple_of((low_bit ^ low) * piece, piece)
            for i, out in enumerate(outs):

                @pl.when(half == i)
                def _(source=source, high=high, low=low, at=at, out=out):
                    lanes = slice(high * inner, (high + 1) * inner)
                    out[pl.ds(at, piece), lanes] = source[high, low].astype(F32)


def merge_body(axis, place, spread, idx, kept, moved, *outs):
    shape = kept.shape
    bit = None if axis is None else (idx[1] >> place) & 1
    for at in itertools.product(*map(range, shape[:-2])):
        if axis is not None:
            if at[axis]:
                continue
            rest = at[:axis] + at[axis + 1 :]
            for out, half in ((outs[0], bit), (outs[1], 1 - bit)):
                here = at[:axis] + (half,) + at[axis + 1 :]
                out[rest] = (kept[here].astype(F32) + moved[here].astype(F32)).astype(BF16)
        elif spread:
            here = (at[0], idx[0] ^ at[1])
            outs[at[1]][at[0]] = (kept[here].astype(F32) + moved[here].astype(F32)).astype(BF16)
        else:
            outs[0][at] = (kept[at].astype(F32) + moved[at].astype(F32)).astype(BF16)


def join_body(axis, idx, *refs):
    out = refs[-1]
    for i, part in enumerate(refs[:-1]):
        for at in itertools.product(*map(range, part.shape[:-2])):
            out[at[:axis] + (i,) + at[axis:]] = part[at]


def pick(value, index, axis=0):
    return lax.dynamic_index_in_dim(value, index, axis, keepdims=False)


class Steps:
    def __init__(self, idx):
        self.idx, self.last = idx, ()

    def call(self, body, name, out_shape, operands, scratch=(), limit_mb=12):
        def marked(idx, *refs):
            ends = len(operands) + len(out_shape)
            body(idx, *refs[:ends], *refs[ends + 1 :])
            refs[ends][...] = jnp.zeros(refs[ends].shape, F32)

        *outs, mark = wide_call(
            marked,
            name,
            list(out_shape) + [struct(8, 128, dtype=F32)],
            list(scratch),
            limit_mb,
            0,
            len(operands) + 1,
            0,
            self.last,
        )(self.idx, *operands)
        self.last = (mark,)
        return outs

    def merge(self, kept, moved, axis=None, place=0, spread=False):
        shape = kept.shape
        if axis is not None:
            shapes = [shape[:axis] + shape[axis + 1 :]] * 2
        else:
            shapes = [shape[:1] + shape[2:]] * shape[1] if spread else [shape]
        body = functools.partial(merge_body, axis, place, spread)
        outs = self.call(body, "merge", [struct(*one) for one in shapes], [kept, moved])
        return outs if len(outs) > 1 else outs[0]

    def join(self, *parts, axis=0):
        shape = parts[0].shape
        shape = shape[:axis] + (len(parts),) + shape[axis:]
        return self.call(functools.partial(join_body, axis), "join", [struct(*shape)], parts)[0]


def per_device(
    frames_in,
    ref_feats,
    out_grad,
    space_query,
    space_key,
    space_value,
    space_output,
    time_query,
    time_key,
    time_value,
    time_output,
):
    n = lax.axis_size("frame")
    clips = lax.axis_size("clip")
    me = lax.axis_index("frame")
    clip = lax.axis_index("clip")
    side, level = clip & 1, clip >> 1
    idx = jnp.stack([me, clip]).astype(jnp.int32)
    _, per, tokens, dim = frames_in.shape
    inner = space_query.shape[1]
    width = inner // HEADS
    lanes = -(-width // 128) * 128
    room = -(-3 * width // 128) * 128
    depth, low = dim // n, inner // n
    rows = per * tokens
    total = n * rows
    share = tokens // n
    few = per * share
    token_rows = n * few
    count, piece = clips // 2, depth // clips
    frames = frames_in.reshape(rows, dim)
    steps = Steps(idx)

    def exchange(parts):
        return [parts[0]] + [flip(parts[r], "frame", r) for r in range(1, n)]

    def gather(value):
        far = flip(value, "frame", 2)
        return [value, flip(value, "frame", 1), far, flip(far, "frame", 1)]

    others = (time_query, time_key, time_value, space_output, time_output)
    own, near, far_pack, first, grad_own, grad_near, across = wide_call(
        functools.partial(pack_body, HEADS, n, per),
        "pack_heads",
        [
            struct(depth, room),
            struct(depth, room),
            struct(2, depth // 2, room),
            struct(3 * depth // 4 + low, inner),
            struct(few, dim),
            struct(few + share, dim),
            struct(2 * few + share, dim),
        ],
        [pltpu.VMEM((HEADS, depth, room), BF16)]
        + [pltpu.VMEM((depth, inner), BF16)] * 6
        + [pltpu.VMEM((low, dim), BF16)] * 2
        + [
            pltpu.VMEM((rows, dim), BF16),
            pltpu.VMEM((share, dim), BF16),
            pltpu.VMEM((rows, dim), F32),
            pltpu.VMEM((few, dim), F32),
            pltpu.SemaphoreType.DMA((10,)),
        ],
        60,
        0,
        11,
        10,
    )(idx, space_query, space_key, space_value, *others, out_grad.reshape(rows, dim), ref_feats[0])
    first = flip(first, "frame", 2)
    far_pack = flip(far_pack, "frame", 2)
    far_frames = flip(after(frames, far_pack), "frame", 2)
    across = flip(after(across, far_pack), "frame", 2)
    side_pack = flip(far_pack, "clip", 1)
    second, third = flip(first, "clip", 1), flip(first, "clip", 2)
    near, grad_near, near_frames = (flip(v, "frame", 1) for v in (near, grad_near, frames))
    packs = [own, near, far_pack, side_pack, flip(far_pack, "frame", 1), flip(side_pack, "frame", 1)]
    all_frames = [frames, near_frames, far_frames, flip(far_frames, "frame", 1)]
    across_near = flip(across, "frame", 1)
    all_refer = [ref_feats[0], grad_near, across, across_near]
    token_grad = [grad_own, grad_near, across, across_near]
    far = [first, second, third]
    far_near = [flip(p, "frame", 1) for p in far]
    others_near = [flip(p, "frame", 1) for p in others]
    frame_ids = jnp.concatenate([(me ^ r) * per + jnp.arange(per) for r in range(n)])
    table = position_rows(frame_ids, dim)

    cut = 3 * depth // 4
    x_all, w_all, q_all, k_all, v_all, probs, *mixed, token_frames, tall_part, flat_part = wide_call(
        functools.partial(spatial_forward_body, n, tokens, width),
        "spatial_forward",
        [
            struct(total + tokens, dim),
            struct(dim, room),
            struct(total + tokens, lanes),
            struct(total + tokens, lanes),
            struct(total + tokens, lanes),
            struct(total, 2 * tokens, dtype=F32),
            *[struct(token_rows, lanes)] * n,
            struct(token_rows, dim),
            struct(cut, inner),
            struct(low, inner),
        ],
        [
            pltpu.VMEM((total, lanes), F32),
            pltpu.VMEM((token_rows, lanes), F32),
            pltpu.VMEM((tokens, dim), F32),
            pltpu.VMEM((rows, dim), F32),
            pltpu.VMEM((token_rows, dim), F32),
            pltpu.SemaphoreType.DMA((2 * n + 8,)),
        ]
        + [pltpu.VMEM((rows, dim), BF16)] * n
        + [pltpu.VMEM(one.shape, BF16) for one in all_refer]
        + [pltpu.VMEM((depth, room), BF16)] * 2
        + [pltpu.VMEM((2, depth // 2, room), BF16)] * 4
        + [pltpu.VMEM((cut + low, inner), BF16)] * 2,
        60,
        2_000_000_000,
        2 * n + 9,
        2 * n + 8,
        tuple(far_near),
    )(idx, *all_frames, *all_refer, *packs, second, third)
    mixed = exchange(mixed)
    fourth = [flip(tall_part, "clip", 1), flip(flat_part, "clip", 2)]
    fourth_near = [flip(p, "frame", 1) for p in fourth]
    blocks = [*others, *others_near, *far, *fourth, *far_near, *fourth_near]
    outs = wide_call(
        functools.partial(temporal_body, n, HEADS, per),
        "temporal",
        [struct(token_rows, lanes)] * n
        + [struct(2 * few, dim)] * n
        + [struct(token_rows, 3 * dim + 4 * inner + 2 * lanes)],
        [
            pltpu.VMEM((n, lanes, dim), BF16),
            pltpu.VMEM((dim, inner), BF16),
            pltpu.VMEM((dim, inner), BF16),
            pltpu.VMEM((dim, inner), BF16),
            pltpu.VMEM((inner, dim), BF16),
            pltpu.VMEM((token_rows, dim), F32),
            pltpu.VMEM((token_rows, dim), F32),
            pltpu.VMEM((token_rows, 128), F32),
            pltpu.VMEM((token_rows, dim), F32),
            pltpu.VMEM((HEADS * token_rows, inner), BF16),
            pltpu.VMEM((HEADS * token_rows, inner), BF16),
        ]
        + [pltpu.VMEM((token_rows, lanes), BF16)] * n
        + [
            pltpu.VMEM((token_rows, dim), BF16),
            pltpu.VMEM(table.shape, F32),
            pltpu.SemaphoreType.DMA((60,)),
        ],
        60,
        5_000_000_000,
        2 * n + 23,
        2 * n + 22,
    )(idx, *mixed, *blocks, token_frames, *token_grad, table)
    mixed_grads = exchange(list(outs[:n]))
    backs = outs[n : 2 * n]

    ours = outs[2 * n]
    keep_tall, send_tall, keep_flat, send_flat = wide_call(
        functools.partial(terms_body, n),
        "temporal_terms",
        [struct(clips, 3, piece, inner)] * 2 + [struct(2, 2, 2, low // 2, inner)] * 2,
        [
            pltpu.VMEM((dim, 2 * token_rows), BF16),
            pltpu.VMEM((inner, 2 * token_rows), BF16),
            pltpu.VMEM((depth, inner), F32),
            pltpu.VMEM((2, low, dim), F32),
        ],
        18,
        1,
        5,
        0,
        tuple(mixed_grads[1:]),
    )(idx, ours, flip(ours, "frame", 1), mixed[0], mixed[2])
    flat_a = flip(send_flat, "clip", 2)
    tall_y = flip(send_tall, "frame", 2)

    keep_out, send_out, keep_term, send_term = wide_call(
        functools.partial(spatial_backward_body, n, tokens, width),
        "spatial_backward",
        [struct(n // 2, rows + share, dim)] * 2 + [struct(count, n, piece, room)] * 2,
        [
            pltpu.VMEM((total, lanes), F32),
            pltpu.VMEM((token_rows, lanes), F32),
            pltpu.VMEM((total + tokens, room), BF16),
            pltpu.VMEM((dim, room), F32),
        ],
        20,
        1,
        n + 7,
        0,
        (send_flat, send_tall),
    )(idx, *mixed_grads, x_all, w_all, q_all, k_all, v_all, probs)

    def to_clip(value, bit):
        return flip(value, "clip", bit)

    head_got = to_clip(send_term, 1)
    out_got = flip(send_out, "frame", 1)
    flat, flat_out = steps.merge(keep_flat, flat_a, 0, 7)
    halves = (2, 2, 2, 3, piece, inner)
    tall, tall_out = steps.merge(keep_tall.reshape(halves), tall_y.reshape(halves), 0, 0)
    tall_got = to_clip(tall_out, 1)
    flat_got = flip(flat_out, "frame", 2)
    halves = (2, 2, n, piece, room)
    head, head_out = steps.merge(keep_term.reshape(halves), head_got.reshape(halves), 1, 1)
    head_got = to_clip(head_out, 2)
    partial, partial_out = steps.merge(keep_out, out_got, 0, 7)
    head = steps.merge(head, head_got)
    head_got = to_clip(head, 4)
    flat, flat_out = steps.merge(flat, flat_got, 0, 0)
    flat_got = to_clip(flat_out, 1)
    tall, tall_out = steps.merge(tall, tall_got, 1, 1)
    tall_got = to_clip(tall_out, 2)
    head_f = exchange(steps.merge(head, head_got, spread=True))
    flat = steps.merge(flat, flat_got)
    flat_got = to_clip(flat, 4)
    tall = steps.merge(tall, tall_got)
    tall_got = to_clip(tall, 4)
    head = steps.join(*head_f, axis=1)
    head_got = to_clip(head, 1)
    backs = exchange(list(backs))
    partial_got = flip(partial_out, "frame", 2)
    head = steps.join(head, head_got, axis=1)
    head_got = to_clip(head, 2)
    flat = steps.merge(flat, flat_got)
    flat_got = to_clip(flat, 2)
    output, frames_grad, refer_grad = steps.call(
        functools.partial(finish_body, n, per),
        "finish",
        [struct(rows, dim)] * 2 + [struct(share, dim)],
        [frames, *backs, partial, partial_got],
        [pltpu.VMEM((2 * few, dim), F32), pltpu.VMEM((2, rows, dim), F32)],
    )
    tall = steps.merge(tall, tall_got)
    tall_got = to_clip(tall, 1)
    head_grads = steps.call(
        functools.partial(place_heads_body, width),
        "place_heads",
        [struct(depth, inner, dtype=F32)] * 3,
        [head, head_got],
    )
    flat = steps.join(flat, flat_got, axis=1)
    flat_got = to_clip(flat, 1)
    tall = steps.join(tall, tall_got, axis=1)
    tall_got = to_clip(tall, 2)
    flat_grads = steps.call(place_flat_body, "place_flat", [struct(low, dim, dtype=F32)] * 2, [flat, flat_got])
    tall_grads = steps.call(place_body, "place_tall", [struct(depth, inner, dtype=F32)] * 3, [tall, tall_got])
    return (
        output.reshape(frames_in.shape),
        frames_grad.reshape(frames_in.shape),
        refer_grad[None],
        *head_grads,
        flat_grads[0],
        *tall_grads,
        flat_grads[1],
    )


def solution(mesh):
    in_specs = (
        P("clip", "frame", None, None),
        P("clip", "frame", None),
        P("clip", "frame", None, None),
        P("frame", None),
        P("frame", None),
        P("frame", None),
        P("frame", None),
        P("frame", None),
        P("frame", None),
        P("frame", None),
        P("frame", None),
    )
    out_specs = (
        P("clip", "frame", None, None),
        P("clip", "frame", None, None),
        P("clip", "frame", None),
        P("frame", None),
        P("frame", None),
        P("frame", None),
        P("frame", None),
        P("frame", None),
        P("frame", None),
        P("frame", None),
        P("frame", None),
    )
    clips = mesh.shape["clip"]
    by_heads = mesh.shape["frame"] == HEADS == 4 and clips == 8
    return jax.shard_map(
        per_device if by_heads else per_device_general, mesh=mesh, in_specs=in_specs, out_specs=out_specs, check_vma=False
    )
```
